256 devices in a mesh: leaf: 32 (over y, z), panel: 8 (over x, core).
Axes of the slice: x: 4, y: 4, z: 8, core: 2. Of those that a mesh axis runs over, the one named last changes fastest.
Arguments:
- rhs_sub: float32 [256, 512, 256], P(('leaf', 'panel')), may hold values from -6 to 6
- rhs_sep: float32 [3, 2048, 256], P(None, ('leaf', 'panel')), may hold values from -6 to 6
- sub_factor: float32 [256, 512, 512], P(('leaf', 'panel')), may hold values from -0.25 to 0.25
- sub_diag: float32 [256, 512], P(('leaf', 'panel')), may hold values from 1 to 2
- sep_factor: float32 [2048, 3584], P(('leaf', 'panel')), may hold values from -0.1875 to 0.1875
- sep_diag: float32 [3, 2048], P(None, ('leaf', 'panel')), may hold values from 1 to 2
- sub_update: float32 [256, 1792, 512], P(('leaf', 'panel')), may hold values from -6 to 6
- update_rows: int32 [256, 1792], P(('leaf', 'panel')), may hold values from 0 to 2047, as said below
- sep_update: float32 [256, 5120, 8], P(('leaf', 'panel')), may hold values from -6 to 6
Outputs:
- solution_sub: float32 [256, 512, 256], P(('leaf', 'panel'))
- solution_sep: float32 [3, 2048, 256], P(None, ('leaf', 'panel'))
The draws below stay inside these ranges and needn't reach their ends.
Inputs may be any that keep to these rules, and one draw needn't show every extreme that they name: Within each level's part of a row of update_rows the entries are distinct rows of that level's node, fewer than the node's row count, and the node's last row is always among them.
All inputs are finite; a program needn't handle non-finite values.
Results may differ from the reference program's by a relative error of at most 0.0003.
Values sent between devices are 32-bit elements; how exact they have to be, the bound alone decides.
A program may use at most 128 MiB of HBM per device.

```python
import jax
import jax.numpy as jnp
from jax import lax

RHS = 256
LOC = 512
SEP_DEV = 8
LEVELS = 3
ROWS = 2048
HALF = 1792
SEPUP = 5120
N_LEAF = 32
N_PANEL = 8


def draw_update_rows(key, part):
    key = jax.random.fold_in(key, 7)
    group_size = ROWS // SEP_DEV
    blocks = []
    for tier_index in range(LEVELS):
        node_count = ROWS // 2 ** tier_index
        chosen_count = node_count // 2
        device_keys = jax.random.split(jax.random.fold_in(key, tier_index), group_size)

        def choose_rows(device_key, node_count=node_count, chosen_count=chosen_count):
            shuffled = jax.random.permutation(device_key, node_count - 1)[:chosen_count - 1].astype(jnp.int32)
            return jnp.concatenate([shuffled, jnp.full((1,), node_count - 1, jnp.int32)])
        blocks.append(jax.vmap(choose_rows)(device_keys))
    return jnp.concatenate(blocks, axis=1)


def shard_levels(stream_key, shape, shards, low, high):
    level = 1.0
    for axis_at, blocks in shards:
        draws = jax.random.uniform(jax.random.fold_in(jax.random.fold_in(stream_key, 6), axis_at), (blocks,), jnp.float32, low / len(shards), high / len(shards))
        level = level * jnp.repeat(jnp.exp(draws), shape[axis_at] // blocks).reshape((-1,) + (1,) * (len(shape) - 1 - axis_at))
    return level


def noise(key, shape, deviation, most, pieces=(), kind=jnp.bfloat16):
    entries = jax.random.normal(key, shape, jnp.float32) * deviation
    if len(pieces) > 0:
        entries = shard_levels(key, shape, pieces, -0.22, 0.18) * entries
    return jnp.clip(entries, min=-most, max=most).astype(kind)


def setup_inputs(seed: int = 0) -> dict:
    streams_of = jax.random.split(jax.random.key(seed), 10)
    return {
        "rhs_sub": noise(streams_of[0], (N_LEAF * N_PANEL, LOC, RHS), 1.0, 6.0, ((0, 256),), jnp.float32),
        "rhs_sep": noise(streams_of[1], (LEVELS, ROWS, RHS), 1.0, 6.0, ((1, 256),), jnp.float32),
        "sub_factor": noise(streams_of[2], (N_LEAF * N_PANEL, LOC, LOC), LOC ** -0.5, 0.25, ((0, 256),), jnp.float32),
        "sub_diag": jnp.clip(1.0 + 1.0 * jax.random.uniform(streams_of[3], (N_LEAF * N_PANEL, LOC), jnp.float32) ** shard_levels(streams_of[3], (N_LEAF * N_PANEL, LOC), ((0, 256),), -0.2, 0.2), 1.0, 2.0),
        "sep_factor": noise(streams_of[4], (ROWS, 7 * ROWS // 4), (ROWS // 2) ** -0.5, 0.1875, ((0, 256),), jnp.float32),
        "sep_diag": jnp.clip(1.0 + 1.0 * jax.random.uniform(streams_of[5], (LEVELS, ROWS), jnp.float32) ** shard_levels(streams_of[5], (LEVELS, ROWS), ((1, 256),), -0.2, 0.2), 1.0, 2.0),
        "sub_update": noise(streams_of[6], (N_LEAF * N_PANEL, HALF, LOC), 1.0, 6.0, ((0, 256),), jnp.float32),
        "update_rows": draw_update_rows(jax.random.fold_in(streams_of[9], 71), 0),
        "sep_update": noise(streams_of[8], (N_LEAF * N_PANEL, SEPUP, SEP_DEV), 1.0, 6.0, ((0, 256),), jnp.float32),
    }


def sub_offset(target, total_rows):
    return sum((total_rows // 2 ** inner_level // 2 for inner_level in range(target)))

def sep_offset(source, target, total_rows):
    offset_value = 0
    for earlier in range(1, source):
        offset_value += sum((total_rows // 2 ** inner_level for inner_level in range(earlier)))
    return offset_value + sum((total_rows // 2 ** inner_level for inner_level in range(target)))

def column_offset(target, total_rows):
    return sum((total_rows // 2 ** inner_level for inner_level in range(target)))

def weight_scale(target, group_size, local_rows, levels, total_rows):
    fan_total = group_size // 2 ** target * local_rows // 2 + (levels - 1 - target) * (total_rows // 2 ** target)
    return float(fan_total) ** (-0.5)

def triangle(strict, diagonal):
    order_size = strict.shape[-1]
    return jnp.tril(strict, -1) + diagonal[..., :, None] * jnp.eye(order_size, dtype=jnp.float32)

def solve_lower(matrix, right_side, transposed):
    return lax.linalg.triangular_solve(matrix, right_side, left_side=True, lower=True, transpose_a=transposed)

def inverse_block(sep_factor, sep_diag, target):
    node_rows = ROWS // 2 ** target
    start = column_offset(target, ROWS)
    strict = sep_factor[:, start:start + node_rows].reshape(2 ** target, node_rows, node_rows)
    return triangle(strict, sep_diag[target].reshape(2 ** target, node_rows))

def reference(rhs_sub, rhs_sep, sub_factor, sub_diag, sep_factor, sep_diag, sub_update, update_rows, sep_update):
    precise = lax.Precision.HIGHEST
    group_size = sub_factor.shape[0]
    sub_lower = triangle(sub_factor, sub_diag)
    sub_solved = solve_lower(sub_lower, rhs_sub, False)
    device_ids = jnp.arange(group_size, dtype=jnp.int32)
    solved = [None] * LEVELS
    for target in reversed(range(LEVELS)):
        node_rows = ROWS // 2 ** target
        group_width = group_size // 2 ** target
        offset_sub = sub_offset(target, ROWS)
        rows_used = update_rows[:, offset_sub:offset_sub + node_rows // 2]
        coupling = sub_update[:, offset_sub:offset_sub + node_rows // 2, :]
        sources = list(range(target + 1, LEVELS))
        blocks = [sep_update[:, sep_offset(source, target, ROWS):sep_offset(source, target, ROWS) + node_rows, :] for source in sources]
        deeper = [solved[source] for source in sources]

        def accumulate(accumulated, record, node_rows=node_rows, group_width=group_width):
            device, rows_here, coupling_here, sub_here, blocks_here, deeper_here = record
            partial_value = jnp.zeros((node_rows, RHS), jnp.float32).at[rows_here].add(jnp.dot(coupling_here, sub_here, precision=precise))
            for coupling_block, deeper_block in zip(blocks_here, deeper_here):
                partial_value = partial_value + jnp.dot(coupling_block, deeper_block, precision=precise)
            node_index = device // group_width
            current = lax.dynamic_index_in_dim(accumulated, node_index, 0, keepdims=False)
            return (lax.dynamic_update_index_in_dim(accumulated, current + partial_value, node_index, 0), None)
        accumulated, unused = lax.scan(accumulate, jnp.zeros((2 ** target, node_rows, RHS), jnp.float32), (device_ids, rows_used, coupling, sub_solved, blocks, deeper))
        level_scale = weight_scale(target, group_size, LOC, LEVELS, ROWS)
        residual = rhs_sep[target] - level_scale * accumulated.reshape(ROWS, RHS)
        inverse = inverse_block(sep_factor, sep_diag, target)
        node_solved = jnp.matmul(inverse, residual.reshape(2 ** target, node_rows, RHS), precision=precise)
        solved[target] = node_solved.reshape(group_size, SEP_DEV, RHS)
    finished = [None] * LEVELS
    for target in range(LEVELS):
        node_rows = ROWS // 2 ** target
        ancestors = list(range(target))
        blocks = [sep_update[:, sep_offset(target, ancestor, ROWS):sep_offset(target, ancestor, ROWS) + ROWS // 2 ** ancestor, :] for ancestor in ancestors]
        node_values = [finished[ancestor].reshape(2 ** ancestor, ROWS // 2 ** ancestor, RHS) for ancestor in ancestors]

        def descend(record, ancestors=ancestors, node_values=node_values):
            device, current, blocks_here = record
            for ancestor, coupling_block, values_here in zip(ancestors, blocks_here, node_values):
                picked = lax.dynamic_index_in_dim(values_here, device // (group_size // 2 ** ancestor), 0, keepdims=False)
                level_scale = weight_scale(ancestor, group_size, LOC, LEVELS, ROWS)
                current = current - level_scale * jnp.dot(coupling_block.T, picked, precision=precise)
            return current
        adjusted = lax.map(descend, (device_ids, solved[target], blocks))
        inverse = inverse_block(sep_factor, sep_diag, target)
        node_final = jnp.matmul(jnp.swapaxes(inverse, 1, 2), adjusted.reshape(2 ** target, node_rows, RHS), precision=precise)
        finished[target] = node_final.reshape(ROWS, RHS)

    def leaves(record):
        device, current, rows_all, coupling_all = record
        for target in range(LEVELS):
            node_rows = ROWS // 2 ** target
            offset_sub = sub_offset(target, ROWS)
            values_here = lax.dynamic_index_in_dim(finished[target].reshape(2 ** target, node_rows, RHS), device // (group_size // 2 ** target), 0, keepdims=False)
            picked = values_here[rows_all[offset_sub:offset_sub + node_rows // 2]]
            level_scale = weight_scale(target, group_size, LOC, LEVELS, ROWS)
            current = current - level_scale * jnp.dot(coupling_all[offset_sub:offset_sub + node_rows // 2].T, picked, precision=precise)
        return current
    adjusted_sub = lax.map(leaves, (device_ids, sub_solved, update_rows, sub_update))
    solution_sub = solve_lower(sub_lower, adjusted_sub, True)
    return (solution_sub, jnp.stack(finished))
```

```python
import functools

import jax
import jax.numpy as jnp
from jax import lax
from jax.experimental import pallas as pl
from jax.experimental.pallas import tpu as pltpu
from jax.sharding import PartitionSpec as P

MESH = pl.DeviceIdType.MESH
F32 = jnp.float32
BF16 = jnp.bfloat16
NN = (((1,), (0,)), ((), ()))
NT = (((1,), (1,)), ((), ()))
TN = (((0,), (0,)), ((), ()))

NX, NY, NZ = 4, 4, 8
ROWS, RHS, LOC, BLK = 2048, 256, 512, 8
LEVELS = 3
LANES = 128
COLS = 16
G2, E21, G1, E20, E10, G0, WIDE = 0, 512, 1536, 2560, 4608, 6656, 8704


def weight_scale(target):
    fan_total = (256 >> target) * LOC // 2 + (LEVELS - 1 - target) * (ROWS >> target)
    return float(fan_total) ** (-0.5)


def split(value):
    high = value.astype(BF16)
    return high, (value - high.astype(F32)).astype(BF16)


def small_dot(left, right, dims):
    left_high, left_low = split(left)
    right_high, right_low = split(right)
    rows = left.shape[0]
    both = jnp.concatenate([left_high, left_low], axis=0)
    first = lax.dot_general(both, right_high, dims, preferred_element_type=F32)
    second = lax.dot_general(left_high, right_low, dims, preferred_element_type=F32)
    return first[:rows] + first[rows:] + second


def place():
    leaf, panel = lax.axis_index("leaf"), lax.axis_index("panel")
    return panel // 2, leaf // NZ, leaf % NZ, panel % 2


def device(x, y, z, c):
    return (y * NZ + z, x * 2 + c)


def chain_kernel(
    ut0, ut1, ut2, m_ref, x0, x1, x2,
    b2c, b1c, b0c, b2x, b2s, b2z, b1x, b1s, b1y, b1t, b1z, b0y, b0s, b0x, b0t, b0z,
    g2, p1, p1r, g1, p0, p0r, g0, q0, q0r, h0, q1, q1r, h1, q2, q2r, h2,
    ssem, rsem,
):
    x, y, z, c = place()
    partner = y + 1 - 2 * (y % 2)
    yy = y % 2
    sibling = device(x, y, z, 1 - c)
    plane = [(a, b) for a in range(NX) for b in range(NY)][1:]
    half = [(a, b) for a in range(NX) for b in range(2)][1:]

    def xs(a):
        return (x + a) % NX

    def ys(b):
        return (y + b) % NY

    def zs(d):
        return (z + d) % NZ

    def pair_y(b):
        return partner if b else y

    barrier = pltpu.get_barrier_semaphore()
    greeted = [device(xs(a), ys(b), z, c) for a, b in plane]
    greeted += [device(x, y, zs(d), c) for d in range(1, NZ)] + [sibling]
    for peer in greeted:
        pl.semaphore_signal(barrier, inc=1, device_id=peer, device_id_type=MESH)
    pl.semaphore_wait(barrier, len(greeted))

    copies = []

    def send(src, dst, peer):
        at = len(copies)
        copy = pltpu.make_async_remote_copy(
            src_ref=src, dst_ref=dst, send_sem=ssem.at[at], recv_sem=rsem.at[at],
            device_id=peer, device_id_type=MESH,
        )
        copy.start()
        copies.append(copy)
        return copy

    def arrive(batch):
        for copy in batch:
            copy.wait_recv()

    mine = pl.ds(pl.multiple_of(c * LANES, LANES), LANES)
    other = pl.ds(pl.multiple_of((1 - c) * LANES, LANES), LANES)
    cols = pl.ds(pl.multiple_of(z * COLS, COLS), COLS)
    spread = pl.ds(pl.multiple_of(c * LANES + z * COLS, COLS), COLS)

    c2 = send(ut2.at[:, other, :], b2c, sibling)
    c1 = send(ut1.at[:, other, :], b1c, sibling)
    c0 = send(ut0.at[:, other, :], b0c, sibling)

    def add_own(total, own):
        def step(i, carry):
            total[i] = total[i] + own[i, mine, :]
            return carry

        lax.fori_loop(0, total.shape[0], step, 0)

    def z_stage(summed, parts):
        return [
            send(summed.at[pl.ds(pl.multiple_of(zs(d) * COLS, COLS), COLS), :], parts.at[d - 1], device(x, y, zs(d), c))
            for d in range(1, NZ)
        ]

    def z_sum(summed, parts, batch):
        arrive(batch)
        total = summed[cols, :]
        for d in range(NZ - 1):
            total = total + parts[d]
        return total

    c2.wait_recv()
    add_own(b2c, ut2)
    x2s = [send(b2c.at[xs(a)], b2x.at[a - 1], device(xs(a), y, z, c)) for a in range(1, NX)]
    c1.wait_recv()
    add_own(b1c, ut1)
    x1s = [send(b1c.at[pl.ds(xs(a) * 2, 2)], b1x.at[a - 1], device(xs(a), y, z, c)) for a in range(1, NX)]
    c0.wait_recv()
    add_own(b0c, ut0)
    y0s = [send(b0c.at[pl.ds(ys(b) * NX, NX)], b0y.at[b - 1], device(x, ys(b), z, c)) for b in range(1, NY)]

    arrive(x2s)
    b2s[...] = b2c[x] + b2x[0] + b2x[1] + b2x[2]
    z2s = z_stage(b2s, b2z)
    arrive(x1s)
    for i in range(2):
        b1s[i] = b1c[x * 2 + i] + b1x[0, i] + b1x[1, i] + b1x[2, i]
    y1s = send(b1s.at[1 - yy], b1y, device(x, partner, z, c))

    r2 = z_sum(b2s, b2z, z2s)
    g2[x] = r2
    a2 = [send(g2.at[x], g2.at[x], device(xs(a), y, z, c)) for a in range(1, NX)]
    y1s.wait_recv()
    b1t[...] = b1s[yy] + b1y[...]
    z1s = z_stage(b1t, b1z)
    arrive(y0s)
    for i in range(NX):
        b0s[i] = b0c[y * NX + i] + b0y[0, i] + b0y[1, i] + b0y[2, i]
    x0s = [send(b0s.at[xs(a)], b0x.at[a - 1], device(xs(a), y, z, c)) for a in range(1, NX)]

    def joined(ref):
        return jnp.concatenate([ref[i] for i in range(ref.shape[0])], axis=1)

    def spill(value, ref):
        for i in range(ref.shape[0]):
            ref[i] = value[:, i * LANES : (i + 1) * LANES]

    def columns(start, size):
        return m_ref[:, start : start + size]

    here1 = yy * NX + x
    here0 = y * NX + x

    def scatter_half(part, landed):
        return [
            send(part.at[(yy if b == 0 else 1 - yy) * NX + xs(a)], landed.at[k], device(xs(a), pair_y(b), z, c))
            for k, (a, b) in enumerate(half)
        ]

    def gather_half(whole):
        return [send(whole.at[here1], whole.at[here1], device(xs(a), pair_y(b), z, c)) for a, b in half]

    def scatter_plane(part, landed):
        return [
            send(part.at[ys(b) * NX + xs(a)], landed.at[k], device(xs(a), ys(b), z, c))
            for k, (a, b) in enumerate(plane)
        ]

    def gather_plane(whole):
        return [send(whole.at[here0], whole.at[here0], device(xs(a), ys(b), z, c)) for a, b in plane]

    def summed(part, here, landed, batch):
        arrive(batch)
        total = part[here]
        for k in range(landed.shape[0]):
            total = total + landed[k]
        return total

    s0_scale, s1_scale = weight_scale(0), weight_scale(1)

    arrive(a2)
    solved2 = small_dot(joined(g2), columns(G2, 512), NT)
    spill(small_dot(solved2, columns(E21, 1024), NN), p1)
    batch = scatter_half(p1, p1r)
    r1 = z_sum(b1t, b1z, z1s)
    arrive(x0s)
    b0t[...] = b0s[x] + b0x[0] + b0x[1] + b0x[2]
    z0s = z_stage(b0t, b0z)
    g1[here1] = r1 - s1_scale * summed(p1, here1, p1r, batch)
    batch = gather_half(g1)
    up0 = small_dot(solved2, columns(E20, 2048), NN)
    arrive(batch)
    solved1 = small_dot(joined(g1), columns(G1, 1024), NT)
    spill(up0 + small_dot(solved1, columns(E10, 2048), NN), p0)
    batch = scatter_plane(p0, p0r)
    r0 = z_sum(b0t, b0z, z0s)
    g0[here0] = r0 - s0_scale * summed(p0, here0, p0r, batch)
    arrive(gather_plane(g0))
    solved0 = small_dot(joined(g0), columns(G0, 2048), NT)

    def hand_out(whole, result):
        result[:, spread, :] = whole[...]
        return [send(whole, result.at[:, spread, :], device(x, y, zs(d), c)) for d in range(1, NZ)]

    spill(small_dot(solved0, columns(G0, 2048), NN), q0)
    batch = scatter_plane(q0, q0r)
    h0[here0] = summed(q0, here0, q0r, batch)
    arrive(gather_plane(h0))
    d0s = hand_out(h0, x0)
    found0 = joined(h0)
    y1 = solved1 - s0_scale * small_dot(found0, columns(E10, 2048), NT)
    spill(small_dot(y1, columns(G1, 1024), NN), q1)
    batch = scatter_half(q1, q1r)
    y2 = solved2 - s0_scale * small_dot(found0, columns(E20, 2048), NT)
    h1[here1] = summed(q1, here1, q1r, batch)
    arrive(gather_half(h1))
    d1s = hand_out(h1, x1)
    y2 = y2 - s1_scale * small_dot(joined(h1), columns(E21, 1024), NT)
    spill(small_dot(y2, columns(G2, 512), NN), q2)
    batch = [send(q2.at[xs(a)], q2r.at[a - 1], device(xs(a), y, z, c)) for a in range(1, NX)]
    h2[x] = summed(q2, x, q2r, batch)
    arrive([send(h2.at[x], h2.at[x], device(xs(a), y, z, c)) for a in range(1, NX)])
    d2s = hand_out(h2, x2)
    last = []
    for result, batch in ((x0, d0s), (x1, d1s), (x2, d2s)):
        arrive(batch)
        last.append(send(result.at[:, mine, :], result.at[:, mine, :], sibling))
    arrive(last)
    for copy in copies:
        copy.wait_send()


N_COPIES = 3 + 3 + 3 + 3 + 7 + 1 + 3 + 7 + 3 + 7 + 7 + 7 + 15 + 15 + 15 + 15 + 7 + 7 + 7 + 7 + 3 + 3 + 7 + 3


def chain(ut0, ut1, ut2, matrix):
    def piece(*lead, rows=COLS):
        return pltpu.VMEM((*lead, rows, LANES), F32)

    scratch = [
        piece(4, rows=LANES), piece(8, rows=LANES), piece(16, rows=LANES),
        piece(3, rows=LANES), piece(rows=LANES), piece(7),
        piece(3, 2, rows=LANES), piece(2, rows=LANES), piece(rows=LANES), piece(rows=LANES), piece(7),
        piece(3, 4, rows=LANES), piece(4, rows=LANES), piece(3, rows=LANES), piece(rows=LANES), piece(7),
        piece(4), piece(8), piece(7), piece(8), piece(16), piece(15), piece(16),
        piece(16), piece(15), piece(16), piece(8), piece(7), piece(8), piece(4), piece(3), piece(4),
        pltpu.SemaphoreType.DMA((N_COPIES,)), pltpu.SemaphoreType.DMA((N_COPIES,)),
    ]
    vmem = pl.BlockSpec(memory_space=pltpu.VMEM)
    return pl.pallas_call(
        chain_kernel,
        out_shape=[jax.ShapeDtypeStruct((n, RHS, LANES), F32) for n in (16, 8, 4)],
        in_specs=[vmem] * 4,
        out_specs=[vmem] * 3,
        scratch_shapes=scratch,
        compiler_params=pltpu.CompilerParams(
            collective_id=0, has_side_effects=True, vmem_limit_bytes=48 * 1024 * 1024
        ),
    )(ut0, ut1, ut2, matrix)


def rounded(value):
    return lax.reduce_precision(value, 8, 7)


def parts(value):
    high = rounded(value)
    return high.astype(BF16), rounded(value - high).astype(BF16)


def fast_dot(left, right, dims):
    lh, ll = parts(left)
    rh, rl = parts(right)
    dot = functools.partial(lax.dot_general, dimension_numbers=dims, preferred_element_type=F32)
    return dot(lh, rh) + (dot(lh, rl) + dot(ll, rh))


def exact_right_dot(left, right, dims):
    lh, ll = parts(left)
    dot = functools.partial(lax.dot_general, dimension_numbers=dims, preferred_element_type=F32)
    return dot(lh, right) + dot(ll, right)


def triangle(strict, diagonal):
    order_size = strict.shape[-1]
    return jnp.tril(strict, -1) + diagonal[..., :, None] * jnp.eye(order_size, dtype=F32)


def solve_lower(matrix, right_side, transposed):
    return lax.linalg.triangular_solve(matrix, right_side, left_side=True, lower=True, transpose_a=transposed)


def reorder(rows):
    return rows // 512 * 512 + rows // 16 % 4 * 128 + rows // 64 % 8 * 16 + rows % 16


def reorder_columns(value):
    lead, width = value.shape
    value = value.reshape(lead, width // 512, NZ, NX, 16)
    return jnp.swapaxes(value, 2, 3).reshape(lead, width)


def body(rhs_sub, rhs_sep, sub_factor, sub_diag, sep_factor, sep_diag, sub_update, update_rows, sep_update):
    position = lax.axis_index(("leaf", "panel"))
    inverses = []
    for level in range(LEVELS):
        node_rows = ROWS >> level
        start = sum(ROWS >> k for k in range(level))
        own = position % (256 >> level) * BLK
        strict = sep_factor[:, start : start + node_rows]
        row_ids = own + lax.broadcasted_iota(jnp.int32, (BLK, node_rows), 0)
        col_ids = lax.broadcasted_iota(jnp.int32, (BLK, node_rows), 1)
        lower = jnp.where(col_ids < row_ids, strict, 0.0)
        inverses.append(lower + jnp.where(col_ids == row_ids, sep_diag[level][:, None], 0.0))
    turned = sep_update[0].T
    e10, e20, e21 = turned[:, :2048], turned[:, 2048:4096], turned[:, 4096:]
    matrix = reorder_columns(jnp.concatenate([inverses[2], e21, inverses[1], e20, e10, inverses[0]], axis=1))
    pairs = [[2 * k, 2 * k + 1] for k in range(NX)]
    lines = [[k * NZ + j for j in range(NZ)] for k in range(NY)]
    matrix = lax.all_gather(matrix, "panel", axis=0, tiled=True, axis_index_groups=pairs)
    matrix = lax.all_gather(matrix, "leaf", axis=0, tiled=True, axis_index_groups=lines)

    sub_lower = triangle(sub_factor[0], sub_diag[0])
    sub_solved = solve_lower(sub_lower, rhs_sub[0], False)
    coupling = sub_update[0]
    terms = fast_dot(sub_solved, coupling, (((0,), (1,)), ((), ())))
    sums, picks = [], []
    start = 0
    for level in range(LEVELS):
        node_rows = ROWS >> level
        count = node_rows // 2
        rows = reorder(update_rows[0, start : start + count])
        ids = lax.broadcasted_iota(jnp.int32, (count, node_rows), 1)
        pick = (rows[:, None] == ids).astype(BF16)
        own = position % (256 >> level) * BLK + jnp.arange(BLK, dtype=jnp.int32)
        mark = (reorder(own)[:, None] == lax.broadcasted_iota(jnp.int32, (BLK, node_rows), 1)).astype(F32)
        placed = jnp.dot(rhs_sep[level].T, mark, precision=lax.Precision.HIGHEST)
        sums.append(placed - weight_scale(level) * exact_right_dot(terms[:, start : start + count], pick, NN))
        picks.append(pick)
        start += count
    ut0 = sums[0].reshape(RHS, 16, LANES).swapaxes(0, 1)
    ut1 = sums[1].reshape(RHS, 2, NX, LANES).transpose(2, 1, 0, 3).reshape(8, RHS, LANES)
    ut2 = sums[2].reshape(RHS, NX, LANES).swapaxes(0, 1)
    found = chain(ut0, ut1, ut2, matrix)

    current = sub_solved
    own_results = []
    start = 0
    for level in range(LEVELS):
        node_rows = ROWS >> level
        count = node_rows // 2
        whole = found[level].swapaxes(0, 1).reshape(RHS, node_rows)
        picked = exact_right_dot(whole, picks[level], NT)
        current = current - weight_scale(level) * fast_dot(coupling[start : start + count], picked, (((0,), (1,)), ((), ())))
        own = position % (256 >> level) * BLK
        at = reorder(own)
        block = lax.dynamic_index_in_dim(found[level], at // LANES, 0, keepdims=False)
        own_results.append(lax.dynamic_slice_in_dim(block, at % LANES, BLK, 1).T)
        start += count
    result_sub = solve_lower(sub_lower, current, True)
    return result_sub[None], jnp.stack(own_results)


def solution(mesh):
    both = ("leaf", "panel")
    in_specs = (
        P(both, None, None), P(None, both, None), P(both, None, None), P(both, None), P(both, None),
        P(None, both), P(both, None, None), P(both, None), P(both, None, None),
    )
    out_specs = (P(both, None, None), P(None, both, None))
    return jax.shard_map(body, mesh=mesh, in_specs=in_specs, out_specs=out_specs, check_vma=False)
```

```python
import jax
import jax.numpy as jnp
from jax import lax
from jax.experimental import pallas as pl
from jax.experimental.pallas import tpu as pltpu
from jax.sharding import PartitionSpec as P

MESH = pl.DeviceIdType.MESH
F32 = jnp.float32
BF16 = jnp.bfloat16
NN = (((1,), (0,)), ((), ()))
NT = (((1,), (1,)), ((), ()))
TN = (((0,), (0,)), ((), ()))

NX, NY, NZ = 4, 4, 8
ROWS, RHS, LOC, BLK = 2048, 256, 512, 8
LEVELS = 3
LANES = 128
COLS = 16
G2, E21, G1, E20, E10, G0, WIDE = 0, 512, 1536, 2560, 4608, 6656, 8704


def weight_scale(target):
    fan_total = (256 >> target) * LOC // 2 + (LEVELS - 1 - target) * (ROWS >> target)
    return float(fan_total) ** (-0.5)


def split(value):
    high = value.astype(BF16)
    return high, (value - high.astype(F32)).astype(BF16)


def small_dot(left, right, dims):
    left_high, left_low = split(left)
    right_high, right_low = split(right)
    rows = left.shape[0]
    both = jnp.concatenate([left_high, left_low], axis=0)
    first = lax.dot_general(both, right_high, dims, preferred_element_type=F32)
    second = lax.dot_general(left_high, right_low, dims, preferred_element_type=F32)
    return first[:rows] + first[rows:] + second


def place():
    leaf, panel = lax.axis_index("leaf"), lax.axis_index("panel")
    return panel // 2, leaf // NZ, leaf % NZ, panel % 2


def device(x, y, z, c):
    return (y * NZ + z, x * 2 + c)


def split3(value):
    high = value.astype(BF16)
    rest = value - high.astype(F32)
    middle = rest.astype(BF16)
    return high, middle, (rest - middle.astype(F32)).astype(BF16)


def exact_dot(left, right):
    return jnp.dot(left, right, precision=lax.Precision.HIGHEST, preferred_element_type=F32)


def iota(shape, dim):
    return lax.broadcasted_iota(jnp.int32, shape, dim)


def reorder(rows):
    return (rows >> 9 << 9) + ((rows >> 4 & 3) << 7) + ((rows >> 6 & 7) << 4) + (rows & 15)


def sub_start(level):
    return sum(ROWS >> k + 1 for k in range(level))


def row_start(level):
    return sum(ROWS >> k for k in range(level))


def invert(factor, scale, inverse):
    lane = iota((32, LANES), 1)
    row, col = iota((LANES, LANES), 0), iota((LANES, LANES), 1)
    blocks, packed = [], []
    for g in range(4):
        at = slice(g * LANES, (g + 1) * LANES)
        block = jnp.where(row > col, factor[at, at] * scale[:, at], 0.0)
        blocks.append(block)
        parts = [jnp.where(lane >> 5 == q, block[32 * q : 32 * q + 32], 0.0) for q in range(4)]
        packed.append(parts[0] + parts[1] + parts[2] + parts[3])
    unit = (iota((32, LANES), 0) == (lane & 31)).astype(F32)
    found = [unit] * 4
    for k in range(31):
        index = (lane & 96) + k
        for g in range(4):
            coefficient = jnp.take_along_axis(packed[g], index, axis=1, mode="promise_in_bounds")
            found[g] = found[g] - coefficient * found[g][k : k + 1, :]
    whole = []
    for g in range(4):
        total = jnp.concatenate([jnp.where(lane >> 5 == q, found[g], 0.0) for q in range(4)], axis=0)
        whole.append(total)
    for bit in (5, 6):
        below = (row >> bit + 1 == col >> bit + 1) & (row >> bit > col >> bit)
        inner = [exact_dot(jnp.where(below, blocks[g], 0.0), whole[g]) for g in range(4)]
        whole = [whole[g] - exact_dot(whole[g], inner[g]) for g in range(4)]
    inverse[...] = jnp.zeros_like(inverse)
    for h in range(2):
        first = slice(h * 256, h * 256 + 128)
        second = slice(h * 256 + 128, h * 256 + 256)
        inner = exact_dot(factor[second, first] * scale[:, first], whole[2 * h])
        inverse[first, first] = whole[2 * h]
        inverse[second, second] = whole[2 * h + 1]
        inverse[second, first] = -exact_dot(whole[2 * h + 1], inner)
    inner = exact_dot(factor[256:, :256] * scale[:, :256], inverse[:256, :256])
    inverse[256:, :256] = -exact_dot(inverse[256:, 256:], inner)


def separator_rows(sep_factor, sep_diag, turned, position):
    inverses = []
    eye = iota((BLK, BLK), 0) == iota((BLK, BLK), 1)
    for level in range(LEVELS):
        node_rows = ROWS >> level
        start = row_start(level)
        strict = sep_factor[:, start : start + node_rows]
        diagonal = jnp.sum(jnp.where(eye, sep_diag[level : level + 1, :], 0.0), axis=1, keepdims=True)
        own = position % (256 >> level) * BLK + iota((BLK, node_rows), 0)
        cols = iota((BLK, node_rows), 1)
        inverses.append(jnp.where(cols < own, strict, 0.0) + jnp.where(cols == own, diagonal, 0.0))
    e10, e20, e21 = turned[:, :2048], turned[:, 2048:4096], turned[:, 4096:]
    pieces = [inverses[2], e21, inverses[1], e20, e10, inverses[0]]
    blocks = [piece[:, i : i + 512] for piece in pieces for i in range(0, piece.shape[1], 512)]
    stacked = jnp.concatenate(blocks, axis=0)
    swap = jnp.where(reorder(iota((512, 512), 0)) == iota((512, 512), 1), 1.0, 0.0).astype(BF16)
    high, middle, low = split3(stacked)
    return (
        jnp.dot(high, swap, preferred_element_type=F32)
        + jnp.dot(middle, swap, preferred_element_type=F32)
        + jnp.dot(low, swap, preferred_element_type=F32)
    )


def whole_kernel(
    diag, rows, rhs_sep, sep_factor, sep_diag, turned, factor_hbm, rhs_hbm, update_hbm,
    out_sub, out_sep,
    factor, rhs, update, inverse, solved_t, current, terms, update_high, update_low, moved_high, moved_low,
    ut0, ut1, ut2, m_ref, x0, x1, x2,
    b2c, b1c, b0c, b2x, b2s, b2z, b1x, b1s, b1y, b1t, b1z, b0y, b0s, b0x, b0t, b0z,
    g2, p1, p1r, g1, p0, p0r, g0, q0, q0r, h0, q1, q1r, h1, q2, q2r, h2,
    lsem, ssem, rsem,
):
    x, y, z, c = place()
    position = lax.axis_index("leaf") * 8 + lax.axis_index("panel")
    partner = y + 1 - 2 * (y % 2)
    yy = y % 2
    sibling = device(x, y, z, 1 - c)
    plane = [(a, b) for a in range(NX) for b in range(NY)][1:]
    half = [(a, b) for a in range(NX) for b in range(2)][1:]

    loads = [
        pltpu.make_async_copy(src, dst, lsem.at[i])
        for i, (src, dst) in enumerate(((factor_hbm, factor), (rhs_hbm, rhs), (update_hbm, update)))
    ]
    for load in loads:
        load.start()

    def xs(a):
        return (x + a) % NX

    def ys(b):
        return (y + b) % NY

    def zs(d):
        return (z + d) % NZ

    def pair_y(b):
        return partner if b else y

    barrier = pltpu.get_barrier_semaphore()
    greeted = [device(xs(a), ys(b), z, c) for a, b in plane]
    greeted += [device(x, y, zs(d), c) for d in range(1, NZ)] + [sibling]
    for peer in greeted:
        pl.semaphore_signal(barrier, inc=1, device_id=peer, device_id_type=MESH)

    copies = []

    def send(src, dst, peer):
        at = len(copies)
        copy = pltpu.make_async_remote_copy(
            src_ref=src, dst_ref=dst, send_sem=ssem.at[at], recv_sem=rsem.at[at],
            device_id=peer, device_id_type=MESH,
        )
        copy.start()
        copies.append(copy)
        return copy

    def arrive(batch):
        for copy in batch:
            copy.wait_recv()

    own_rows = separator_rows(sep_factor, sep_diag, turned, position)
    for i in range(WIDE // 512):
        m_ref[z, c, :, i * 512 : (i + 1) * 512] = own_rows[i * BLK : (i + 1) * BLK]
    pl.semaphore_wait(barrier, len(greeted))

    def pass_on(block, columns, peer):
        ref = m_ref.at[block, c, :, columns]
        return send(ref, ref, peer)

    everything, front, back = pl.ds(0, WIDE), pl.ds(0, WIDE // 2), pl.ds(WIDE // 2, WIDE // 2)
    right, left = device(x, y, zs(1), c), device(x, y, zs(NZ - 1), c)
    ring = [[pass_on(z, everything, right), pass_on(z, everything, left)]]
    shared = [pass_on(z, everything, sibling)]

    def ring_step():
        step = len(ring)
        arrive(ring[-1])
        from_left, from_right = zs(NZ - step), zs(step)
        if step < 3:
            ring.append([pass_on(from_left, everything, right), pass_on(from_right, everything, left)])
        elif step == 3:
            ring.append([pass_on(from_left, front, right), pass_on(from_right, back, left)])
        else:
            ring.append([])
        if step < 4:
            shared.append(pass_on(from_left, everything, sibling))
            shared.append(pass_on(from_right, everything, sibling))
        else:
            shared.append(pass_on(from_left, everything, sibling))

    scale = 1.0 / diag[...]
    loads[0].wait()
    invert(factor, scale, inverse)
    loads[1].wait()
    right_t = rhs[...].T
    solved_t[...] = small_dot(right_t, inverse[...], NT) * scale
    current[...] = solved_t[...]
    ring_step()
    loads[2].wait()
    solved_high, solved_low = split(solved_t[...])
    solved_both = jnp.concatenate([solved_high, solved_low], axis=0)

    def coupling_terms(level):
        def step(i, carry):
            at = pl.ds(pl.multiple_of(sub_start(level) + i * 256, 256), 256)
            high, low = split(update[at, :])
            update_high[at, :] = high
            update_low[at, :] = low
            first = lax.dot_general(solved_both, high, NT, preferred_element_type=F32)
            second = lax.dot_general(solved_high, low, NT, preferred_element_type=F32)
            top, bottom = split(first[:RHS] + first[RHS:] + second)
            terms[:RHS, at] = top
            terms[RHS:, at] = bottom
            return carry

        lax.fori_loop(0, (ROWS >> level) // 512, step, 0)

    places = []
    for level in range(LEVELS):
        count = ROWS >> level + 1
        places.append(reorder(rows[:, sub_start(level) : sub_start(level) + count]))

    def chosen(level, i):
        count = ROWS >> level + 1
        ids = iota((256, count), 0) + i * 256
        return jnp.where(ids == places[level], 1.0, 0.0).astype(BF16)

    own_chunk = [y * NX + x, x * 2 + yy, x]
    mark = jnp.where(iota((BLK, LANES), 1) == z * 16 + c * BLK + iota((BLK, LANES), 0), 1.0, 0.0)

    def node_terms(level, ut):
        count = ROWS >> level + 1
        listed = terms[:, sub_start(level) : sub_start(level) + count]

        def step(i, carry):
            both = lax.dot_general(listed, chosen(level, i), NT, preferred_element_type=F32)
            total = (both[:RHS] + both[RHS:]) * -weight_scale(level)
            for k in range(2):
                q = 2 * i + k
                at = q % NX * 2 + q // NX if level == 1 else q
                ut[at] = total[:, k * LANES : (k + 1) * LANES]
            return carry

        lax.fori_loop(0, (ROWS >> level) // 256, step, 0)
        own = lax.dot_general(rhs_sep[level], mark, TN, precision=lax.Precision.HIGHEST, preferred_element_type=F32)
        ut[own_chunk[level]] = ut[own_chunk[level]] + own

    mine = pl.ds(pl.multiple_of(c * LANES, LANES), LANES)
    other = pl.ds(pl.multiple_of((1 - c) * LANES, LANES), LANES)
    cols = pl.ds(pl.multiple_of(z * COLS, COLS), COLS)
    spread = pl.ds(pl.multiple_of(c * LANES + z * COLS, COLS), COLS)

    def add_own(total, own):
        def step(i, carry):
            total[i] = total[i] + own[i, mine, :]
            return carry

        lax.fori_loop(0, total.shape[0], step, 0)

    def z_stage(summed, parts):
        return [
            send(summed.at[pl.ds(pl.multiple_of(zs(d) * COLS, COLS), COLS), :], parts.at[d - 1], device(x, y, zs(d), c))
            for d in range(1, NZ)
        ]

    def z_sum(summed, parts, batch):
        arrive(batch)
        total = summed[cols, :]
        for d in range(NZ - 1):
            total = total + parts[d]
        return total

    pieces = [(2, i) for i in range(2)] + [(1, i) for i in range(4)] + [(0, i) for i in range(8)]

    def work(amount):
        for _ in range(amount):
            if pieces:
                level, i = pieces.pop()
                count = ROWS >> level + 1
                listed = slice(sub_start(level), sub_start(level) + count)
                at = slice(row_start(level) + i * 256, row_start(level) + i * 256 + 256)
                pick = chosen(level, i)
                moved_high[at, :] = jnp.dot(pick, update_high[listed, :], preferred_element_type=F32).astype(BF16)
                moved_low[at, :] = jnp.dot(pick, update_low[listed, :], preferred_element_type=F32).astype(BF16)

    coupling_terms(2)
    node_terms(2, ut2)
    c2 = send(ut2.at[:, other, :], b2c, sibling)
    coupling_terms(1)
    node_terms(1, ut1)
    c1 = send(ut1.at[:, other, :], b1c, sibling)
    c2.wait_recv()
    add_own(b2c, ut2)
    x2s = [send(b2c.at[xs(a)], b2x.at[a - 1], device(xs(a), y, z, c)) for a in range(1, NX)]
    coupling_terms(0)
    ring_step()
    c1.wait_recv()
    add_own(b1c, ut1)
    x1s = [send(b1c.at[pl.ds(xs(a) * 2, 2)], b1x.at[a - 1], device(xs(a), y, z, c)) for a in range(1, NX)]
    node_terms(0, ut0)
    c0 = send(ut0.at[:, other, :], b0c, sibling)

    arrive(x2s)
    b2s[...] = b2c[x] + b2x[0] + b2x[1] + b2x[2]
    z2s = z_stage(b2s, b2z)
    c0.wait_recv()
    add_own(b0c, ut0)
    y0s = [send(b0c.at[pl.ds(ys(b) * NX, NX)], b0y.at[b - 1], device(x, ys(b), z, c)) for b in range(1, NY)]
    ring_step()
    work(1)
    arrive(x1s)
    for i in range(2):
        b1s[i] = b1c[x * 2 + i] + b1x[0, i] + b1x[1, i] + b1x[2, i]
    y1s = send(b1s.at[1 - yy], b1y, device(x, partner, z, c))

    r2 = z_sum(b2s, b2z, z2s)
    g2[x] = r2
    a2 = [send(g2.at[x], g2.at[x], device(xs(a), y, z, c)) for a in range(1, NX)]
    work(1)
    y1s.wait_recv()
    b1t[...] = b1s[yy] + b1y[...]
    z1s = z_stage(b1t, b1z)
    work(1)
    ring_step()
    arrive(shared)

    def joined(ref):
        return jnp.concatenate([ref[i] for i in range(ref.shape[0])], axis=1)

    def spill(value, ref):
        for i in range(ref.shape[0]):
            ref[i] = value[:, i * LANES : (i + 1) * LANES]

    def columns(start, size):
        return m_ref[:, :, :, start : start + size].reshape(LANES, size)

    here1 = yy * NX + x
    here0 = y * NX + x

    def scatter_half(part, landed):
        return [
            send(part.at[(yy if b == 0 else 1 - yy) * NX + xs(a)], landed.at[k], device(xs(a), pair_y(b), z, c))
            for k, (a, b) in enumerate(half)
        ]

    def gather_half(whole):
        return [send(whole.at[here1], whole.at[here1], device(xs(a), pair_y(b), z, c)) for a, b in half]

    def scatter_plane(part, landed):
        return [
            send(part.at[ys(b) * NX + xs(a)], landed.at[k], device(xs(a), ys(b), z, c))
            for k, (a, b) in enumerate(plane)
        ]

    def gather_plane(whole):
        return [send(whole.at[here0], whole.at[here0], device(xs(a), ys(b), z, c)) for a, b in plane]

    def summed(part, here, landed, batch):
        arrive(batch)
        total = part[here]
        for k in range(landed.shape[0]):
            total = total + landed[k]
        return total

    s0_scale, s1_scale = weight_scale(0), weight_scale(1)

    arrive(a2)
    solved2 = small_dot(joined(g2), columns(G2, 512), NT)
    spill(small_dot(solved2, columns(E21, 1024), NN), p1)
    batch = scatter_half(p1, p1r)
    work(1)
    arrive(y0s)
    for i in range(NX):
        b0s[i] = b0c[y * NX + i] + b0y[0, i] + b0y[1, i] + b0y[2, i]
    x0s = [send(b0s.at[xs(a)], b0x.at[a - 1], device(xs(a), y, z, c)) for a in range(1, NX)]
    r1 = z_sum(b1t, b1z, z1s)
    g1[here1] = r1 - s1_scale * summed(p1, here1, p1r, batch)
    batch = gather_half(g1)
    up0 = small_dot(solved2, columns(E20, 2048), NN)
    work(1)
    arrive(x0s)
    b0t[...] = b0s[x] + b0x[0] + b0x[1] + b0x[2]
    z0s = z_stage(b0t, b0z)
    arrive(batch)
    solved1 = small_dot(joined(g1), columns(G1, 1024), NT)
    spill(up0 + small_dot(solved1, columns(E10, 2048), NN), p0)
    batch = scatter_plane(p0, p0r)
    work(2)
    r0 = z_sum(b0t, b0z, z0s)
    g0[here0] = r0 - s0_scale * summed(p0, here0, p0r, batch)
    batch = gather_plane(g0)
    work(2)
    arrive(batch)
    solved0 = small_dot(joined(g0), columns(G0, 2048), NT)

    def hand_out(whole, result):
        result[:, spread, :] = whole[...]
        return [send(whole, result.at[:, spread, :], device(x, y, zs(d), c)) for d in range(1, NZ)]

    spill(small_dot(solved0, columns(G0, 2048), NN), q0)
    batch = scatter_plane(q0, q0r)
    work(2)
    h0[here0] = summed(q0, here0, q0r, batch)
    batch = gather_plane(h0)
    work(2)
    arrive(batch)
    d0s = hand_out(h0, x0)
    found0 = joined(h0)
    y1 = solved1 - s0_scale * small_dot(found0, columns(E10, 2048), NT)
    spill(small_dot(y1, columns(G1, 1024), NN), q1)
    batch = scatter_half(q1, q1r)
    work(2)
    y2 = solved2 - s0_scale * small_dot(found0, columns(E20, 2048), NT)
    h1[here1] = summed(q1, here1, q1r, batch)
    batch = gather_half(h1)
    work(99)
    arrive(batch)
    d1s = hand_out(h1, x1)
    y2 = y2 - s1_scale * small_dot(joined(h1), columns(E21, 1024), NT)
    spill(small_dot(y2, columns(G2, 512), NN), q2)
    batch = [send(q2.at[xs(a)], q2r.at[a - 1], device(xs(a), y, z, c)) for a in range(1, NX)]
    h2[x] = summed(q2, x, q2r, batch)
    arrive([send(h2.at[x], h2.at[x], device(xs(a), y, z, c)) for a in range(1, NX)])
    d2s = hand_out(h2, x2)

    def swap_cores(result, batch):
        arrive(batch)
        return send(result.at[:, mine, :], result.at[:, mine, :], sibling)

    def take_in(level, result, copy):
        copy.wait_recv()

        def step(i, carry):
            at = pl.ds(pl.multiple_of(row_start(level) + i * 256, 256), 256)
            both = jnp.concatenate([result[2 * i], result[2 * i + 1]], axis=1)
            high, low = split(both)
            stacked = jnp.concatenate([high, low], axis=0)
            first = jnp.dot(stacked, moved_high[at, :], preferred_element_type=F32)
            second = jnp.dot(high, moved_low[at, :], preferred_element_type=F32)
            current[...] = current[...] - weight_scale(level) * (first[:RHS] + first[RHS:] + second)
            return carry

        lax.fori_loop(0, (ROWS >> level) // 256, step, 0)
        chunk = [here0, here1, x][level]
        out_sep[level] = lax.dot_general(
            mark, result[chunk], NT, precision=lax.Precision.HIGHEST, preferred_element_type=F32
        )

    w0 = swap_cores(x0, d0s)
    w1 = swap_cores(x1, d1s)
    take_in(0, x0, w0)
    w2 = swap_cores(x2, d2s)
    take_in(1, x1, w1)
    take_in(2, x2, w2)
    out_sub[...] = small_dot(current[...] * scale, inverse[...], NN).T
    for copy in copies:
        copy.wait_send()


N_COPIES = 3 + 3 + 3 + 3 + 7 + 1 + 3 + 7 + 3 + 7 + 7 + 7 + 15 + 15 + 15 + 15 + 7 + 7 + 7 + 7 + 3 + 3 + 7 + 3 + 8 + 8


def whole(*operands):
    def piece(*lead, rows=COLS):
        return pltpu.VMEM((*lead, rows, LANES), F32)

    scratch = [
        pltpu.VMEM((LOC, LOC), F32), pltpu.VMEM((LOC, RHS), F32), pltpu.VMEM((1792, LOC), F32),
        pltpu.VMEM((LOC, LOC), F32), pltpu.VMEM((RHS, LOC), F32), pltpu.VMEM((RHS, LOC), F32),
        pltpu.VMEM((2 * RHS, 1792), BF16), pltpu.VMEM((1792, LOC), BF16), pltpu.VMEM((1792, LOC), BF16),
        pltpu.VMEM((3584, LOC), BF16), pltpu.VMEM((3584, LOC), BF16),
        piece(16, rows=RHS), piece(8, rows=RHS), piece(4, rows=RHS),
        pltpu.VMEM((NZ, 2, BLK, WIDE), F32),
        piece(16, rows=RHS), piece(8, rows=RHS), piece(4, rows=RHS),
        piece(4, rows=LANES), piece(8, rows=LANES), piece(16, rows=LANES),
        piece(3, rows=LANES), piece(rows=LANES), piece(7),
        piece(3, 2, rows=LANES), piece(2, rows=LANES), piece(rows=LANES), piece(rows=LANES), piece(7),
        piece(3, 4, rows=LANES), piece(4, rows=LANES), piece(3, rows=LANES), piece(rows=LANES), piece(7),
        piece(4), piece(8), piece(7), piece(8), piece(16), piece(15), piece(16),
        piece(16), piece(15), piece(16), piece(8), piece(7), piece(8), piece(4), piece(3), piece(4),
        pltpu.SemaphoreType.DMA((3,)), pltpu.SemaphoreType.DMA((N_COPIES,)), pltpu.SemaphoreType.DMA((N_COPIES,)),
    ]
    vmem = pl.BlockSpec(memory_space=pltpu.VMEM)
    hbm = pl.BlockSpec(memory_space=pl.ANY)
    return pl.pallas_call(
        whole_kernel,
        out_shape=[jax.ShapeDtypeStruct((LOC, RHS), F32), jax.ShapeDtypeStruct((LEVELS, BLK, RHS), F32)],
        in_specs=[vmem] * 6 + [hbm] * 3,
        out_specs=[vmem] * 2,
        scratch_shapes=scratch,
        compiler_params=pltpu.CompilerParams(
            collective_id=0, has_side_effects=True, vmem_limit_bytes=58 * 1024 * 1024
        ),
    )(*operands)


def body(rhs_sub, rhs_sep, sub_factor, sub_diag, sep_factor, sep_diag, sub_update, update_rows, sep_update):
    result_sub, result_sep = whole(
        sub_diag, update_rows, rhs_sep, sep_factor, sep_diag, sep_update[0].T, sub_factor[0], rhs_sub[0], sub_update[0]
    )
    return result_sub[None], result_sep


def solution(mesh):
    both = ("leaf", "panel")
    in_specs = (
        P(both, None, None), P(None, both, None), P(both, None, None), P(both, None), P(both, None),
        P(None, both), P(both, None, None), P(both, None), P(both, None, None),
    )
    out_specs = (P(both, None, None), P(None, both, None))
    return jax.shard_map(body, mesh=mesh, in_specs=in_specs, out_specs=out_specs, check_vma=False)
```

```python
import jax
import jax.numpy as jnp
from jax import lax
from jax.experimental import pallas as pl
from jax.experimental.pallas import tpu as pltpu
from jax.sharding import PartitionSpec as P

MESH = pl.DeviceIdType.MESH
F32 = jnp.float32
BF16 = jnp.bfloat16
NN = (((1,), (0,)), ((), ()))
NT = (((1,), (1,)), ((), ()))
TN = (((0,), (0,)), ((), ()))

NX, NY, NZ = 4, 4, 8
ROWS, RHS, LOC, BLK = 2048, 256, 512, 8
LEVELS = 3
LANES = 128
COLS = 16
G2, E21, G1, E20, E10, G0, WIDE = 0, 512, 1536, 2560, 4608, 6656, 8704


def weight_scale(target):
    fan_total = (256 >> target) * LOC // 2 + (LEVELS - 1 - target) * (ROWS >> target)
    return float(fan_total) ** (-0.5)


def split(value):
    high = value.astype(BF16)
    return high, (value - high.astype(F32)).astype(BF16)


def small_dot(left, right, dims):
    left_high, left_low = split(left)
    right_high, right_low = split(right)
    rows = left.shape[0]
    both = jnp.concatenate([left_high, left_low], axis=0)
    first = lax.dot_general(both, right_high, dims, preferred_element_type=F32)
    second = lax.dot_general(left_high, right_low, dims, preferred_element_type=F32)
    return first[:rows] + first[rows:] + second


def place():
    leaf, panel = lax.axis_index("leaf"), lax.axis_index("panel")
    return panel // 2, leaf // NZ, leaf % NZ, panel % 2


def device(x, y, z, c):
    return (y * NZ + z, x * 2 + c)


def hops(step, size):
    return min(step, size - step)


X_PEERS = (2, 1, 3)
Y_PEERS = (2, 1, 3)
Z_PEERS = (4, 3, 5, 2, 6, 1, 7)
PLANE = sorted(
    [(a, b) for a in range(NX) for b in range(NY)][1:], key=lambda ab: -hops(ab[0], NX) - hops(ab[1], NY)
)
HALF = sorted([(a, b) for a in range(NX) for b in range(2)][1:], key=lambda ab: -hops(ab[0], NX) - ab[1])
ROUNDS = ((0, 1536), (1536, 4608), (4608, 8704))


def split3(value):
    high = value.astype(BF16)
    rest = value - high.astype(F32)
    middle = rest.astype(BF16)
    return high, middle, (rest - middle.astype(F32)).astype(BF16)


def exact_dot(left, right):
    return jnp.dot(left, right, precision=lax.Precision.HIGHEST, preferred_element_type=F32)


def iota(shape, dim):
    return lax.broadcasted_iota(jnp.int32, shape, dim)


def reorder(rows):
    return (rows >> 9 << 9) + ((rows >> 4 & 3) << 7) + ((rows >> 6 & 7) << 4) + (rows & 15)


def sub_start(level):
    return sum(ROWS >> k + 1 for k in range(level))


def row_start(level):
    return sum(ROWS >> k for k in range(level))


def invert(factor, scale, inverse):
    lane = iota((32, LANES), 1)
    row, col = iota((LANES, LANES), 0), iota((LANES, LANES), 1)
    blocks, packed = [], []
    for g in range(4):
        at = slice(g * LANES, (g + 1) * LANES)
        block = jnp.where(row > col, factor[at, at] * scale[:, at], 0.0)
        blocks.append(block)
        parts = [jnp.where(lane >> 5 == q, block[32 * q : 32 * q + 32], 0.0) for q in range(4)]
        packed.append(parts[0] + parts[1] + parts[2] + parts[3])
    unit = (iota((32, LANES), 0) == (lane & 31)).astype(F32)
    found = [unit] * 4
    for k in range(31):
        index = (lane & 96) + k
        for g in range(4):
            coefficient = jnp.take_along_axis(packed[g], index, axis=1, mode="promise_in_bounds")
            found[g] = found[g] - coefficient * found[g][k : k + 1, :]
    whole = []
    for g in range(4):
        total = jnp.concatenate([jnp.where(lane >> 5 == q, found[g], 0.0) for q in range(4)], axis=0)
        whole.append(total)
    for bit in (5, 6):
        below = (row >> bit + 1 == col >> bit + 1) & (row >> bit > col >> bit)
        inner = [exact_dot(jnp.where(below, blocks[g], 0.0), whole[g]) for g in range(4)]
        whole = [whole[g] - exact_dot(whole[g], inner[g]) for g in range(4)]
    inverse[...] = jnp.zeros_like(inverse)
    for h in range(2):
        first = slice(h * 256, h * 256 + 128)
        second = slice(h * 256 + 128, h * 256 + 256)
        inner = exact_dot(factor[second, first] * scale[:, first], whole[2 * h])
        inverse[first, first] = whole[2 * h]
        inverse[second, second] = whole[2 * h + 1]
        inverse[second, first] = -exact_dot(whole[2 * h + 1], inner)
    inner = exact_dot(factor[256:, :256] * scale[:, :256], inverse[:256, :256])
    inverse[256:, :256] = -exact_dot(inverse[256:, 256:], inner)


def separator_rows(sep_factor, sep_diag, turned, position):
    inverses = []
    eye = iota((BLK, BLK), 0) == iota((BLK, BLK), 1)
    for level in range(LEVELS):
        node_rows = ROWS >> level
        start = row_start(level)
        strict = sep_factor[:, start : start + node_rows]
        diagonal = jnp.sum(jnp.where(eye, sep_diag[level : level + 1, :], 0.0), axis=1, keepdims=True)
        own = position % (256 >> level) * BLK + iota((BLK, node_rows), 0)
        cols = iota((BLK, node_rows), 1)
        inverses.append(jnp.where(cols < own, strict, 0.0) + jnp.where(cols == own, diagonal, 0.0))
    e10, e20, e21 = turned[:, :2048], turned[:, 2048:4096], turned[:, 4096:]
    pieces = [inverses[2], e21, inverses[1], e20, e10, inverses[0]]
    blocks = [piece[:, i : i + 512] for piece in pieces for i in range(0, piece.shape[1], 512)]
    stacked = jnp.concatenate(blocks, axis=0)
    swap = jnp.where(reorder(iota((512, 512), 0)) == iota((512, 512), 1), 1.0, 0.0).astype(BF16)
    high, middle, low = split3(stacked)
    return (
        jnp.dot(high, swap, preferred_element_type=F32)
        + jnp.dot(middle, swap, preferred_element_type=F32)
        + jnp.dot(low, swap, preferred_element_type=F32)
    )


def whole_kernel(
    diag, rows, rhs_sep, sep_factor, sep_diag, turned, factor_hbm, rhs_hbm, update_hbm,
    out_sub, out_sep,
    factor, rhs, update, inverse, solved_t, current, terms, update_high, update_low, moved_high, moved_low,
    ut0, ut1, ut2, m_ref, x0, x1, x2,
    b2c, b1c, b0c, b2x, b2s, b2z, b1x, b1s, b1y, b1t, b1z, b0y, b0x, b0p, b0q, b0u, b0v, b0t, b0z,
    g2, p1, p1r, g1, p0, p0r, g0, q0, q0r, h0, q1, q1r, h1, q2, q2r, h2,
    lsem, ssem, rsem,
):
    x, y, z, c = place()
    position = lax.axis_index("leaf") * 8 + lax.axis_index("panel")
    partner = y + 1 - 2 * (y % 2)
    yy = y % 2
    sibling = device(x, y, z, 1 - c)
    loads = [
        pltpu.make_async_copy(src, dst, lsem.at[i])
        for i, (src, dst) in enumerate(((factor_hbm, factor), (rhs_hbm, rhs), (update_hbm, update)))
    ]
    for load in loads:
        load.start()

    def xs(a):
        return (x + a) % NX

    def ys(b):
        return (y + b) % NY

    def zs(d):
        return (z + d) % NZ

    def pair_y(b):
        return partner if b else y

    barrier = pltpu.get_barrier_semaphore()
    greeted = [device(xs(a), ys(b), z, c) for a, b in PLANE]
    greeted += [device(x, y, zs(d), c) for d in range(1, NZ)] + [sibling]
    for peer in greeted:
        pl.semaphore_signal(barrier, inc=1, device_id=peer, device_id_type=MESH)

    copies = []

    def send(src, dst, peer):
        at = len(copies)
        copy = pltpu.make_async_remote_copy(
            src_ref=src, dst_ref=dst, send_sem=ssem.at[at], recv_sem=rsem.at[at],
            device_id=peer, device_id_type=MESH,
        )
        copy.start()
        copies.append(copy)
        return copy

    def arrive(batch):
        for copy in batch:
            copy.wait_recv()

    own_rows = separator_rows(sep_factor, sep_diag, turned, position)
    for i in range(WIDE // 512):
        m_ref[z, c, :, i * 512 : (i + 1) * 512] = own_rows[i * BLK : (i + 1) * BLK]
    pl.semaphore_wait(barrier, len(greeted))

    right, left = device(x, y, zs(1), c), device(x, y, zs(NZ - 1), c)

    def pass_on(block, start, size, peer):
        ref = m_ref.at[block, c, :, pl.ds(start, size)]
        return send(ref, ref, peer)

    ring, steps, shared = [], [1] * len(ROUNDS), [None] * len(ROUNDS)
    for start, stop in ROUNDS:
        ring.append([pass_on(z, start, stop - start, right), pass_on(z, start, stop - start, left)])

    def advance(turn):
        step = steps[turn]
        steps[turn] = step + 1
        start, stop = ROUNDS[turn]
        size = stop - start
        from_left, from_right = zs(NZ - step), zs(step)
        arrive(ring[turn])
        if step < 3:
            ring[turn] = [pass_on(from_left, start, size, right), pass_on(from_right, start, size, left)]
        elif step == 3:
            ring[turn] = [
                pass_on(from_left, start, size // 2, right),
                pass_on(from_right, start + size // 2, size // 2, left),
            ]
        else:
            ref = m_ref.at[:, c, :, pl.ds(start, size)]
            shared[turn] = [send(ref, ref, sibling)]

    scale = 1.0 / diag[...]
    loads[0].wait()
    invert(factor, scale, inverse)
    loads[1].wait()
    right_t = rhs[...].T
    solved_t[...] = small_dot(right_t, inverse[...], NT) * scale
    current[...] = solved_t[...]
    advance(0)
    loads[2].wait()
    solved_high, solved_low = split(solved_t[...])
    solved_both = jnp.concatenate([solved_high, solved_low], axis=0)

    def coupling_terms(level):
        def step(i, carry):
            at = pl.ds(pl.multiple_of(sub_start(level) + i * 256, 256), 256)
            high, low = split(update[at, :])
            update_high[at, :] = high
            update_low[at, :] = low
            first = lax.dot_general(solved_both, high, NT, preferred_element_type=F32)
            second = lax.dot_general(solved_high, low, NT, preferred_element_type=F32)
            top, bottom = split(first[:RHS] + first[RHS:] + second)
            terms[:RHS, at] = top
            terms[RHS:, at] = bottom
            return carry

        lax.fori_loop(0, (ROWS >> level) // 512, step, 0)

    places = []
    for level in range(LEVELS):
        count = ROWS >> level + 1
        places.append(reorder(rows[:, sub_start(level) : sub_start(level) + count]))

    def chosen(level, i):
        count = ROWS >> level + 1
        ids = iota((256, count), 0) + i * 256
        return jnp.where(ids == places[level], 1.0, 0.0).astype(BF16)

    mark = jnp.where(iota((BLK, LANES), 1) == z * 16 + c * BLK + iota((BLK, LANES), 0), 1.0, 0.0)

    def node_terms(level, ut, first, last):
        count = ROWS >> level + 1
        listed = terms[:, sub_start(level) : sub_start(level) + count]

        def step(i, carry):
            both = lax.dot_general(listed, chosen(level, i), NT, preferred_element_type=F32)
            total = (both[:RHS] + both[RHS:]) * -weight_scale(level)
            for k in range(2):
                part = total[:, k * LANES : (k + 1) * LANES]
                if level == 0:
                    ut[i // 2, i % 2 * 2 + k] = part
                elif level == 1:
                    ut[(i % 2 * 2 + k) * 2 + i // 2] = part
                else:
                    ut[2 * i + k] = part
            return carry

        lax.fori_loop(first, last, step, 0)

    def own_term(level):
        return lax.dot_general(
            rhs_sep[level], mark, TN, precision=lax.Precision.HIGHEST, preferred_element_type=F32
        )

    mine = pl.ds(pl.multiple_of(c * LANES, LANES), LANES)
    other = pl.ds(pl.multiple_of((1 - c) * LANES, LANES), LANES)
    cols = pl.ds(pl.multiple_of(z * COLS, COLS), COLS)
    spread = pl.ds(pl.multiple_of(c * LANES + z * COLS, COLS), COLS)

    def add_own(total, own):
        def step(i, carry):
            total[i] = total[i] + own[i, mine, :]
            return carry

        lax.fori_loop(0, total.shape[0], step, 0)

    def z_stage(summed, parts):
        return [
            send(summed.at[pl.ds(pl.multiple_of(zs(d) * COLS, COLS), COLS), :], parts.at[d - 1], device(x, y, zs(d), c))
            for d in Z_PEERS
        ]

    def z_sum(summed, parts, batch):
        arrive(batch)
        total = summed[cols, :]
        for d in range(NZ - 1):
            total = total + parts[d]
        return total

    pieces = [(2, i) for i in range(2)] + [(1, i) for i in range(4)] + [(0, i) for i in range(8)]

    def work(amount):
        for _ in range(amount):
            if pieces:
                level, i = pieces.pop()
                count = ROWS >> level + 1
                listed = slice(sub_start(level), sub_start(level) + count)
                at = slice(row_start(level) + i * 256, row_start(level) + i * 256 + 256)
                pick = chosen(level, i)
                moved_high[at, :] = jnp.dot(pick, update_high[listed, :], preferred_element_type=F32).astype(BF16)
                moved_low[at, :] = jnp.dot(pick, update_low[listed, :], preferred_element_type=F32).astype(BF16)

    def x_send(piece, landed):
        return [send(piece(xs(a)), landed.at[a - 1], device(xs(a), y, z, c)) for a in X_PEERS]

    def y_send(piece, landed):
        return [send(piece(ys(b)), landed.at[b - 1], device(x, ys(b), z, c)) for b in Y_PEERS]

    coupling_terms(2)
    node_terms(2, ut2, 0, 2)
    ut2[x] = ut2[x] + own_term(2)
    c2 = send(ut2.at[:, other, :], b2c, sibling)
    advance(1)
    coupling_terms(1)
    node_terms(1, ut1, 0, 4)
    ut1[x * 2 + yy] = ut1[x * 2 + yy] + own_term(1)
    c1 = send(ut1.at[:, other, :], b1c, sibling)
    arrive([c2])
    add_own(b2c, ut2)
    x2s = x_send(lambda to: b2c.at[to], b2x)
    advance(0)
    coupling_terms(0)
    advance(2)
    arrive([c1])
    add_own(b1c, ut1)
    x1s = x_send(lambda to: b1c.at[pl.ds(to * 2, 2)], b1x)
    node_terms(0, ut0, 0, 2)
    advance(1)
    node_terms(0, ut0, 2, 4)
    lower = jnp.where(y < 2, 1.0, 0.0)
    own0 = own_term(0)
    ut0[y % 2, x] = ut0[y % 2, x] + own0 * lower
    c0a = send(ut0.at[0:2, :, other, :], b0c.at[0:2], sibling)
    advance(0)
    arrive(x2s)
    b2s[...] = b2c[x] + b2x[0] + b2x[1] + b2x[2]
    z2s = z_stage(b2s, b2z)
    node_terms(0, ut0, 4, 6)
    advance(2)
    node_terms(0, ut0, 6, 8)
    ut0[2 + y % 2, x] = ut0[2 + y % 2, x] + own0 * (1.0 - lower)
    c0b = send(ut0.at[2:4, :, other, :], b0c.at[2:4], sibling)
    advance(1)

    def add_rows(first):
        def step(i, carry):
            for k in range(NX):
                b0c[first + i, k] = b0c[first + i, k] + ut0[first + i, k, mine, :]
            return carry

        lax.fori_loop(0, 2, step, 0)

    arrive([c0a])
    add_rows(0)
    arrive([c0b])
    add_rows(2)
    mid = LANES // 2
    y0s = y_send(lambda to: b0c.at[to, :, 0:mid, :], b0y)
    x0s = x_send(lambda to: b0c.at[:, to, mid:LANES, :], b0x)
    advance(0)
    r2 = z_sum(b2s, b2z, z2s)
    g2[x] = r2
    a2 = [send(g2.at[x], g2.at[x], device(xs(a), y, z, c)) for a in X_PEERS]
    advance(2)
    arrive(x1s)
    for i in range(2):
        b1s[i] = b1c[x * 2 + i] + b1x[0, i] + b1x[1, i] + b1x[2, i]
    y1s = send(b1s.at[1 - yy], b1y, device(x, partner, z, c))
    work(1)
    arrive([y1s])
    b1t[...] = b1s[yy] + b1y[...]
    z1s = z_stage(b1t, b1z)

    def joined(ref):
        return jnp.concatenate([ref[i] for i in range(ref.shape[0])], axis=1)

    def spill(value, ref):
        for i in range(ref.shape[0]):
            ref[i] = value[:, i * LANES : (i + 1) * LANES]

    def columns(start, size):
        return m_ref[:, :, :, start : start + size].reshape(LANES, size)

    here1 = yy * NX + x
    here0 = y * NX + x

    def scatter_half(part, landed):
        return [
            send(part.at[(yy if b == 0 else 1 - yy) * NX + xs(a)], landed.at[k], device(xs(a), pair_y(b), z, c))
            for k, (a, b) in enumerate(HALF)
        ]

    def gather_half(whole):
        return [send(whole.at[here1], whole.at[here1], device(xs(a), pair_y(b), z, c)) for a, b in HALF]

    def scatter_plane(part, landed):
        return [
            send(part.at[ys(b) * NX + xs(a)], landed.at[k], device(xs(a), ys(b), z, c))
            for k, (a, b) in enumerate(PLANE)
        ]

    def gather_plane(whole):
        return [send(whole.at[here0], whole.at[here0], device(xs(a), ys(b), z, c)) for a, b in PLANE]

    def summed(part, here, landed, batch):
        arrive(batch)
        total = part[here]
        for k in range(landed.shape[0]):
            total = total + landed[k]
        return total

    s0_scale, s1_scale = weight_scale(0), weight_scale(1)

    arrive(shared[0])
    arrive(a2)
    solved2 = small_dot(joined(g2), columns(G2, 512), NT)
    spill(small_dot(solved2, columns(E21, 1024), NN), p1)
    p1s = scatter_half(p1, p1r)
    advance(1)
    work(1)
    arrive(y0s)
    for i in range(NX):
        b0p[i] = b0c[y, i, 0:mid, :] + b0y[0, i] + b0y[1, i] + b0y[2, i]
    x0t = x_send(lambda to: b0p.at[to], b0u)
    arrive(x0s)
    for i in range(NY):
        b0q[i] = b0c[i, x, mid:LANES, :] + b0x[0, i] + b0x[1, i] + b0x[2, i]
    y0t = y_send(lambda to: b0q.at[to], b0v)
    r1 = z_sum(b1t, b1z, z1s)
    g1[here1] = r1 - s1_scale * summed(p1, here1, p1r, p1s)
    a1 = gather_half(g1)
    arrive(shared[1])
    up0 = small_dot(solved2, columns(E20, 2048), NN)
    advance(2)
    arrive(x0t)
    b0t[0:mid, :] = b0p[x] + b0u[0] + b0u[1] + b0u[2]
    arrive(y0t)
    b0t[mid:LANES, :] = b0q[y] + b0v[0] + b0v[1] + b0v[2]
    z0s = z_stage(b0t, b0z)
    arrive(a1)
    solved1 = small_dot(joined(g1), columns(G1, 1024), NT)
    arrive(shared[2])
    spill(up0 + small_dot(solved1, columns(E10, 2048), NN), p0)
    p0s = scatter_plane(p0, p0r)
    work(2)
    r0 = z_sum(b0t, b0z, z0s)
    g0[here0] = r0 - s0_scale * summed(p0, here0, p0r, p0s)
    a0 = gather_plane(g0)
    work(2)
    arrive(a0)
    solved0 = small_dot(joined(g0), columns(G0, 2048), NT)

    def block_of(d):
        return pl.ds(pl.multiple_of(c * LANES + zs(d) * COLS, COLS), COLS)

    def along_z(chunk, at, result):
        result[at, spread, :] = chunk[at]
        return [send(chunk.at[at], result.at[at, spread, :], device(x, y, zs(d), c)) for d in Z_PEERS]

    spill(small_dot(solved0, columns(G0, 2048), NN), q0)
    q0s = scatter_plane(q0, q0r)
    work(2)
    h0[here0] = summed(q0, here0, q0r, q0s)
    a0 = gather_plane(h0)
    work(2)
    arrive(a0)
    x0[:, spread, :] = h0[...]
    far0, near0 = [
        [send(h0, x0.at[:, spread, :], device(x, y, zs(d), c)) for d in ds] for ds in ((2, 6), (1, 7))
    ]
    found0 = joined(h0)
    y1 = solved1 - s0_scale * small_dot(found0, columns(E10, 2048), NT)
    spill(small_dot(y1, columns(G1, 1024), NN), q1)
    q1s = scatter_half(q1, q1r)
    y2 = solved2 - s0_scale * small_dot(found0, columns(E20, 2048), NT)
    work(1)
    h1[here1] = summed(q1, here1, q1r, q1s)
    a1 = gather_half(h1)
    z1h = along_z(h1, here1, x1)
    work(2)
    arrive(a1)
    y2 = y2 - s1_scale * small_dot(joined(h1), columns(E21, 1024), NT)
    spill(small_dot(y2, columns(G2, 512), NN), q2)
    q2s = x_send(lambda to: q2.at[to], q2r)
    arrive(far0)
    low, high = block_of(6), block_of(2)
    far0 = [
        send(x0.at[:, low, :], x0.at[:, low, :], device(x, y, zs(1), c)),
        send(x0.at[:, high, :], x0.at[:, high, :], device(x, y, zs(7), c)),
        send(x0.at[0:8, low, :], x0.at[0:8, low, :], device(x, y, zs(2), c)),
        send(x0.at[8:16, high, :], x0.at[8:16, high, :], device(x, y, zs(6), c)),
    ]
    h2[x] = summed(q2, x, q2r, q2s)
    z2h = along_z(h2, x, x2)
    arrive(z1h)
    w1 = [send(x1.at[here1, mine, :], x1.at[here1, mine, :], device(xs(a), pair_y(b), z, c)) for a, b in HALF]
    work(99)
    arrive(near0)
    arrive(z2h)
    w2 = [send(x2.at[x, mine, :], x2.at[x, mine, :], device(xs(a), y, z, c)) for a in X_PEERS]

    def swap_cores(result, batch):
        arrive(batch)
        return send(result.at[:, mine, :], result.at[:, mine, :], sibling)

    def take_in(level, result, copy):
        arrive([copy])

        def step(i, carry):
            at = pl.ds(pl.multiple_of(row_start(level) + i * 256, 256), 256)
            both = jnp.concatenate([result[2 * i], result[2 * i + 1]], axis=1)
            high, low = split(both)
            stacked = jnp.concatenate([high, low], axis=0)
            first = jnp.dot(stacked, moved_high[at, :], preferred_element_type=F32)
            second = jnp.dot(high, moved_low[at, :], preferred_element_type=F32)
            current[...] = current[...] - weight_scale(level) * (first[:RHS] + first[RHS:] + second)
            return carry

        lax.fori_loop(0, (ROWS >> level) // 256, step, 0)
        chunk = [here0, here1, x][level]
        out_sep[level] = lax.dot_general(
            mark, result[chunk], NT, precision=lax.Precision.HIGHEST, preferred_element_type=F32
        )

    w0 = swap_cores(x0, far0)
    take_in(0, x0, w0)
    w1 = swap_cores(x1, w1)
    w2 = swap_cores(x2, w2)
    take_in(1, x1, w1)
    take_in(2, x2, w2)
    out_sub[...] = small_dot(current[...] * scale, inverse[...], NN).T
    for copy in copies:
        copy.wait_send()


N_COPIES = 256


def whole(*operands):
    def piece(*lead, rows=COLS):
        return pltpu.VMEM((*lead, rows, LANES), F32)

    scratch = [
        pltpu.VMEM((LOC, LOC), F32), pltpu.VMEM((LOC, RHS), F32), pltpu.VMEM((1792, LOC), F32),
        pltpu.VMEM((LOC, LOC), F32), pltpu.VMEM((RHS, LOC), F32), pltpu.VMEM((RHS, LOC), F32),
        pltpu.VMEM((2 * RHS, 1792), BF16), pltpu.VMEM((1792, LOC), BF16), pltpu.VMEM((1792, LOC), BF16),
        pltpu.VMEM((3584, LOC), BF16), pltpu.VMEM((3584, LOC), BF16),
        piece(4, 4, rows=RHS), piece(8, rows=RHS), piece(4, rows=RHS),
        pltpu.VMEM((NZ, 2, BLK, WIDE), F32),
        piece(16, rows=RHS), piece(8, rows=RHS), piece(4, rows=RHS),
        piece(4, rows=LANES), piece(8, rows=LANES), piece(4, 4, rows=LANES),
        piece(3, rows=LANES), piece(rows=LANES), piece(7),
        piece(3, 2, rows=LANES), piece(2, rows=LANES), piece(rows=LANES), piece(rows=LANES), piece(7),
        piece(3, 4, rows=64), piece(3, 4, rows=64), piece(4, rows=64), piece(4, rows=64),
        piece(3, rows=64), piece(3, rows=64), piece(rows=LANES), piece(7),
        piece(4), piece(8), piece(7), piece(8), piece(16), piece(15), piece(16),
        piece(16), piece(15), piece(16), piece(8), piece(7), piece(8), piece(4), piece(3), piece(4),
        pltpu.SemaphoreType.DMA((3,)), pltpu.SemaphoreType.DMA((N_COPIES,)), pltpu.SemaphoreType.DMA((N_COPIES,)),
    ]
    vmem = pl.BlockSpec(memory_space=pltpu.VMEM)
    hbm = pl.BlockSpec(memory_space=pl.ANY)
    return pl.pallas_call(
        whole_kernel,
        out_shape=[jax.ShapeDtypeStruct((LOC, RHS), F32), jax.ShapeDtypeStruct((LEVELS, BLK, RHS), F32)],
        in_specs=[vmem] * 6 + [hbm] * 3,
        out_specs=[vmem] * 2,
        scratch_shapes=scratch,
        compiler_params=pltpu.CompilerParams(
            collective_id=0, has_side_effects=True, vmem_limit_bytes=58 * 1024 * 1024
        ),
    )(*operands)


def body(rhs_sub, rhs_sep, sub_factor, sub_diag, sep_factor, sep_diag, sub_update, update_rows, sep_update):
    result_sub, result_sep = whole(
        sub_diag, update_rows, rhs_sep, sep_factor, sep_diag, sep_update[0].T, sub_factor[0], rhs_sub[0], sub_update[0]
    )
    return result_sub[None], result_sep


def solution(mesh):
    both = ("leaf", "panel")
    in_specs = (
        P(both, None, None), P(None, both, None), P(both, None, None), P(both, None), P(both, None),
        P(None, both), P(both, None, None), P(both, None), P(both, None, None),
    )
    out_specs = (P(both, None, None), P(None, both, None))
    return jax.shard_map(body, mesh=mesh, in_specs=in_specs, out_specs=out_specs, check_vma=False)
```

```python
import jax
import jax.numpy as jnp
from jax import lax
from jax.experimental import pallas as pl
from jax.experimental.pallas import tpu as pltpu
from jax.sharding import PartitionSpec as P

MESH = pl.DeviceIdType.MESH
F32 = jnp.float32
BF16 = jnp.bfloat16
NN = (((1,), (0,)), ((), ()))
NT = (((1,), (1,)), ((), ()))
TN = (((0,), (0,)), ((), ()))

NX, NY, NZ = 4, 4, 8
ROWS, RHS, LOC, BLK = 2048, 256, 512, 8
LEVELS = 3
LANES = 128
COLS = 16
G2, E21, G1, E20, E10, G0, WIDE = 0, 512, 1536, 2560, 4608, 6656, 8704


def weight_scale(target):
    fan_total = (256 >> target) * LOC // 2 + (LEVELS - 1 - target) * (ROWS >> target)
    return float(fan_total) ** (-0.5)


def split(value):
    high = value.astype(BF16)
    return high, (value - high.astype(F32)).astype(BF16)


def small_dot(left, right, dims):
    left_high, left_low = split(left)
    right_high, right_low = split(right)
    rows = left.shape[0]
    both = jnp.concatenate([left_high, left_low], axis=0)
    first = lax.dot_general(both, right_high, dims, preferred_element_type=F32)
    second = lax.dot_general(left_high, right_low, dims, preferred_element_type=F32)
    return first[:rows] + first[rows:] + second


def place():
    leaf, panel = lax.axis_index("leaf"), lax.axis_index("panel")
    return panel // 2, leaf // NZ, leaf % NZ, panel % 2


def device(x, y, z, c):
    return (y * NZ + z, x * 2 + c)


def hops(step, size):
    return min(step, size - step)


X_PEERS = (2, 1, 3)
Y_PEERS = (2, 1, 3)
Z_PEERS = (4, 3, 5, 2, 6, 1, 7)
PLANE = sorted(
    [(a, b) for a in range(NX) for b in range(NY)][1:], key=lambda ab: -hops(ab[0], NX) - hops(ab[1], NY)
)
HALF = sorted([(a, b) for a in range(NX) for b in range(2)][1:], key=lambda ab: -hops(ab[0], NX) - ab[1])
ROUNDS = ((0, 1536), (1536, 4608), (4608, 8704))


def split3(value):
    high = value.astype(BF16)
    rest = value - high.astype(F32)
    middle = rest.astype(BF16)
    return high, middle, (rest - middle.astype(F32)).astype(BF16)


def exact_dot(left, right):
    return jnp.dot(left, right, precision=lax.Precision.HIGHEST, preferred_element_type=F32)


def iota(shape, dim):
    return lax.broadcasted_iota(jnp.int32, shape, dim)


def reorder(rows):
    return (rows >> 9 << 9) + ((rows >> 4 & 3) << 7) + ((rows >> 6 & 7) << 4) + (rows & 15)


def sub_start(level):
    return sum(ROWS >> k + 1 for k in range(level))


def row_start(level):
    return sum(ROWS >> k for k in range(level))


def invert(factor, scale, inverse):
    lane = iota((32, LANES), 1)
    row, col = iota((LANES, LANES), 0), iota((LANES, LANES), 1)
    blocks, packed = [], []
    for g in range(4):
        at = slice(g * LANES, (g + 1) * LANES)
        block = jnp.where(row > col, factor[at, at] * scale[:, at], 0.0)
        blocks.append(block)
        parts = [jnp.where(lane >> 5 == q, block[32 * q : 32 * q + 32], 0.0) for q in range(4)]
        packed.append(parts[0] + parts[1] + parts[2] + parts[3])
    unit = (iota((32, LANES), 0) == (lane & 31)).astype(F32)
    found = [unit] * 4
    for k in range(31):
        index = (lane & 96) + k
        for g in range(4):
            coefficient = jnp.take_along_axis(packed[g], index, axis=1, mode="promise_in_bounds")
            found[g] = found[g] - coefficient * found[g][k : k + 1, :]
    whole = []
    for g in range(4):
        total = jnp.concatenate([jnp.where(lane >> 5 == q, found[g], 0.0) for q in range(4)], axis=0)
        whole.append(total)
    for bit in (5, 6):
        below = (row >> bit + 1 == col >> bit + 1) & (row >> bit > col >> bit)
        inner = [exact_dot(jnp.where(below, blocks[g], 0.0), whole[g]) for g in range(4)]
        whole = [whole[g] - exact_dot(whole[g], inner[g]) for g in range(4)]
    inverse[...] = jnp.zeros_like(inverse)
    for h in range(2):
        first = slice(h * 256, h * 256 + 128)
        second = slice(h * 256 + 128, h * 256 + 256)
        inner = exact_dot(factor[second, first] * scale[:, first], whole[2 * h])
        inverse[first, first] = whole[2 * h]
        inverse[second, second] = whole[2 * h + 1]
        inverse[second, first] = -exact_dot(whole[2 * h + 1], inner)
    inner = exact_dot(factor[256:, :256] * scale[:, :256], inverse[:256, :256])
    inverse[256:, :256] = -exact_dot(inverse[256:, 256:], inner)


def separator_rows(sep_factor, sep_diag, turned, position):
    inverses = []
    eye = iota((BLK, BLK), 0) == iota((BLK, BLK), 1)
    for level in range(LEVELS):
        node_rows = ROWS >> level
        start = row_start(level)
        strict = sep_factor[:, start : start + node_rows]
        diagonal = jnp.sum(jnp.where(eye, sep_diag[level : level + 1, :], 0.0), axis=1, keepdims=True)
        own = position % (256 >> level) * BLK + iota((BLK, node_rows), 0)
        cols = iota((BLK, node_rows), 1)
        inverses.append(jnp.where(cols < own, strict, 0.0) + jnp.where(cols == own, diagonal, 0.0))
    e10, e20, e21 = turned[:, :2048], turned[:, 2048:4096], turned[:, 4096:]
    pieces = [inverses[2], e21, inverses[1], e20, e10, inverses[0]]
    blocks = [piece[:, i : i + 512] for piece in pieces for i in range(0, piece.shape[1], 512)]
    stacked = jnp.concatenate(blocks, axis=0)
    swap = jnp.where(reorder(iota((512, 512), 0)) == iota((512, 512), 1), 1.0, 0.0).astype(BF16)
    high, middle, low = split3(stacked)
    return (
        jnp.dot(high, swap, preferred_element_type=F32)
        + jnp.dot(middle, swap, preferred_element_type=F32)
        + jnp.dot(low, swap, preferred_element_type=F32)
    )


def whole_kernel(
    diag, rows, rhs_sep, sep_factor, sep_diag, turned, factor_hbm, rhs_hbm, update_hbm,
    out_sub, out_sep,
    factor, rhs, update, inverse, solved_t, current, terms, update_high, update_low, moved_high, moved_low,
    ut0, ut1, ut2, m_ref, x0, x1, x2,
    b2c, b1c, b0c, b2x, b2s, b2z, b1x, b1s, b1y, b1t, b1z, b0y, b0x, b0p, b0q, b0u, b0v, b0t, b0z,
    g2, p1, p1r, g1, p0, p0r, g0, q0, q0r, h0, q1, q1r, h1, q2, q2r, h2,
    lsem, ssem, rsem,
):
    x, y, z, c = place()
    position = lax.axis_index("leaf") * 8 + lax.axis_index("panel")
    partner = y + 1 - 2 * (y % 2)
    yy = y % 2
    sibling = device(x, y, z, 1 - c)
    loads = [
        pltpu.make_async_copy(src, dst, lsem.at[i])
        for i, (src, dst) in enumerate(((factor_hbm, factor), (rhs_hbm, rhs), (update_hbm, update)))
    ]
    for load in loads:
        load.start()

    def xs(a):
        return (x + a) % NX

    def ys(b):
        return (y + b) % NY

    def zs(d):
        return (z + d) % NZ

    def pair_y(b):
        return partner if b else y

    barrier = pltpu.get_barrier_semaphore()
    greeted = [device(xs(a), ys(b), z, c) for a, b in PLANE]
    greeted += [device(x, y, zs(d), c) for d in range(1, NZ)] + [sibling]
    for peer in greeted:
        pl.semaphore_signal(barrier, inc=1, device_id=peer, device_id_type=MESH)

    copies = []

    def send(src, dst, peer):
        at = len(copies)
        copy = pltpu.make_async_remote_copy(
            src_ref=src, dst_ref=dst, send_sem=ssem.at[at], recv_sem=rsem.at[at],
            device_id=peer, device_id_type=MESH,
        )
        copy.start()
        copies.append(copy)
        return copy

    def arrive(batch):
        for copy in batch:
            copy.wait_recv()

    own_rows = separator_rows(sep_factor, sep_diag, turned, position)
    for i in range(WIDE // 512):
        m_ref[z, c, :, i * 512 : (i + 1) * 512] = own_rows[i * BLK : (i + 1) * BLK]

    scale = 1.0 / diag[...]
    loads[0].wait()
    invert(factor, scale, inverse)
    loads[1].wait()
    right_t = rhs[...].T
    solved_t[...] = small_dot(right_t, inverse[...], NT) * scale
    current[...] = solved_t[...]

    pl.semaphore_wait(barrier, len(greeted))

    right, left = device(x, y, zs(1), c), device(x, y, zs(NZ - 1), c)

    def pass_on(block, start, size, peer):
        ref = m_ref.at[block, c, :, pl.ds(start, size)]
        return send(ref, ref, peer)

    ring, steps, shared = [], [1] * len(ROUNDS), [None] * len(ROUNDS)
    for start, stop in ROUNDS:
        ring.append([pass_on(z, start, stop - start, right), pass_on(z, start, stop - start, left)])

    def advance(turn):
        step = steps[turn]
        steps[turn] = step + 1
        start, stop = ROUNDS[turn]
        size = stop - start
        from_left, from_right = zs(NZ - step), zs(step)
        arrive(ring[turn])
        if step < 3:
            ring[turn] = [pass_on(from_left, start, size, right), pass_on(from_right, start, size, left)]
        elif step == 3:
            ring[turn] = [
                pass_on(from_left, start, size // 2, right),
                pass_on(from_right, start + size // 2, size // 2, left),
            ]
        else:
            ref = m_ref.at[:, c, :, pl.ds(start, size)]
            shared[turn] = [send(ref, ref, sibling)]

    loads[2].wait()
    solved_high, solved_low = split(solved_t[...])
    solved_both = jnp.concatenate([solved_high, solved_low], axis=0)

    def coupling_terms(level):
        def step(i, carry):
            at = pl.ds(pl.multiple_of(sub_start(level) + i * 256, 256), 256)
            high, low = split(update[at, :])
            update_high[at, :] = high
            update_low[at, :] = low
            first = lax.dot_general(solved_both, high, NT, preferred_element_type=F32)
            second = lax.dot_general(solved_high, low, NT, preferred_element_type=F32)
            top, bottom = split(first[:RHS] + first[RHS:] + second)
            terms[:RHS, at] = top
            terms[RHS:, at] = bottom
            return carry

        lax.fori_loop(0, (ROWS >> level) // 512, step, 0)

    places = []
    for level in range(LEVELS):
        count = ROWS >> level + 1
        places.append(reorder(rows[:, sub_start(level) : sub_start(level) + count]))

    def chosen(level, i):
        count = ROWS >> level + 1
        ids = iota((256, count), 0) + i * 256
        return jnp.where(ids == places[level], 1.0, 0.0).astype(BF16)

    mark = jnp.where(iota((BLK, LANES), 1) == z * 16 + c * BLK + iota((BLK, LANES), 0), 1.0, 0.0)

    def node_terms(level, ut, first, last):
        count = ROWS >> level + 1
        listed = terms[:, sub_start(level) : sub_start(level) + count]

        def step(i, carry):
            both = lax.dot_general(listed, chosen(level, i), NT, preferred_element_type=F32)
            total = (both[:RHS] + both[RHS:]) * -weight_scale(level)
            for k in range(2):
                part = total[:, k * LANES : (k + 1) * LANES]
                if level == 0:
                    ut[i // 2, i % 2 * 2 + k] = part
                elif level == 1:
                    ut[(i % 2 * 2 + k) * 2 + i // 2] = part
                else:
                    ut[2 * i + k] = part
            return carry

        lax.fori_loop(first, last, step, 0)

    def own_term(level):
        return lax.dot_general(
            rhs_sep[level], mark, TN, precision=lax.Precision.HIGHEST, preferred_element_type=F32
        )

    mine = pl.ds(pl.multiple_of(c * LANES, LANES), LANES)
    other = pl.ds(pl.multiple_of((1 - c) * LANES, LANES), LANES)
    cols = pl.ds(pl.multiple_of(z * COLS, COLS), COLS)
    spread = pl.ds(pl.multiple_of(c * LANES + z * COLS, COLS), COLS)

    def add_own(total, own):
        def step(i, carry):
            total[i] = total[i] + own[i, mine, :]
            return carry

        lax.fori_loop(0, total.shape[0], step, 0)

    def z_stage(summed, parts):
        return [
            send(summed.at[pl.ds(pl.multiple_of(zs(d) * COLS, COLS), COLS), :], parts.at[d - 1], device(x, y, zs(d), c))
            for d in Z_PEERS
        ]

    def z_sum(summed, parts, batch):
        arrive(batch)
        total = summed[cols, :]
        for d in range(NZ - 1):
            total = total + parts[d]
        return total

    pieces = [(2, i) for i in range(2)] + [(1, i) for i in range(4)] + [(0, i) for i in range(8)]

    def work(amount):
        for _ in range(amount):
            if pieces:
                level, i = pieces.pop()
                count = ROWS >> level + 1
                listed = slice(sub_start(level), sub_start(level) + count)
                at = slice(row_start(level) + i * 256, row_start(level) + i * 256 + 256)
                pick = chosen(level, i)
                moved_high[at, :] = jnp.dot(pick, update_high[listed, :], preferred_element_type=F32).astype(BF16)
                moved_low[at, :] = jnp.dot(pick, update_low[listed, :], preferred_element_type=F32).astype(BF16)

    def x_send(piece, landed):
        return [send(piece(xs(a)), landed.at[a - 1], device(xs(a), y, z, c)) for a in X_PEERS]

    def y_send(piece, landed):
        return [send(piece(ys(b)), landed.at[b - 1], device(x, ys(b), z, c)) for b in Y_PEERS]

    coupling_terms(2)
    node_terms(2, ut2, 0, 2)
    ut2[x] = ut2[x] + own_term(2)
    c2 = send(ut2.at[:, other, :], b2c, sibling)
    coupling_terms(1)
    node_terms(1, ut1, 0, 4)
    ut1[x * 2 + yy] = ut1[x * 2 + yy] + own_term(1)
    c1 = send(ut1.at[:, other, :], b1c, sibling)
    arrive([c2])
    add_own(b2c, ut2)
    x2s = x_send(lambda to: b2c.at[to], b2x)
    advance(0)
    coupling_terms(0)
    advance(1)
    arrive([c1])
    add_own(b1c, ut1)
    x1s = x_send(lambda to: b1c.at[pl.ds(to * 2, 2)], b1x)
    node_terms(0, ut0, 0, 2)
    advance(2)
    node_terms(0, ut0, 2, 4)
    lower = jnp.where(y < 2, 1.0, 0.0)
    own0 = own_term(0)
    ut0[y % 2, x] = ut0[y % 2, x] + own0 * lower
    c0a = send(ut0.at[0:2, :, other, :], b0c.at[0:2], sibling)
    advance(0)
    arrive(x2s)
    b2s[...] = b2c[x] + b2x[0] + b2x[1] + b2x[2]
    z2s = z_stage(b2s, b2z)
    node_terms(0, ut0, 4, 6)
    advance(1)
    node_terms(0, ut0, 6, 8)
    ut0[2 + y % 2, x] = ut0[2 + y % 2, x] + own0 * (1.0 - lower)
    c0b = send(ut0.at[2:4, :, other, :], b0c.at[2:4], sibling)

    def add_rows(first):
        def step(i, carry):
            for k in range(NX):
                b0c[first + i, k] = b0c[first + i, k] + ut0[first + i, k, mine, :]
            return carry

        lax.fori_loop(0, 2, step, 0)

    arrive([c0a])
    add_rows(0)
    arrive([c0b])
    add_rows(2)
    mid = LANES // 2
    y0s = y_send(lambda to: b0c.at[to, :, 0:mid, :], b0y)
    x0s = x_send(lambda to: b0c.at[:, to, mid:LANES, :], b0x)
    advance(2)
    advance(0)
    r2 = z_sum(b2s, b2z, z2s)
    g2[x] = r2
    a2 = [send(g2.at[x], g2.at[x], device(xs(a), y, z, c)) for a in X_PEERS]
    advance(1)
    arrive(x1s)
    for i in range(2):
        b1s[i] = b1c[x * 2 + i] + b1x[0, i] + b1x[1, i] + b1x[2, i]
    y1s = send(b1s.at[1 - yy], b1y, device(x, partner, z, c))
    work(1)
    arrive([y1s])
    b1t[...] = b1s[yy] + b1y[...]
    z1s = z_stage(b1t, b1z)
    advance(0)

    def joined(ref):
        return jnp.concatenate([ref[i] for i in range(ref.shape[0])], axis=1)

    def spill(value, ref):
        for i in range(ref.shape[0]):
            ref[i] = value[:, i * LANES : (i + 1) * LANES]

    def columns(start, size):
        return m_ref[:, :, :, start : start + size].reshape(LANES, size)

    here1 = yy * NX + x
    here0 = y * NX + x

    def scatter_half(part, landed):
        return [
            send(part.at[(yy if b == 0 else 1 - yy) * NX + xs(a)], landed.at[k], device(xs(a), pair_y(b), z, c))
            for k, (a, b) in enumerate(HALF)
        ]

    def gather_half(whole):
        return [send(whole.at[here1], whole.at[here1], device(xs(a), pair_y(b), z, c)) for a, b in HALF]

    def scatter_plane(part, landed):
        return [
            send(part.at[ys(b) * NX + xs(a)], landed.at[k], device(xs(a), ys(b), z, c))
            for k, (a, b) in enumerate(PLANE)
        ]

    def gather_plane(whole):
        return [send(whole.at[here0], whole.at[here0], device(xs(a), ys(b), z, c)) for a, b in PLANE]

    def summed(part, here, landed, batch):
        arrive(batch)
        total = part[here]
        for k in range(landed.shape[0]):
            total = total + landed[k]
        return total

    s0_scale, s1_scale = weight_scale(0), weight_scale(1)

    arrive(a2)
    advance(2)
    arrive(shared[0])
    solved2 = small_dot(joined(g2), columns(G2, 512), NT)
    spill(small_dot(solved2, columns(E21, 1024), NN), p1)
    p1s = scatter_half(p1, p1r)
    advance(1)
    work(1)
    arrive(y0s)
    for i in range(NX):
        b0p[i] = b0c[y, i, 0:mid, :] + b0y[0, i] + b0y[1, i] + b0y[2, i]
    x0t = x_send(lambda to: b0p.at[to], b0u)
    arrive(x0s)
    for i in range(NY):
        b0q[i] = b0c[i, x, mid:LANES, :] + b0x[0, i] + b0x[1, i] + b0x[2, i]
    y0t = y_send(lambda to: b0q.at[to], b0v)
    r1 = z_sum(b1t, b1z, z1s)
    g1[here1] = r1 - s1_scale * summed(p1, here1, p1r, p1s)
    a1 = gather_half(g1)
    arrive(shared[1])
    up0 = small_dot(solved2, columns(E20, 2048), NN)
    advance(2)
    arrive(x0t)
    b0t[0:mid, :] = b0p[x] + b0u[0] + b0u[1] + b0u[2]
    arrive(y0t)
    b0t[mid:LANES, :] = b0q[y] + b0v[0] + b0v[1] + b0v[2]
    z0s = z_stage(b0t, b0z)
    arrive(a1)
    solved1 = small_dot(joined(g1), columns(G1, 1024), NT)
    arrive(shared[2])
    spill(up0 + small_dot(solved1, columns(E10, 2048), NN), p0)
    p0s = scatter_plane(p0, p0r)
    work(2)
    r0 = z_sum(b0t, b0z, z0s)
    g0[here0] = r0 - s0_scale * summed(p0, here0, p0r, p0s)
    a0 = gather_plane(g0)
    work(2)
    arrive(a0)
    solved0 = small_dot(joined(g0), columns(G0, 2048), NT)

    def block_of(d):
        return pl.ds(pl.multiple_of(c * LANES + zs(d) * COLS, COLS), COLS)

    def along_z(chunk, at, result):
        result[at, spread, :] = chunk[at]
        return [send(chunk.at[at], result.at[at, spread, :], device(x, y, zs(d), c)) for d in Z_PEERS]

    spill(small_dot(solved0, columns(G0, 2048), NN), q0)
    q0s = scatter_plane(q0, q0r)
    work(2)
    h0[here0] = summed(q0, here0, q0r, q0s)
    a0 = gather_plane(h0)
    work(2)
    arrive(a0)
    x0[:, spread, :] = h0[...]
    far0, near0 = [
        [send(h0, x0.at[:, spread, :], device(x, y, zs(d), c)) for d in ds] for ds in ((2, 6), (1, 7))
    ]
    found0 = joined(h0)
    y1 = solved1 - s0_scale * small_dot(found0, columns(E10, 2048), NT)
    spill(small_dot(y1, columns(G1, 1024), NN), q1)
    q1s = scatter_half(q1, q1r)
    y2 = solved2 - s0_scale * small_dot(found0, columns(E20, 2048), NT)
    work(1)
    h1[here1] = summed(q1, here1, q1r, q1s)
    a1 = gather_half(h1)
    z1h = along_z(h1, here1, x1)
    work(2)
    arrive(a1)
    y2 = y2 - s1_scale * small_dot(joined(h1), columns(E21, 1024), NT)
    spill(small_dot(y2, columns(G2, 512), NN), q2)
    q2s = x_send(lambda to: q2.at[to], q2r)
    arrive(far0)
    low, high = block_of(6), block_of(2)
    far0 = [
        send(x0.at[:, low, :], x0.at[:, low, :], device(x, y, zs(1), c)),
        send(x0.at[:, high, :], x0.at[:, high, :], device(x, y, zs(7), c)),
        send(x0.at[0:8, low, :], x0.at[0:8, low, :], device(x, y, zs(2), c)),
        send(x0.at[8:16, high, :], x0.at[8:16, high, :], device(x, y, zs(6), c)),
    ]
    h2[x] = summed(q2, x, q2r, q2s)
    z2h = along_z(h2, x, x2)
    arrive(z1h)
    w1 = [send(x1.at[here1, mine, :], x1.at[here1, mine, :], device(xs(a), pair_y(b), z, c)) for a, b in HALF]
    work(99)
    arrive(near0)
    arrive(z2h)
    w2 = [send(x2.at[x, mine, :], x2.at[x, mine, :], device(xs(a), y, z, c)) for a in X_PEERS]

    def swap_cores(result, batch):
        arrive(batch)
        return send(result.at[:, mine, :], result.at[:, mine, :], sibling)

    def take_in(level, result, copy):
        arrive([copy])

        def step(i, carry):
            at = pl.ds(pl.multiple_of(row_start(level) + i * 256, 256), 256)
            both = jnp.concatenate([result[2 * i], result[2 * i + 1]], axis=1)
            high, low = split(both)
            stacked = jnp.concatenate([high, low], axis=0)
            first = jnp.dot(stacked, moved_high[at, :], preferred_element_type=F32)
            second = jnp.dot(high, moved_low[at, :], preferred_element_type=F32)
            current[...] = current[...] - weight_scale(level) * (first[:RHS] + first[RHS:] + second)
            return carry

        lax.fori_loop(0, (ROWS >> level) // 256, step, 0)
        chunk = [here0, here1, x][level]
        out_sep[level] = lax.dot_general(
            mark, result[chunk], NT, precision=lax.Precision.HIGHEST, preferred_element_type=F32
        )

    w0 = swap_cores(x0, far0)
    take_in(0, x0, w0)
    w1 = swap_cores(x1, w1)
    w2 = swap_cores(x2, w2)
    take_in(1, x1, w1)
    take_in(2, x2, w2)
    out_sub[...] = small_dot(current[...] * scale, inverse[...], NN).T
    for copy in copies:
        copy.wait_send()


N_COPIES = 256


def whole(*operands):
    def piece(*lead, rows=COLS):
        return pltpu.VMEM((*lead, rows, LANES), F32)

    scratch = [
        pltpu.VMEM((LOC, LOC), F32), pltpu.VMEM((LOC, RHS), F32), pltpu.VMEM((1792, LOC), F32),
        pltpu.VMEM((LOC, LOC), F32), pltpu.VMEM((RHS, LOC), F32), pltpu.VMEM((RHS, LOC), F32),
        pltpu.VMEM((2 * RHS, 1792), BF16), pltpu.VMEM((1792, LOC), BF16), pltpu.VMEM((1792, LOC), BF16),
        pltpu.VMEM((3584, LOC), BF16), pltpu.VMEM((3584, LOC), BF16),
        piece(4, 4, rows=RHS), piece(8, rows=RHS), piece(4, rows=RHS),
        pltpu.VMEM((NZ, 2, BLK, WIDE), F32),
        piece(16, rows=RHS), piece(8, rows=RHS), piece(4, rows=RHS),
        piece(4, rows=LANES), piece(8, rows=LANES), piece(4, 4, rows=LANES),
        piece(3, rows=LANES), piece(rows=LANES), piece(7),
        piece(3, 2, rows=LANES), piece(2, rows=LANES), piece(rows=LANES), piece(rows=LANES), piece(7),
        piece(3, 4, rows=64), piece(3, 4, rows=64), piece(4, rows=64), piece(4, rows=64),
        piece(3, rows=64), piece(3, rows=64), piece(rows=LANES), piece(7),
        piece(4), piece(8), piece(7), piece(8), piece(16), piece(15), piece(16),
        piece(16), piece(15), piece(16), piece(8), piece(7), piece(8), piece(4), piece(3), piece(4),
        pltpu.SemaphoreType.DMA((3,)), pltpu.SemaphoreType.DMA((N_COPIES,)), pltpu.SemaphoreType.DMA((N_COPIES,)),
    ]
    vmem = pl.BlockSpec(memory_space=pltpu.VMEM)
    hbm = pl.BlockSpec(memory_space=pl.ANY)
    return pl.pallas_call(
        whole_kernel,
        out_shape=[jax.ShapeDtypeStruct((LOC, RHS), F32), jax.ShapeDtypeStruct((LEVELS, BLK, RHS), F32)],
        in_specs=[vmem] * 6 + [hbm] * 3,
        out_specs=[vmem] * 2,
        scratch_shapes=scratch,
        compiler_params=pltpu.CompilerParams(
            collective_id=0, has_side_effects=True, vmem_limit_bytes=58 * 1024 * 1024
        ),
    )(*operands)


def body(rhs_sub, rhs_sep, sub_factor, sub_diag, sep_factor, sep_diag, sub_update, update_rows, sep_update):
    result_sub, result_sep = whole(
        sub_diag, update_rows, rhs_sep, sep_factor, sep_diag, sep_update[0].T, sub_factor[0], rhs_sub[0], sub_update[0]
    )
    return result_sub[None], result_sep


def solution(mesh):
    both = ("leaf", "panel")
    in_specs = (
        P(both, None, None), P(None, both, None), P(both, None, None), P(both, None), P(both, None),
        P(None, both), P(both, None, None), P(both, None), P(both, None, None),
    )
    out_specs = (P(both, None, None), P(None, both, None))
    return jax.shard_map(body, mesh=mesh, in_specs=in_specs, out_specs=out_specs, check_vma=False)
```

```python
import jax
import jax.numpy as jnp
from jax import lax
from jax.experimental import pallas as pl
from jax.experimental.pallas import tpu as pltpu
from jax.sharding import PartitionSpec as P

MESH = pl.DeviceIdType.MESH
F32 = jnp.float32
BF16 = jnp.bfloat16
NN = (((1,), (0,)), ((), ()))
NT = (((1,), (1,)), ((), ()))
TN = (((0,), (0,)), ((), ()))

NX, NY, NZ = 4, 4, 8
ROWS, RHS, LOC, BLK = 2048, 256, 512, 8
LEVELS = 3
LANES = 128
COLS = 16
G2, E21, G1, E20, E10, G0, WIDE = 0, 512, 1536, 2560, 4608, 6656, 8704


def weight_scale(target):
    fan_total = (256 >> target) * LOC // 2 + (LEVELS - 1 - target) * (ROWS >> target)
    return float(fan_total) ** (-0.5)


def split(value):
    high = value.astype(BF16)
    return high, (value - high.astype(F32)).astype(BF16)


def small_dot(left, right, dims):
    left_high, left_low = split(left)
    right_high, right_low = split(right)
    rows = left.shape[0]
    both = jnp.concatenate([left_high, left_low], axis=0)
    first = lax.dot_general(both, right_high, dims, preferred_element_type=F32)
    second = lax.dot_general(left_high, right_low, dims, preferred_element_type=F32)
    return first[:rows] + first[rows:] + second


def place():
    leaf, panel = lax.axis_index("leaf"), lax.axis_index("panel")
    return panel // 2, leaf // NZ, leaf % NZ, panel % 2


def device(x, y, z, c):
    return (y * NZ + z, x * 2 + c)


def hops(step, size):
    return min(step, size - step)


X_PEERS = (2, 1, 3)
Y_PEERS = (2, 1, 3)
Z_PEERS = (4, 3, 5, 2, 6, 1, 7)
PLANE = sorted(
    [(a, b) for a in range(NX) for b in range(NY)][1:], key=lambda ab: -hops(ab[0], NX) - hops(ab[1], NY)
)
HALF = sorted([(a, b) for a in range(NX) for b in range(2)][1:], key=lambda ab: -hops(ab[0], NX) - ab[1])
ROUNDS = ((0, 1536), (1536, 4608), (4608, 8704))


def split3(value):
    high = value.astype(BF16)
    rest = value - high.astype(F32)
    middle = rest.astype(BF16)
    return high, middle, (rest - middle.astype(F32)).astype(BF16)


def exact_dot(left, right):
    return jnp.dot(left, right, precision=lax.Precision.HIGHEST, preferred_element_type=F32)


def iota(shape, dim):
    return lax.broadcasted_iota(jnp.int32, shape, dim)


def reorder(rows):
    return (rows >> 9 << 9) + ((rows >> 4 & 3) << 7) + ((rows >> 6 & 7) << 4) + (rows & 15)


def sub_start(level):
    return sum(ROWS >> k + 1 for k in range(level))


def row_start(level):
    return sum(ROWS >> k for k in range(level))


def invert(factor, scale, inverse):
    lane = iota((32, LANES), 1)
    row, col = iota((LANES, LANES), 0), iota((LANES, LANES), 1)
    blocks, packed = [], []
    for g in range(4):
        at = slice(g * LANES, (g + 1) * LANES)
        block = jnp.where(row > col, factor[at, at] * scale[:, at], 0.0)
        blocks.append(block)
        parts = [jnp.where(lane >> 5 == q, block[32 * q : 32 * q + 32], 0.0) for q in range(4)]
        packed.append(parts[0] + parts[1] + parts[2] + parts[3])
    unit = (iota((32, LANES), 0) == (lane & 31)).astype(F32)
    found = [unit] * 4
    for k in range(31):
        index = (lane & 96) + k
        for g in range(4):
            coefficient = jnp.take_along_axis(packed[g], index, axis=1, mode="promise_in_bounds")
            found[g] = found[g] - coefficient * found[g][k : k + 1, :]
    whole = []
    for g in range(4):
        total = jnp.concatenate([jnp.where(lane >> 5 == q, found[g], 0.0) for q in range(4)], axis=0)
        whole.append(total)
    for bit in (5, 6):
        below = (row >> bit + 1 == col >> bit + 1) & (row >> bit > col >> bit)
        inner = [exact_dot(jnp.where(below, blocks[g], 0.0), whole[g]) for g in range(4)]
        whole = [whole[g] - exact_dot(whole[g], inner[g]) for g in range(4)]
    inverse[...] = jnp.zeros_like(inverse)
    for h in range(2):
        first = slice(h * 256, h * 256 + 128)
        second = slice(h * 256 + 128, h * 256 + 256)
        inner = exact_dot(factor[second, first] * scale[:, first], whole[2 * h])
        inverse[first, first] = whole[2 * h]
        inverse[second, second] = whole[2 * h + 1]
        inverse[second, first] = -exact_dot(whole[2 * h + 1], inner)
    inner = exact_dot(factor[256:, :256] * scale[:, :256], inverse[:256, :256])
    inverse[256:, :256] = -exact_dot(inverse[256:, 256:], inner)


def separator_rows(sep_factor, sep_diag, turned, position):
    inverses = []
    eye = iota((BLK, BLK), 0) == iota((BLK, BLK), 1)
    for level in range(LEVELS):
        node_rows = ROWS >> level
        start = row_start(level)
        strict = sep_factor[:, start : start + node_rows]
        diagonal = jnp.sum(jnp.where(eye, sep_diag[level : level + 1, :], 0.0), axis=1, keepdims=True)
        own = position % (256 >> level) * BLK + iota((BLK, node_rows), 0)
        cols = iota((BLK, node_rows), 1)
        inverses.append(jnp.where(cols < own, strict, 0.0) + jnp.where(cols == own, diagonal, 0.0))
    e10, e20, e21 = turned[:, :2048], turned[:, 2048:4096], turned[:, 4096:]
    pieces = [inverses[2], e21, inverses[1], e20, e10, inverses[0]]
    blocks = [piece[:, i : i + 512] for piece in pieces for i in range(0, piece.shape[1], 512)]
    stacked = jnp.concatenate(blocks, axis=0)
    swap = jnp.where(reorder(iota((512, 512), 0)) == iota((512, 512), 1), 1.0, 0.0).astype(BF16)
    high, middle, low = split3(stacked)
    return (
        jnp.dot(high, swap, preferred_element_type=F32)
        + jnp.dot(middle, swap, preferred_element_type=F32)
        + jnp.dot(low, swap, preferred_element_type=F32)
    )


def whole_kernel(
    diag, rows, rhs_sep, sep_factor, sep_diag, turned, factor_hbm, rhs_hbm, update_hbm,
    out_sub, out_sep,
    factor, rhs, update, inverse, solved_t, current, terms, update_high, update_low, moved_high, moved_low,
    ut0, ut1, ut2, m_ref, x0, x1, x2,
    b2c, b1c, b0c, b2x, b2s, b2z, b1x, b1y, b1p, b1q, b1u, b1v, b1t, b1z, b0y, b0x, b0p, b0q, b0u, b0v, b0t, b0z,
    g2, p1, p1r, g1, p0, p0r, g0, q0, q0r, h0, q1, q1r, h1, q2, q2r, h2,
    lsem, ssem, rsem,
):
    x, y, z, c = place()
    position = lax.axis_index("leaf") * 8 + lax.axis_index("panel")
    partner = y + 1 - 2 * (y % 2)
    yy = y % 2
    sibling = device(x, y, z, 1 - c)
    loads = [
        pltpu.make_async_copy(src, dst, lsem.at[i])
        for i, (src, dst) in enumerate(((factor_hbm, factor), (rhs_hbm, rhs), (update_hbm, update)))
    ]
    for load in loads:
        load.start()

    def xs(a):
        return (x + a) % NX

    def ys(b):
        return (y + b) % NY

    def zs(d):
        return (z + d) % NZ

    def pair_y(b):
        return partner if b else y

    barrier = pltpu.get_barrier_semaphore()
    greeted = [device(xs(a), ys(b), z, c) for a, b in PLANE]
    greeted += [device(x, y, zs(d), c) for d in range(1, NZ)] + [sibling]
    for peer in greeted:
        pl.semaphore_signal(barrier, inc=1, device_id=peer, device_id_type=MESH)

    copies = []

    def send(src, dst, peer):
        at = len(copies)
        copy = pltpu.make_async_remote_copy(
            src_ref=src, dst_ref=dst, send_sem=ssem.at[at], recv_sem=rsem.at[at],
            device_id=peer, device_id_type=MESH,
        )
        copy.start()
        copies.append(copy)
        return copy

    def arrive(batch):
        for copy in batch:
            copy.wait_recv()

    own_rows = separator_rows(sep_factor, sep_diag, turned, position)
    for i in range(WIDE // 512):
        m_ref[z, c, :, i * 512 : (i + 1) * 512] = own_rows[i * BLK : (i + 1) * BLK]

    scale = 1.0 / diag[...]
    loads[0].wait()
    invert(factor, scale, inverse)
    loads[1].wait()
    right_t = rhs[...].T
    solved_t[...] = small_dot(right_t, inverse[...], NT) * scale
    current[...] = solved_t[...]

    pl.semaphore_wait(barrier, len(greeted))

    right, left = device(x, y, zs(1), c), device(x, y, zs(NZ - 1), c)

    def pass_on(block, start, size, peer):
        ref = m_ref.at[block, c, :, pl.ds(start, size)]
        return send(ref, ref, peer)

    ring, steps, shared = [], [1] * len(ROUNDS), [None] * len(ROUNDS)
    for start, stop in ROUNDS:
        ring.append([pass_on(z, start, stop - start, right), pass_on(z, start, stop - start, left)])

    def advance(turn):
        step = steps[turn]
        steps[turn] = step + 1
        start, stop = ROUNDS[turn]
        size = stop - start
        from_left, from_right = zs(NZ - step), zs(step)
        arrive(ring[turn])
        if step < 3:
            ring[turn] = [pass_on(from_left, start, size, right), pass_on(from_right, start, size, left)]
        elif step == 3:
            ring[turn] = [
                pass_on(from_left, start, size // 2, right),
                pass_on(from_right, start + size // 2, size // 2, left),
            ]
        else:
            ref = m_ref.at[:, c, :, pl.ds(start, size)]
            shared[turn] = [send(ref, ref, sibling)]

    loads[2].wait()
    solved_high, solved_low = split(solved_t[...])
    solved_both = jnp.concatenate([solved_high, solved_low], axis=0)

    def coupling_terms(level):
        def step(i, carry):
            at = pl.ds(pl.multiple_of(sub_start(level) + i * 256, 256), 256)
            high, low = split(update[at, :])
            update_high[at, :] = high
            update_low[at, :] = low
            first = lax.dot_general(solved_both, high, NT, preferred_element_type=F32)
            second = lax.dot_general(solved_high, low, NT, preferred_element_type=F32)
            top, bottom = split(first[:RHS] + first[RHS:] + second)
            terms[:RHS, at] = top
            terms[RHS:, at] = bottom
            return carry

        lax.fori_loop(0, (ROWS >> level) // 512, step, 0)

    places = []
    for level in range(LEVELS):
        count = ROWS >> level + 1
        places.append(reorder(rows[:, sub_start(level) : sub_start(level) + count]))

    def chosen(level, i):
        count = ROWS >> level + 1
        ids = iota((256, count), 0) + i * 256
        return jnp.where(ids == places[level], 1.0, 0.0).astype(BF16)

    mark = jnp.where(iota((BLK, LANES), 1) == z * 16 + c * BLK + iota((BLK, LANES), 0), 1.0, 0.0)

    def node_terms(level, ut, first, last):
        count = ROWS >> level + 1
        listed = terms[:, sub_start(level) : sub_start(level) + count]

        def step(i, carry):
            both = lax.dot_general(listed, chosen(level, i), NT, preferred_element_type=F32)
            total = (both[:RHS] + both[RHS:]) * -weight_scale(level)
            for k in range(2):
                part = total[:, k * LANES : (k + 1) * LANES]
                if level == 0:
                    ut[i // 2, i % 2 * 2 + k] = part
                elif level == 1:
                    ut[i % 2 * 2 + k, i // 2] = part
                else:
                    ut[2 * i + k] = part
            return carry

        lax.fori_loop(first, last, step, 0)

    def own_term(level):
        return lax.dot_general(
            rhs_sep[level], mark, TN, precision=lax.Precision.HIGHEST, preferred_element_type=F32
        )

    mine = pl.ds(pl.multiple_of(c * LANES, LANES), LANES)
    other = pl.ds(pl.multiple_of((1 - c) * LANES, LANES), LANES)
    cols = pl.ds(pl.multiple_of(z * COLS, COLS), COLS)
    spread = pl.ds(pl.multiple_of(c * LANES + z * COLS, COLS), COLS)

    def add_own(total, own):
        def step(i, carry):
            total[i] = total[i] + own[i, mine, :]
            return carry

        lax.fori_loop(0, total.shape[0], step, 0)

    def z_stage(summed, parts):
        return [
            send(summed.at[pl.ds(pl.multiple_of(zs(d) * COLS, COLS), COLS), :], parts.at[d - 1], device(x, y, zs(d), c))
            for d in Z_PEERS
        ]

    def z_sum(summed, parts, batch):
        arrive(batch)
        total = summed[cols, :]
        for d in range(NZ - 1):
            total = total + parts[d]
        return total

    pieces = [(2, i) for i in range(2)] + [(1, i) for i in range(4)] + [(0, i) for i in range(8)]

    def work(amount):
        for _ in range(amount):
            if pieces:
                level, i = pieces.pop()
                count = ROWS >> level + 1
                listed = slice(sub_start(level), sub_start(level) + count)
                at = slice(row_start(level) + i * 256, row_start(level) + i * 256 + 256)
                pick = chosen(level, i)
                moved_high[at, :] = jnp.dot(pick, update_high[listed, :], preferred_element_type=F32).astype(BF16)
                moved_low[at, :] = jnp.dot(pick, update_low[listed, :], preferred_element_type=F32).astype(BF16)

    def x_send(piece, landed):
        return [send(piece(xs(a)), landed.at[a - 1], device(xs(a), y, z, c)) for a in X_PEERS]

    def y_send(piece, landed):
        return [send(piece(ys(b)), landed.at[b - 1], device(x, ys(b), z, c)) for b in Y_PEERS]

    coupling_terms(2)
    node_terms(2, ut2, 0, 2)
    ut2[x] = ut2[x] + own_term(2)
    c2 = send(ut2.at[:, other, :], b2c, sibling)
    coupling_terms(1)
    arrive([c2])
    add_own(b2c, ut2)
    x2s = x_send(lambda to: b2c.at[to], b2x)
    node_terms(1, ut1, 0, 4)
    ut1[x, yy] = ut1[x, yy] + own_term(1)
    c1 = send(ut1.at[:, :, other, :], b1c, sibling)
    advance(0)
    coupling_terms(0)
    mid = LANES // 2
    arrive([c1])

    def add_pair(i, carry):
        for k in range(2):
            b1c[i, k] = b1c[i, k] + ut1[i, k, mine, :]
        return carry

    lax.fori_loop(0, NX, add_pair, 0)
    x1s = x_send(lambda to: b1c.at[to, :, 0:mid, :], b1x)
    y1s = send(b1c.at[:, 1 - yy, mid:LANES, :], b1y, device(x, partner, z, c))
    advance(1)
    node_terms(0, ut0, 0, 2)
    node_terms(0, ut0, 2, 4)
    lower = jnp.where(y < 2, 1.0, 0.0)
    own0 = own_term(0)
    ut0[y % 2, x] = ut0[y % 2, x] + own0 * lower
    c0a = send(ut0.at[0:2, :, other, :], b0c.at[0:2], sibling)
    arrive(x2s)
    b2s[...] = b2c[x] + b2x[0] + b2x[1] + b2x[2]
    z2s = z_stage(b2s, b2z)
    advance(2)
    advance(0)
    node_terms(0, ut0, 4, 6)
    node_terms(0, ut0, 6, 8)
    ut0[2 + y % 2, x] = ut0[2 + y % 2, x] + own0 * (1.0 - lower)
    c0b = send(ut0.at[2:4, :, other, :], b0c.at[2:4], sibling)
    advance(1)

    def add_rows(first):
        def step(i, carry):
            for k in range(NX):
                b0c[first + i, k] = b0c[first + i, k] + ut0[first + i, k, mine, :]
            return carry

        lax.fori_loop(0, 2, step, 0)

    arrive([c0a])
    add_rows(0)
    arrive([c0b])
    add_rows(2)
    y0s = y_send(lambda to: b0c.at[to, :, 0:mid, :], b0y)
    x0s = x_send(lambda to: b0c.at[:, to, mid:LANES, :], b0x)
    advance(2)
    advance(0)
    r2 = z_sum(b2s, b2z, z2s)
    g2[x] = r2
    a2 = [send(g2.at[x], g2.at[x], device(xs(a), y, z, c)) for a in X_PEERS]
    arrive(x1s)
    for i in range(2):
        b1p[i] = b1c[x, i, 0:mid, :] + b1x[0, i] + b1x[1, i] + b1x[2, i]
    y1t = send(b1p.at[1 - yy], b1v, device(x, partner, z, c))
    arrive([y1s])
    for i in range(NX):
        b1q[i] = b1c[i, yy, mid:LANES, :] + b1y[i]
    x1t = x_send(lambda to: b1q.at[to], b1u)
    advance(1)
    work(1)
    arrive([y1t])
    b1t[0:mid, :] = b1p[yy] + b1v[...]
    arrive(x1t)
    b1t[mid:LANES, :] = b1q[x] + b1u[0] + b1u[1] + b1u[2]
    z1s = z_stage(b1t, b1z)
    advance(0)

    def joined(ref):
        return jnp.concatenate([ref[i] for i in range(ref.shape[0])], axis=1)

    def spill(value, ref):
        for i in range(ref.shape[0]):
            ref[i] = value[:, i * LANES : (i + 1) * LANES]

    def columns(start, size):
        return m_ref[:, :, :, start : start + size].reshape(LANES, size)

    here1 = yy * NX + x
    here0 = y * NX + x

    def scatter_half(part, landed):
        return [
            send(part.at[(yy if b == 0 else 1 - yy) * NX + xs(a)], landed.at[k], device(xs(a), pair_y(b), z, c))
            for k, (a, b) in enumerate(HALF)
        ]

    def gather_half(whole):
        return [send(whole.at[here1], whole.at[here1], device(xs(a), pair_y(b), z, c)) for a, b in HALF]

    def scatter_plane(part, landed):
        return [
            send(part.at[ys(b) * NX + xs(a)], landed.at[k], device(xs(a), ys(b), z, c))
            for k, (a, b) in enumerate(PLANE)
        ]

    def gather_plane(whole):
        return [send(whole.at[here0], whole.at[here0], device(xs(a), ys(b), z, c)) for a, b in PLANE]

    def summed(part, here, landed, batch):
        arrive(batch)
        total = part[here]
        for k in range(landed.shape[0]):
            total = total + landed[k]
        return total

    s0_scale, s1_scale = weight_scale(0), weight_scale(1)

    arrive(a2)
    advance(2)
    arrive(shared[0])
    solved2 = small_dot(joined(g2), columns(G2, 512), NT)
    spill(small_dot(solved2, columns(E21, 1024), NN), p1)
    p1s = scatter_half(p1, p1r)
    advance(1)
    work(1)
    arrive(y0s)
    for i in range(NX):
        b0p[i] = b0c[y, i, 0:mid, :] + b0y[0, i] + b0y[1, i] + b0y[2, i]
    x0t = x_send(lambda to: b0p.at[to], b0u)
    arrive(x0s)
    for i in range(NY):
        b0q[i] = b0c[i, x, mid:LANES, :] + b0x[0, i] + b0x[1, i] + b0x[2, i]
    y0t = y_send(lambda to: b0q.at[to], b0v)
    r1 = z_sum(b1t, b1z, z1s)
    g1[here1] = r1 - s1_scale * summed(p1, here1, p1r, p1s)
    a1 = gather_half(g1)
    arrive(shared[1])
    up0 = small_dot(solved2, columns(E20, 2048), NN)
    advance(2)
    arrive(x0t)
    b0t[0:mid, :] = b0p[x] + b0u[0] + b0u[1] + b0u[2]
    arrive(y0t)
    b0t[mid:LANES, :] = b0q[y] + b0v[0] + b0v[1] + b0v[2]
    z0s = z_stage(b0t, b0z)
    arrive(a1)
    solved1 = small_dot(joined(g1), columns(G1, 1024), NT)
    arrive(shared[2])
    spill(up0 + small_dot(solved1, columns(E10, 2048), NN), p0)
    p0s = scatter_plane(p0, p0r)
    work(2)
    r0 = z_sum(b0t, b0z, z0s)
    g0[here0] = r0 - s0_scale * summed(p0, here0, p0r, p0s)
    a0 = gather_plane(g0)
    work(2)
    arrive(a0)
    solved0 = small_dot(joined(g0), columns(G0, 2048), NT)

    def block_of(d):
        return pl.ds(pl.multiple_of(c * LANES + zs(d) * COLS, COLS), COLS)

    def along_z(chunk, at, result):
        result[at, spread, :] = chunk[at]
        return [send(chunk.at[at], result.at[at, spread, :], device(x, y, zs(d), c)) for d in Z_PEERS]

    spill(small_dot(solved0, columns(G0, 2048), NN), q0)
    q0s = scatter_plane(q0, q0r)
    work(2)
    h0[here0] = summed(q0, here0, q0r, q0s)
    a0 = gather_plane(h0)
    work(2)
    arrive(a0)
    x0[:, spread, :] = h0[...]
    far0, near0 = [
        [send(h0, x0.at[:, spread, :], device(x, y, zs(d), c)) for d in ds] for ds in ((2, 6), (1, 7))
    ]
    found0 = joined(h0)
    y1 = solved1 - s0_scale * small_dot(found0, columns(E10, 2048), NT)
    spill(small_dot(y1, columns(G1, 1024), NN), q1)
    q1s = scatter_half(q1, q1r)
    y2 = solved2 - s0_scale * small_dot(found0, columns(E20, 2048), NT)
    work(1)
    h1[here1] = summed(q1, here1, q1r, q1s)
    a1 = gather_half(h1)
    z1h = along_z(h1, here1, x1)
    work(2)
    arrive(a1)
    y2 = y2 - s1_scale * small_dot(joined(h1), columns(E21, 1024), NT)
    spill(small_dot(y2, columns(G2, 512), NN), q2)
    q2s = x_send(lambda to: q2.at[to], q2r)
    arrive(far0)
    low, high = block_of(6), block_of(2)
    far0 = [
        send(x0.at[:, low, :], x0.at[:, low, :], device(x, y, zs(1), c)),
        send(x0.at[:, high, :], x0.at[:, high, :], device(x, y, zs(7), c)),
        send(x0.at[0:8, low, :], x0.at[0:8, low, :], device(x, y, zs(2), c)),
        send(x0.at[8:16, high, :], x0.at[8:16, high, :], device(x, y, zs(6), c)),
    ]
    h2[x] = summed(q2, x, q2r, q2s)
    z2h = along_z(h2, x, x2)
    arrive(z1h)
    w1 = [send(x1.at[here1, mine, :], x1.at[here1, mine, :], device(xs(a), pair_y(b), z, c)) for a, b in HALF]
    work(99)
    arrive(near0)
    arrive(z2h)
    w2 = [send(x2.at[x, mine, :], x2.at[x, mine, :], device(xs(a), y, z, c)) for a in X_PEERS]

    def swap_cores(result, batch):
        arrive(batch)
        return send(result.at[:, mine, :], result.at[:, mine, :], sibling)

    def take_in(level, result, copy):
        arrive([copy])

        def step(i, carry):
            at = pl.ds(pl.multiple_of(row_start(level) + i * 256, 256), 256)
            both = jnp.concatenate([result[2 * i], result[2 * i + 1]], axis=1)
            high, low = split(both)
            stacked = jnp.concatenate([high, low], axis=0)
            first = jnp.dot(stacked, moved_high[at, :], preferred_element_type=F32)
            second = jnp.dot(high, moved_low[at, :], preferred_element_type=F32)
            current[...] = current[...] - weight_scale(level) * (first[:RHS] + first[RHS:] + second)
            return carry

        lax.fori_loop(0, (ROWS >> level) // 256, step, 0)
        chunk = [here0, here1, x][level]
        out_sep[level] = lax.dot_general(
            mark, result[chunk], NT, precision=lax.Precision.HIGHEST, preferred_element_type=F32
        )

    w0 = swap_cores(x0, far0)
    take_in(0, x0, w0)
    w1 = swap_cores(x1, w1)
    w2 = swap_cores(x2, w2)
    take_in(1, x1, w1)
    take_in(2, x2, w2)
    out_sub[...] = small_dot(current[...] * scale, inverse[...], NN).T
    for copy in copies:
        copy.wait_send()


N_COPIES = 256


def whole(*operands):
    def piece(*lead, rows=COLS):
        return pltpu.VMEM((*lead, rows, LANES), F32)

    scratch = [
        pltpu.VMEM((LOC, LOC), F32), pltpu.VMEM((LOC, RHS), F32), pltpu.VMEM((1792, LOC), F32),
        pltpu.VMEM((LOC, LOC), F32), pltpu.VMEM((RHS, LOC), F32), pltpu.VMEM((RHS, LOC), F32),
        pltpu.VMEM((2 * RHS, 1792), BF16), pltpu.VMEM((1792, LOC), BF16), pltpu.VMEM((1792, LOC), BF16),
        pltpu.VMEM((3584, LOC), BF16), pltpu.VMEM((3584, LOC), BF16),
        piece(4, 4, rows=RHS), piece(4, 2, rows=RHS), piece(4, rows=RHS),
        pltpu.VMEM((NZ, 2, BLK, WIDE), F32),
        piece(16, rows=RHS), piece(8, rows=RHS), piece(4, rows=RHS),
        piece(4, rows=LANES), piece(4, 2, rows=LANES), piece(4, 4, rows=LANES),
        piece(3, rows=LANES), piece(rows=LANES), piece(7),
        piece(3, 2, rows=64), piece(4, rows=64), piece(2, rows=64), piece(4, rows=64),
        piece(3, rows=64), piece(rows=64), piece(rows=LANES), piece(7),
        piece(3, 4, rows=64), piece(3, 4, rows=64), piece(4, rows=64), piece(4, rows=64),
        piece(3, rows=64), piece(3, rows=64), piece(rows=LANES), piece(7),
        piece(4), piece(8), piece(7), piece(8), piece(16), piece(15), piece(16),
        piece(16), piece(15), piece(16), piece(8), piece(7), piece(8), piece(4), piece(3), piece(4),
        pltpu.SemaphoreType.DMA((3,)), pltpu.SemaphoreType.DMA((N_COPIES,)), pltpu.SemaphoreType.DMA((N_COPIES,)),
    ]
    vmem = pl.BlockSpec(memory_space=pltpu.VMEM)
    hbm = pl.BlockSpec(memory_space=pl.ANY)
    return pl.pallas_call(
        whole_kernel,
        out_shape=[jax.ShapeDtypeStruct((LOC, RHS), F32), jax.ShapeDtypeStruct((LEVELS, BLK, RHS), F32)],
        in_specs=[vmem] * 6 + [hbm] * 3,
        out_specs=[vmem] * 2,
        scratch_shapes=scratch,
        compiler_params=pltpu.CompilerParams(
            collective_id=0, has_side_effects=True, vmem_limit_bytes=58 * 1024 * 1024
        ),
    )(*operands)


def copy_kernel(first, second, first_out, second_out, sems):
    moves = [
        pltpu.make_async_copy(first, first_out, sems.at[0]),
        pltpu.make_async_copy(second, second_out, sems.at[1]),
    ]
    for move in moves:
        move.start()
    for move in moves:
        move.wait()


def hand_on(*results):
    hbm = pl.BlockSpec(memory_space=pl.ANY)
    return pl.pallas_call(
        copy_kernel,
        out_shape=[jax.ShapeDtypeStruct(result.shape, F32) for result in results],
        in_specs=[hbm] * 2,
        out_specs=[hbm] * 2,
        scratch_shapes=[pltpu.SemaphoreType.DMA((2,))],
        compiler_params=pltpu.CompilerParams(vmem_limit_bytes=58 * 1024 * 1024),
    )(*results)


def body(rhs_sub, rhs_sep, sub_factor, sub_diag, sep_factor, sep_diag, sub_update, update_rows, sep_update):
    result_sub, result_sep = whole(
        sub_diag, update_rows, rhs_sep, sep_factor, sep_diag, sep_update[0].T, sub_factor[0], rhs_sub[0], sub_update[0]
    )
    return hand_on(result_sub[None], result_sep)


def solution(mesh):
    both = ("leaf", "panel")
    in_specs = (
        P(both, None, None), P(None, both, None), P(both, None, None), P(both, None), P(both, None),
        P(None, both), P(both, None, None), P(both, None), P(both, None, None),
    )
    out_specs = (P(both, None, None), P(None, both, None))
    return jax.shard_map(body, mesh=mesh, in_specs=in_specs, out_specs=out_specs, check_vma=False)
```

```python
import jax
import jax.numpy as jnp
from jax import lax
from jax.experimental import pallas as pl
from jax.experimental.pallas import tpu as pltpu
from jax.sharding import PartitionSpec as P

MESH = pl.DeviceIdType.MESH
F32 = jnp.float32
BF16 = jnp.bfloat16
NN = (((1,), (0,)), ((), ()))
NT = (((1,), (1,)), ((), ()))
TN = (((0,), (0,)), ((), ()))

NX, NY, NZ = 4, 4, 8
ROWS, RHS, LOC, BLK = 2048, 256, 512, 8
LEVELS = 3
LANES = 128
COLS = 16
G2, E21, G1, E20, E10, G0, WIDE = 0, 512, 1536, 2560, 4608, 6656, 8704


def weight_scale(target):
    fan_total = (256 >> target) * LOC // 2 + (LEVELS - 1 - target) * (ROWS >> target)
    return float(fan_total) ** (-0.5)


def split(value):
    high = value.astype(BF16)
    return high, (value - high.astype(F32)).astype(BF16)


def small_dot(left, right, dims):
    left_high, left_low = split(left)
    right_high, right_low = right if isinstance(right, tuple) else split(right)
    rows = left.shape[0]
    both = jnp.concatenate([left_high, left_low], axis=0)
    first = lax.dot_general(both, right_high, dims, preferred_element_type=F32)
    second = lax.dot_general(left_high, right_low, dims, preferred_element_type=F32)
    return first[:rows] + first[rows:] + second


def place():
    leaf, panel = lax.axis_index("leaf"), lax.axis_index("panel")
    return panel // 2, leaf // NZ, leaf % NZ, panel % 2


def device(x, y, z, c):
    return (y * NZ + z, x * 2 + c)


def hops(step, size):
    return min(step, size - step)


X_PEERS = (2, 1, 3)
Y_PEERS = (2, 1, 3)
Z_PEERS = (4, 3, 5, 2, 6, 1, 7)
PLANE = sorted(
    [(a, b) for a in range(NX) for b in range(NY)][1:], key=lambda ab: -hops(ab[0], NX) - hops(ab[1], NY)
)
SIDE = sorted(
    [(a, d) for a in range(NX) for d in range(NZ)][1:], key=lambda ad: -hops(ad[0], NX) - hops(ad[1], NZ)
)
HALF = sorted([(a, b) for a in range(NX) for b in range(2)][1:], key=lambda ab: -hops(ab[0], NX) - ab[1])
ROUNDS = ((0, 1536), (1536, 4608), (4608, 8704))


def split3(value):
    high = value.astype(BF16)
    rest = value - high.astype(F32)
    middle = rest.astype(BF16)
    return high, middle, (rest - middle.astype(F32)).astype(BF16)


def exact_dot(left, right):
    return jnp.dot(left, right, precision=lax.Precision.HIGHEST, preferred_element_type=F32)


def iota(shape, dim):
    return lax.broadcasted_iota(jnp.int32, shape, dim)


def reorder(rows):
    return (rows >> 9 << 9) + ((rows >> 4 & 3) << 7) + ((rows >> 6 & 7) << 4) + (rows & 15)


def sub_start(level):
    return sum(ROWS >> k + 1 for k in range(level))


def row_start(level):
    return sum(ROWS >> k for k in range(level))


def invert(factor, scale, inverse):
    lane = iota((32, LANES), 1)
    row, col = iota((LANES, LANES), 0), iota((LANES, LANES), 1)
    blocks, packed = [], []
    for g in range(4):
        at = slice(g * LANES, (g + 1) * LANES)
        block = jnp.where(row > col, factor[at, at] * scale[:, at], 0.0)
        blocks.append(block)
        parts = [jnp.where(lane >> 5 == q, block[32 * q : 32 * q + 32], 0.0) for q in range(4)]
        packed.append(parts[0] + parts[1] + parts[2] + parts[3])
    unit = (iota((32, LANES), 0) == (lane & 31)).astype(F32)
    found = [unit] * 4
    for k in range(31):
        index = (lane & 96) + k
        for g in range(4):
            coefficient = jnp.take_along_axis(packed[g], index, axis=1, mode="promise_in_bounds")
            found[g] = found[g] - coefficient * found[g][k : k + 1, :]
    whole = []
    for g in range(4):
        total = jnp.concatenate([jnp.where(lane >> 5 == q, found[g], 0.0) for q in range(4)], axis=0)
        whole.append(total)
    for bit in (5, 6):
        below = (row >> bit + 1 == col >> bit + 1) & (row >> bit > col >> bit)
        inner = [exact_dot(jnp.where(below, blocks[g], 0.0), whole[g]) for g in range(4)]
        whole = [whole[g] - exact_dot(whole[g], inner[g]) for g in range(4)]
    inverse[...] = jnp.zeros_like(inverse)
    for h in range(2):
        first = slice(h * 256, h * 256 + 128)
        second = slice(h * 256 + 128, h * 256 + 256)
        inner = exact_dot(factor[second, first] * scale[:, first], whole[2 * h])
        inverse[first, first] = whole[2 * h]
        inverse[second, second] = whole[2 * h + 1]
        inverse[second, first] = -exact_dot(whole[2 * h + 1], inner)
    inner = exact_dot(factor[256:, :256] * scale[:, :256], inverse[:256, :256])
    inverse[256:, :256] = -exact_dot(inverse[256:, 256:], inner)


def separator_rows(sep_factor, sep_diag, turned, position):
    inverses = []
    eye = iota((BLK, BLK), 0) == iota((BLK, BLK), 1)
    for level in range(LEVELS):
        node_rows = ROWS >> level
        start = row_start(level)
        strict = sep_factor[:, start : start + node_rows]
        diagonal = jnp.sum(jnp.where(eye, sep_diag[level : level + 1, :], 0.0), axis=1, keepdims=True)
        own = position % (256 >> level) * BLK + iota((BLK, node_rows), 0)
        cols = iota((BLK, node_rows), 1)
        inverses.append(jnp.where(cols < own, strict, 0.0) + jnp.where(cols == own, diagonal, 0.0))
    e10, e20, e21 = turned[:, :2048], turned[:, 2048:4096], turned[:, 4096:]
    pieces = [inverses[2], e21, inverses[1], e20, e10, inverses[0]]
    blocks = [piece[:, i : i + 512] for piece in pieces for i in range(0, piece.shape[1], 512)]
    stacked = jnp.concatenate(blocks, axis=0)
    swap = jnp.where(reorder(iota((512, 512), 0)) == iota((512, 512), 1), 1.0, 0.0).astype(BF16)
    high, middle, low = split3(stacked)
    return (
        jnp.dot(high, swap, preferred_element_type=F32)
        + jnp.dot(middle, swap, preferred_element_type=F32)
        + jnp.dot(low, swap, preferred_element_type=F32)
    )


def whole_kernel(
    diag, rows, rhs_sep, sep_factor, sep_diag, turned, factor_hbm, rhs_hbm, update_hbm,
    out_sub, out_sep,
    factor, rhs, update, inverse, solved_t, current, terms, update_high, update_low, moved_high, moved_low,
    ut0, ut1, ut2, m_ref, m_high, m_low, x0, x1, x2,
    b2c, b1c, b0c, b2x, b2s, b2z, b1x, b1y, b1p, b1q, b1u, b1v, b1t, b1z, b0y, b0x, b0p, b0q, b0u, b0v, b0t, b0z,
    g2, p1, p1r, g1, p0, p0r, g0, q0, q0r, h0, q1, q1r, h1, q2, q2r, h2,
    lsem, ssem, rsem,
):
    x, y, z, c = place()
    position = lax.axis_index("leaf") * 8 + lax.axis_index("panel")
    partner = y + 1 - 2 * (y % 2)
    yy = y % 2
    sibling = device(x, y, z, 1 - c)
    loads = [
        pltpu.make_async_copy(src, dst, lsem.at[i])
        for i, (src, dst) in enumerate(((factor_hbm, factor), (rhs_hbm, rhs), (update_hbm, update)))
    ]
    for load in loads:
        load.start()

    def xs(a):
        return (x + a) % NX

    def ys(b):
        return (y + b) % NY

    def zs(d):
        return (z + d) % NZ

    def pair_y(b):
        return partner if b else y

    barrier = pltpu.get_barrier_semaphore()
    greeted = [device(xs(a), ys(b), z, c) for a, b in PLANE]
    greeted += [device(xs(a), y, zs(d), c) for a, d in SIDE if d > 0] + [sibling]
    for peer in greeted:
        pl.semaphore_signal(barrier, inc=1, device_id=peer, device_id_type=MESH)

    copies = []

    def send(src, dst, peer):
        at = len(copies)
        copy = pltpu.make_async_remote_copy(
            src_ref=src, dst_ref=dst, send_sem=ssem.at[at], recv_sem=rsem.at[at],
            device_id=peer, device_id_type=MESH,
        )
        copy.start()
        copies.append(copy)
        return copy

    def arrive(batch):
        for copy in batch:
            copy.wait_recv()

    own_rows = separator_rows(sep_factor, sep_diag, turned, position)
    for i in range(WIDE // 512):
        m_ref[z, c, :, i * 512 : (i + 1) * 512] = own_rows[i * BLK : (i + 1) * BLK]

    scale = 1.0 / diag[...]
    loads[0].wait()
    invert(factor, scale, inverse)
    loads[1].wait()
    right_t = rhs[...].T
    solved_t[...] = small_dot(right_t, inverse[...], NT) * scale
    current[...] = solved_t[...]

    pl.semaphore_wait(barrier, len(greeted))

    right, left = device(x, y, zs(1), c), device(x, y, zs(NZ - 1), c)

    def pass_on(block, start, size, peer):
        ref = m_ref.at[block, c, :, pl.ds(start, size)]
        return send(ref, ref, peer)

    ring, steps, shared = [], [1] * len(ROUNDS), [None] * len(ROUNDS)
    for start, stop in ROUNDS:
        ring.append([pass_on(z, start, stop - start, right), pass_on(z, start, stop - start, left)])

    def advance(turn):
        step = steps[turn]
        steps[turn] = step + 1
        start, stop = ROUNDS[turn]
        size = stop - start
        from_left, from_right = zs(NZ - step), zs(step)
        arrive(ring[turn])
        if step < 3:
            ring[turn] = [pass_on(from_left, start, size, right), pass_on(from_right, start, size, left)]
        elif step == 3:
            ring[turn] = [
                pass_on(from_left, start, size // 2, right),
                pass_on(from_right, start + size // 2, size // 2, left),
            ]
        else:
            ref = m_ref.at[:, c, :, pl.ds(start, size)]
            shared[turn] = [send(ref, ref, sibling)]

    loads[2].wait()
    solved_high, solved_low = split(solved_t[...])
    solved_both = jnp.concatenate([solved_high, solved_low], axis=0)

    def coupling_terms(level):
        def step(i, carry):
            at = pl.ds(pl.multiple_of(sub_start(level) + i * 256, 256), 256)
            high, low = split(update[at, :])
            update_high[at, :] = high
            update_low[at, :] = low
            first = lax.dot_general(solved_both, high, NT, preferred_element_type=F32)
            second = lax.dot_general(solved_high, low, NT, preferred_element_type=F32)
            top, bottom = split(first[:RHS] + first[RHS:] + second)
            terms[:RHS, at] = top
            terms[RHS:, at] = bottom
            return carry

        lax.fori_loop(0, (ROWS >> level) // 512, step, 0)

    places = []
    for level in range(LEVELS):
        count = ROWS >> level + 1
        places.append(reorder(rows[:, sub_start(level) : sub_start(level) + count]))

    def chosen(level, i):
        count = ROWS >> level + 1
        ids = iota((256, count), 0) + i * 256
        return jnp.where(ids == places[level], 1.0, 0.0).astype(BF16)

    mark = jnp.where(iota((BLK, LANES), 1) == z * 16 + c * BLK + iota((BLK, LANES), 0), 1.0, 0.0)

    def node_terms(level, ut, first, last):
        count = ROWS >> level + 1
        listed = terms[:, sub_start(level) : sub_start(level) + count]

        def step(i, carry):
            both = lax.dot_general(listed, chosen(level, i), NT, preferred_element_type=F32)
            total = (both[:RHS] + both[RHS:]) * -weight_scale(level)
            for k in range(2):
                part = total[:, k * LANES : (k + 1) * LANES]
                if level == 0:
                    ut[i // 2, i % 2 * 2 + k] = part
                elif level == 1:
                    ut[i % 2 * 2 + k, i // 2] = part
                else:
                    ut[2 * i + k] = part
            return carry

        lax.fori_loop(first, last, step, 0)

    def own_term(level):
        return lax.dot_general(
            rhs_sep[level], mark, TN, precision=lax.Precision.HIGHEST, preferred_element_type=F32
        )

    mine = pl.ds(pl.multiple_of(c * LANES, LANES), LANES)
    other = pl.ds(pl.multiple_of((1 - c) * LANES, LANES), LANES)
    cols = pl.ds(pl.multiple_of(z * COLS, COLS), COLS)
    spread = pl.ds(pl.multiple_of(c * LANES + z * COLS, COLS), COLS)

    def add_own(total, own):
        def step(i, carry):
            total[i] = total[i] + own[i, mine, :]
            return carry

        lax.fori_loop(0, total.shape[0], step, 0)

    def z_stage(summed, parts):
        return [
            send(summed.at[pl.ds(pl.multiple_of(zs(d) * COLS, COLS), COLS), :], parts.at[d - 1], device(x, y, zs(d), c))
            for d in Z_PEERS
        ]

    def z_sum(summed, parts, batch):
        arrive(batch)
        total = summed[cols, :]
        for d in range(NZ - 1):
            total = total + parts[d]
        return total

    pieces = [(2, i) for i in range(2)] + [(1, i) for i in range(4)] + [(0, i) for i in range(8)]

    def work(amount):
        for _ in range(amount):
            if pieces:
                level, i = pieces.pop()
                count = ROWS >> level + 1
                listed = slice(sub_start(level), sub_start(level) + count)
                at = slice(row_start(level) + i * 256, row_start(level) + i * 256 + 256)
                pick = chosen(level, i)
                moved_high[at, :] = jnp.dot(pick, update_high[listed, :], preferred_element_type=F32).astype(BF16)
                moved_low[at, :] = jnp.dot(pick, update_low[listed, :], preferred_element_type=F32).astype(BF16)

    def x_send(piece, landed):
        return [send(piece(xs(a)), landed.at[a - 1], device(xs(a), y, z, c)) for a in X_PEERS]

    def y_send(piece, landed):
        return [send(piece(ys(b)), landed.at[b - 1], device(x, ys(b), z, c)) for b in Y_PEERS]

    coupling_terms(2)
    node_terms(2, ut2, 0, 2)
    ut2[x] = ut2[x] + own_term(2)
    c2 = send(ut2.at[:, other, :], b2c, sibling)
    coupling_terms(1)
    arrive([c2])
    add_own(b2c, ut2)
    x2s = x_send(lambda to: b2c.at[to], b2x)
    node_terms(1, ut1, 0, 4)
    ut1[x, yy] = ut1[x, yy] + own_term(1)
    c1 = send(ut1.at[:, :, other, :], b1c, sibling)
    advance(0)
    coupling_terms(0)
    mid = LANES // 2
    arrive([c1])

    def add_pair(i, carry):
        for k in range(2):
            b1c[i, k] = b1c[i, k] + ut1[i, k, mine, :]
        return carry

    lax.fori_loop(0, NX, add_pair, 0)
    x1s = x_send(lambda to: b1c.at[to, :, 0:mid, :], b1x)
    y1s = send(b1c.at[:, 1 - yy, mid:LANES, :], b1y, device(x, partner, z, c))
    advance(1)
    node_terms(0, ut0, 0, 2)
    node_terms(0, ut0, 2, 4)
    lower = jnp.where(y < 2, 1.0, 0.0)
    own0 = own_term(0)
    ut0[y % 2, x] = ut0[y % 2, x] + own0 * lower
    c0a = send(ut0.at[0:2, :, other, :], b0c.at[0:2], sibling)
    arrive(x2s)
    b2s[...] = b2c[x] + b2x[0] + b2x[1] + b2x[2]
    z2s = z_stage(b2s, b2z)
    node_terms(0, ut0, 4, 6)
    advance(2)
    node_terms(0, ut0, 6, 8)
    ut0[2 + y % 2, x] = ut0[2 + y % 2, x] + own0 * (1.0 - lower)
    c0b = send(ut0.at[2:4, :, other, :], b0c.at[2:4], sibling)
    advance(0)

    def add_rows(first):
        def step(i, carry):
            for k in range(NX):
                b0c[first + i, k] = b0c[first + i, k] + ut0[first + i, k, mine, :]
            return carry

        lax.fori_loop(0, 2, step, 0)

    arrive([c0a])
    add_rows(0)
    x0s = x_send(lambda to: b0c.at[0:2, to, mid:LANES, :], b0x.at[:, 0:2])
    arrive([c0b])
    add_rows(2)
    y0s = y_send(lambda to: b0c.at[to, :, 0:mid, :], b0y)
    x0s += x_send(lambda to: b0c.at[2:4, to, mid:LANES, :], b0x.at[:, 2:4])
    advance(1)
    advance(2)
    advance(0)
    r2 = z_sum(b2s, b2z, z2s)
    g2[x] = r2
    a2 = [send(g2.at[x], g2.at[x], device(xs(a), y, z, c)) for a in X_PEERS]
    arrive(x1s)
    for i in range(2):
        b1p[i] = b1c[x, i, 0:mid, :] + b1x[0, i] + b1x[1, i] + b1x[2, i]
    y1t = send(b1p.at[1 - yy], b1v, device(x, partner, z, c))
    arrive([y1s])
    for i in range(NX):
        b1q[i] = b1c[i, yy, mid:LANES, :] + b1y[i]
    x1t = x_send(lambda to: b1q.at[to], b1u)
    advance(1)
    work(1)
    arrive([y1t])
    b1t[0:mid, :] = b1p[yy] + b1v[...]
    arrive(x1t)
    b1t[mid:LANES, :] = b1q[x] + b1u[0] + b1u[1] + b1u[2]
    z1s = z_stage(b1t, b1z)
    advance(0)

    def joined(ref):
        return jnp.concatenate([ref[i] for i in range(ref.shape[0])], axis=1)

    def spill(value, ref):
        for i in range(ref.shape[0]):
            ref[i] = value[:, i * LANES : (i + 1) * LANES]

    def columns(start, size):
        return m_high[:, start : start + size], m_low[:, start : start + size]

    def unpack(turn):
        arrive(shared[turn])
        start, stop = ROUNDS[turn]
        for at in range(start, stop, 512):
            high, low = split(m_ref[:, :, :, at : at + 512].reshape(LANES, 512))
            m_high[:, at : at + 512] = high
            m_low[:, at : at + 512] = low

    here1 = yy * NX + x
    here0 = y * NX + x

    def scatter_half(part, landed):
        return [
            send(part.at[(yy if b == 0 else 1 - yy) * NX + xs(a)], landed.at[k], device(xs(a), pair_y(b), z, c))
            for k, (a, b) in enumerate(HALF)
        ]

    def gather_half(whole):
        return [send(whole.at[here1], whole.at[here1], device(xs(a), pair_y(b), z, c)) for a, b in HALF]

    def scatter_plane(part, landed):
        return [
            send(part.at[ys(b) * NX + xs(a)], landed.at[k], device(xs(a), ys(b), z, c))
            for k, (a, b) in enumerate(PLANE)
        ]

    def gather_plane(whole):
        return [send(whole.at[here0], whole.at[here0], device(xs(a), ys(b), z, c)) for a, b in PLANE]

    def summed(part, here, landed, batch):
        arrive(batch)
        total = part[here]
        for k in range(landed.shape[0]):
            total = total + landed[k]
        return total

    s0_scale, s1_scale = weight_scale(0), weight_scale(1)

    arrive(a2)
    advance(2)
    unpack(0)
    solved2 = small_dot(joined(g2), columns(G2, 512), NT)
    spill(small_dot(solved2, columns(E21, 1024), NN), p1)
    p1s = scatter_half(p1, p1r)
    advance(1)
    work(1)
    arrive(y0s)
    for i in range(NX):
        b0p[i] = b0c[y, i, 0:mid, :] + b0y[0, i] + b0y[1, i] + b0y[2, i]
    x0t = x_send(lambda to: b0p.at[to], b0u)
    arrive(x0s)
    for i in range(NY):
        b0q[i] = b0c[i, x, mid:LANES, :] + b0x[0, i] + b0x[1, i] + b0x[2, i]
    y0t = y_send(lambda to: b0q.at[to], b0v)
    r1 = z_sum(b1t, b1z, z1s)
    g1[here1] = r1 - s1_scale * summed(p1, here1, p1r, p1s)
    a1 = gather_half(g1)
    unpack(1)
    up0 = small_dot(solved2, columns(E20, 2048), NN)
    advance(2)
    arrive(x0t)
    b0t[0:mid, :] = b0p[x] + b0u[0] + b0u[1] + b0u[2]
    arrive(y0t)
    b0t[mid:LANES, :] = b0q[y] + b0v[0] + b0v[1] + b0v[2]
    z0s = z_stage(b0t, b0z)
    arrive(a1)
    solved1 = small_dot(joined(g1), columns(G1, 1024), NT)
    unpack(2)
    spill(up0 + small_dot(solved1, columns(E10, 2048), NN), p0)
    p0s = scatter_plane(p0, p0r)
    work(2)
    r0 = z_sum(b0t, b0z, z0s)
    g0[here0] = r0 - s0_scale * summed(p0, here0, p0r, p0s)
    a0 = gather_plane(g0)
    work(2)
    arrive(a0)
    solved0 = small_dot(joined(g0), columns(G0, 2048), NT)

    def block_of(d):
        return pl.ds(pl.multiple_of(c * LANES + zs(d) * COLS, COLS), COLS)

    def along_z(chunk, at, result):
        result[at, spread, :] = chunk[at]
        return [send(chunk.at[at], result.at[at, spread, :], device(x, y, zs(d), c)) for d in Z_PEERS]

    spill(small_dot(solved0, columns(G0, 2048), NN), q0)
    q0s = scatter_plane(q0, q0r)
    work(2)
    h0[here0] = summed(q0, here0, q0r, q0s)
    a0 = gather_plane(h0)
    work(2)
    arrive(a0)
    x0[:, spread, :] = h0[...]
    far0, near0 = [
        [send(h0, x0.at[:, spread, :], device(x, y, zs(d), c)) for d in ds] for ds in ((2, 6), (1, 7))
    ]
    found0 = joined(h0)
    y1 = solved1 - s0_scale * small_dot(found0, columns(E10, 2048), NT)
    spill(small_dot(y1, columns(G1, 1024), NN), q1)
    q1s = scatter_half(q1, q1r)
    y2 = solved2 - s0_scale * small_dot(found0, columns(E20, 2048), NT)
    work(1)
    h1[here1] = summed(q1, here1, q1r, q1s)
    a1 = gather_half(h1)
    z1h = along_z(h1, here1, x1)
    work(2)
    arrive(a1)
    y2 = y2 - s1_scale * small_dot(joined(h1), columns(E21, 1024), NT)
    spill(small_dot(y2, columns(G2, 512), NN), q2)
    q2s = x_send(lambda to: q2.at[to], q2r)
    arrive(far0)
    low, high = block_of(6), block_of(2)
    far0 = [
        send(x0.at[:, low, :], x0.at[:, low, :], device(x, y, zs(1), c)),
        send(x0.at[:, high, :], x0.at[:, high, :], device(x, y, zs(7), c)),
        send(x0.at[0:8, low, :], x0.at[0:8, low, :], device(x, y, zs(2), c)),
        send(x0.at[8:16, high, :], x0.at[8:16, high, :], device(x, y, zs(6), c)),
    ]
    h2[x] = summed(q2, x, q2r, q2s)
    x2[x, spread, :] = h2[x]
    z2h = [send(h2.at[x], x2.at[x, spread, :], device(xs(a), y, zs(d), c)) for a, d in SIDE]
    arrive(z1h)
    w1 = [send(x1.at[here1, mine, :], x1.at[here1, mine, :], device(xs(a), pair_y(b), z, c)) for a, b in HALF]
    work(99)
    arrive(near0)

    def swap_cores(result, batch):
        arrive(batch)
        return send(result.at[:, mine, :], result.at[:, mine, :], sibling)

    def take_in(level, result, copy):
        arrive([copy])

        def step(i, carry):
            at = pl.ds(pl.multiple_of(row_start(level) + i * 256, 256), 256)
            both = jnp.concatenate([result[2 * i], result[2 * i + 1]], axis=1)
            high, low = split(both)
            stacked = jnp.concatenate([high, low], axis=0)
            first = jnp.dot(stacked, moved_high[at, :], preferred_element_type=F32)
            second = jnp.dot(high, moved_low[at, :], preferred_element_type=F32)
            current[...] = current[...] - weight_scale(level) * (first[:RHS] + first[RHS:] + second)
            return carry

        lax.fori_loop(0, (ROWS >> level) // 256, step, 0)
        chunk = [here0, here1, x][level]
        out_sep[level] = lax.dot_general(
            mark, result[chunk], NT, precision=lax.Precision.HIGHEST, preferred_element_type=F32
        )

    w0 = swap_cores(x0, far0)
    w1 = swap_cores(x1, w1)
    take_in(0, x0, w0)
    w2 = swap_cores(x2, z2h)
    take_in(1, x1, w1)
    take_in(2, x2, w2)
    out_sub[...] = small_dot(current[...] * scale, inverse[...], NN).T
    for copy in copies:
        copy.wait_send()


N_COPIES = 320


def whole(*operands):
    def piece(*lead, rows=COLS):
        return pltpu.VMEM((*lead, rows, LANES), F32)

    scratch = [
        pltpu.VMEM((LOC, LOC), F32), pltpu.VMEM((LOC, RHS), F32), pltpu.VMEM((1792, LOC), F32),
        pltpu.VMEM((LOC, LOC), F32), pltpu.VMEM((RHS, LOC), F32), pltpu.VMEM((RHS, LOC), F32),
        pltpu.VMEM((2 * RHS, 1792), BF16), pltpu.VMEM((1792, LOC), BF16), pltpu.VMEM((1792, LOC), BF16),
        pltpu.VMEM((3584, LOC), BF16), pltpu.VMEM((3584, LOC), BF16),
        piece(4, 4, rows=RHS), piece(4, 2, rows=RHS), piece(4, rows=RHS),
        pltpu.VMEM((NZ, 2, BLK, WIDE), F32), pltpu.VMEM((LANES, WIDE), BF16), pltpu.VMEM((LANES, WIDE), BF16),
        piece(16, rows=RHS), piece(8, rows=RHS), piece(4, rows=RHS),
        piece(4, rows=LANES), piece(4, 2, rows=LANES), piece(4, 4, rows=LANES),
        piece(3, rows=LANES), piece(rows=LANES), piece(7),
        piece(3, 2, rows=64), piece(4, rows=64), piece(2, rows=64), piece(4, rows=64),
        piece(3, rows=64), piece(rows=64), piece(rows=LANES), piece(7),
        piece(3, 4, rows=64), piece(3, 4, rows=64), piece(4, rows=64), piece(4, rows=64),
        piece(3, rows=64), piece(3, rows=64), piece(rows=LANES), piece(7),
        piece(4), piece(8), piece(7), piece(8), piece(16), piece(15), piece(16),
        piece(16), piece(15), piece(16), piece(8), piece(7), piece(8), piece(4), piece(3), piece(4),
        pltpu.SemaphoreType.DMA((3,)), pltpu.SemaphoreType.DMA((N_COPIES,)), pltpu.SemaphoreType.DMA((N_COPIES,)),
    ]
    vmem = pl.BlockSpec(memory_space=pltpu.VMEM)
    hbm = pl.BlockSpec(memory_space=pl.ANY)
    return pl.pallas_call(
        whole_kernel,
        out_shape=[jax.ShapeDtypeStruct((LOC, RHS), F32), jax.ShapeDtypeStruct((LEVELS, BLK, RHS), F32)],
        in_specs=[vmem] * 6 + [hbm] * 3,
        out_specs=[vmem] * 2,
        scratch_shapes=scratch,
        compiler_params=pltpu.CompilerParams(
            collective_id=0, has_side_effects=True, vmem_limit_bytes=58 * 1024 * 1024
        ),
    )(*operands)


def copy_kernel(first, second, first_out, second_out):
    first_out[...] = first[...]
    second_out[...] = second[...]


def hand_on(*results):
    vmem = pl.BlockSpec(memory_space=pltpu.VMEM)
    return pl.pallas_call(
        copy_kernel,
        out_shape=[jax.ShapeDtypeStruct(result.shape, F32) for result in results],
        in_specs=[vmem] * 2,
        out_specs=[vmem] * 2,
        compiler_params=pltpu.CompilerParams(vmem_limit_bytes=58 * 1024 * 1024),
    )(*results)


def body(rhs_sub, rhs_sep, sub_factor, sub_diag, sep_factor, sep_diag, sub_update, update_rows, sep_update):
    result_sub, result_sep = whole(
        sub_diag, update_rows, rhs_sep, sep_factor, sep_diag, sep_update[0].T, sub_factor[0], rhs_sub[0], sub_update[0]
    )
    return hand_on(result_sub[None], result_sep)


def solution(mesh):
    both = ("leaf", "panel")
    in_specs = (
        P(both, None, None), P(None, both, None), P(both, None, None), P(both, None), P(both, None),
        P(None, both), P(both, None, None), P(both, None), P(both, None, None),
    )
    out_specs = (P(both, None, None), P(None, both, None))
    return jax.shard_map(body, mesh=mesh, in_specs=in_specs, out_specs=out_specs, check_vma=False)
```

```python
import jax
import jax.numpy as jnp
from jax import lax
from jax.experimental import pallas as pl
from jax.experimental.pallas import tpu as pltpu
from jax.sharding import PartitionSpec as P

MESH = pl.DeviceIdType.MESH
F32 = jnp.float32
BF16 = jnp.bfloat16
NN = (((1,), (0,)), ((), ()))
NT = (((1,), (1,)), ((), ()))
TN = (((0,), (0,)), ((), ()))

NX, NY, NZ = 4, 4, 8
ROWS, RHS, LOC, BLK = 2048, 256, 512, 8
LEVELS = 3
LANES = 128
COLS = 16
G2, E21, G1, E20, E10, G0, WIDE = 0, 512, 1536, 2560, 4608, 6656, 8704


def weight_scale(target):
    fan_total = (256 >> target) * LOC // 2 + (LEVELS - 1 - target) * (ROWS >> target)
    return float(fan_total) ** (-0.5)


def split(value):
    high = value.astype(BF16)
    return high, (value - high.astype(F32)).astype(BF16)


def small_dot(left, right, dims):
    left_high, left_low = split(left)
    right_high, right_low = right if isinstance(right, tuple) else split(right)
    rows = left.shape[0]
    both = jnp.concatenate([left_high, left_low], axis=0)
    first = lax.dot_general(both, right_high, dims, preferred_element_type=F32)
    second = lax.dot_general(left_high, right_low, dims, preferred_element_type=F32)
    return first[:rows] + first[rows:] + second


def place():
    leaf, panel = lax.axis_index("leaf"), lax.axis_index("panel")
    return panel // 2, leaf // NZ, leaf % NZ, panel % 2


def device(x, y, z, c):
    return (y * NZ + z, x * 2 + c)


def hops(step, size):
    return min(step, size - step)


X_PEERS = (2, 1, 3)
Y_PEERS = (2, 1, 3)
Z_PEERS = (4, 3, 5, 2, 6, 1, 7)
PLANE = sorted(
    [(a, b) for a in range(NX) for b in range(NY)][1:], key=lambda ab: -hops(ab[0], NX) - hops(ab[1], NY)
)
SIDE = sorted(
    [(a, d) for a in range(NX) for d in range(NZ)][1:], key=lambda ad: -hops(ad[0], NX) - hops(ad[1], NZ)
)
HALF = sorted([(a, b) for a in range(NX) for b in range(2)][1:], key=lambda ab: -hops(ab[0], NX) - ab[1])
ROUNDS = ((0, 1536), (1536, 4608), (4608, 8704))


def split3(value):
    high = value.astype(BF16)
    rest = value - high.astype(F32)
    middle = rest.astype(BF16)
    return high, middle, (rest - middle.astype(F32)).astype(BF16)


def exact_dot(left, right):
    return jnp.dot(left, right, precision=lax.Precision.HIGHEST, preferred_element_type=F32)


def iota(shape, dim):
    return lax.broadcasted_iota(jnp.int32, shape, dim)


def reorder(rows):
    return (rows >> 9 << 9) + ((rows >> 4 & 3) << 7) + ((rows >> 6 & 7) << 4) + (rows & 15)


def sub_start(level):
    return sum(ROWS >> k + 1 for k in range(level))


def row_start(level):
    return sum(ROWS >> k for k in range(level))


def invert(factor, scale, inverse):
    lane = iota((32, LANES), 1)
    row, col = iota((LANES, LANES), 0), iota((LANES, LANES), 1)
    blocks, packed = [], []
    for g in range(4):
        at = slice(g * LANES, (g + 1) * LANES)
        block = jnp.where(row > col, factor[at, at] * scale[:, at], 0.0)
        blocks.append(block)
        parts = [jnp.where(lane >> 5 == q, block[32 * q : 32 * q + 32], 0.0) for q in range(4)]
        packed.append(parts[0] + parts[1] + parts[2] + parts[3])
    unit = (iota((32, LANES), 0) == (lane & 31)).astype(F32)
    found = [unit] * 4
    for k in range(31):
        index = (lane & 96) + k
        for g in range(4):
            coefficient = jnp.take_along_axis(packed[g], index, axis=1, mode="promise_in_bounds")
            found[g] = found[g] - coefficient * found[g][k : k + 1, :]
    whole = []
    for g in range(4):
        total = jnp.concatenate([jnp.where(lane >> 5 == q, found[g], 0.0) for q in range(4)], axis=0)
        whole.append(total)
    for bit in (5, 6):
        below = (row >> bit + 1 == col >> bit + 1) & (row >> bit > col >> bit)
        inner = [exact_dot(jnp.where(below, blocks[g], 0.0), whole[g]) for g in range(4)]
        whole = [whole[g] - exact_dot(whole[g], inner[g]) for g in range(4)]
    inverse[...] = jnp.zeros_like(inverse)
    for h in range(2):
        first = slice(h * 256, h * 256 + 128)
        second = slice(h * 256 + 128, h * 256 + 256)
        inner = exact_dot(factor[second, first] * scale[:, first], whole[2 * h])
        inverse[first, first] = whole[2 * h]
        inverse[second, second] = whole[2 * h + 1]
        inverse[second, first] = -exact_dot(whole[2 * h + 1], inner)
    inner = exact_dot(factor[256:, :256] * scale[:, :256], inverse[:256, :256])
    inverse[256:, :256] = -exact_dot(inverse[256:, 256:], inner)


def separator_rows(sep_factor, sep_diag, turned, position):
    inverses = []
    eye = iota((BLK, BLK), 0) == iota((BLK, BLK), 1)
    for level in range(LEVELS):
        node_rows = ROWS >> level
        start = row_start(level)
        strict = sep_factor[:, start : start + node_rows]
        diagonal = jnp.sum(jnp.where(eye, sep_diag[level : level + 1, :], 0.0), axis=1, keepdims=True)
        own = position % (256 >> level) * BLK + iota((BLK, node_rows), 0)
        cols = iota((BLK, node_rows), 1)
        inverses.append(jnp.where(cols < own, strict, 0.0) + jnp.where(cols == own, diagonal, 0.0))
    e10, e20, e21 = turned[:, :2048], turned[:, 2048:4096], turned[:, 4096:]
    pieces = [inverses[2], e21, inverses[1], e20, e10, inverses[0]]
    blocks = [piece[:, i : i + 512] for piece in pieces for i in range(0, piece.shape[1], 512)]
    stacked = jnp.concatenate(blocks, axis=0)
    swap = jnp.where(reorder(iota((512, 512), 0)) == iota((512, 512), 1), 1.0, 0.0).astype(BF16)
    count = stacked.shape[0]
    exact = jnp.concatenate([part.astype(F32) for part in split3(stacked)], axis=0).astype(BF16)
    moved = jnp.dot(exact, swap, preferred_element_type=F32)
    return moved[:count] + moved[count : 2 * count] + moved[2 * count :]


def whole_kernel(
    diag, rows, rhs_sep, sep_factor, sep_diag, turned, factor_hbm, rhs_hbm, update_hbm,
    out_sub, out_sep,
    factor, rhs, update, inverse, solved_t, current, terms, update_high, update_low, moved_high, moved_low,
    inverse_high, inverse_low,
    ut0, ut1, ut2, m_ref, m_high, m_low, x0, x1, x2,
    b2c, b1c, b0c, b2x, b2s, b2z, b1x, b1y, b1p, b1q, b1u, b1v, b1t, b1z, b0y, b0x, b0p, b0q, b0u, b0v, b0t, b0z,
    g2, p1, p1r, g1, p0, p0r, g0, q0, q0r, h0, q1, q1r, h1, q2, q2r, h2,
    lsem, ssem, rsem,
):
    x, y, z, c = place()
    position = lax.axis_index("leaf") * 8 + lax.axis_index("panel")
    partner = y + 1 - 2 * (y % 2)
    yy = y % 2
    sibling = device(x, y, z, 1 - c)
    loads = [
        pltpu.make_async_copy(src, dst, lsem.at[i])
        for i, (src, dst) in enumerate(((factor_hbm, factor), (rhs_hbm, rhs), (update_hbm, update)))
    ]
    for load in loads:
        load.start()

    def xs(a):
        return (x + a) % NX

    def ys(b):
        return (y + b) % NY

    def zs(d):
        return (z + d) % NZ

    def pair_y(b):
        return partner if b else y

    barrier = pltpu.get_barrier_semaphore()
    greeted = [device(xs(a), ys(b), z, c) for a, b in PLANE]
    greeted += [device(xs(a), y, zs(d), c) for a, d in SIDE if d > 0] + [sibling]
    for peer in greeted:
        pl.semaphore_signal(barrier, inc=1, device_id=peer, device_id_type=MESH)

    copies = []

    def send(src, dst, peer):
        at = len(copies)
        copy = pltpu.make_async_remote_copy(
            src_ref=src, dst_ref=dst, send_sem=ssem.at[at], recv_sem=rsem.at[at],
            device_id=peer, device_id_type=MESH,
        )
        copy.start()
        copies.append(copy)
        return copy

    def arrive(batch):
        for copy in batch:
            copy.wait_recv()

    loads[0].wait()
    loads[1].wait()
    own_rows = separator_rows(sep_factor, sep_diag, turned, position)
    for i in range(WIDE // 512):
        m_ref[z, c, :, i * 512 : (i + 1) * 512] = own_rows[i * BLK : (i + 1) * BLK]

    scale = 1.0 / diag[...]
    invert(factor, scale, inverse)
    right_t = rhs[...].T
    solved_t[...] = small_dot(right_t, inverse[...], NT) * scale

    pl.semaphore_wait(barrier, len(greeted))

    right, left = device(x, y, zs(1), c), device(x, y, zs(NZ - 1), c)

    def pass_on(block, start, size, peer):
        ref = m_ref.at[block, c, :, pl.ds(start, size)]
        return send(ref, ref, peer)

    ring, steps, shared = [], [1] * len(ROUNDS), [None] * len(ROUNDS)
    for start, stop in ROUNDS:
        ring.append([pass_on(z, start, stop - start, right), pass_on(z, start, stop - start, left)])

    def advance(turn):
        step = steps[turn]
        steps[turn] = step + 1
        start, stop = ROUNDS[turn]
        size = stop - start
        from_left, from_right = zs(NZ - step), zs(step)
        arrive(ring[turn])
        if step < 3:
            ring[turn] = [pass_on(from_left, start, size, right), pass_on(from_right, start, size, left)]
        elif step == 3:
            ring[turn] = [
                pass_on(from_left, start, size // 2, right),
                pass_on(from_right, start + size // 2, size // 2, left),
            ]
        else:
            ref = m_ref.at[:, c, :, pl.ds(start, size)]
            shared[turn] = [send(ref, ref, sibling)]

    loads[2].wait()
    solved_high, solved_low = split(solved_t[...])
    solved_both = jnp.concatenate([solved_high, solved_low], axis=0)

    def coupling_terms(level):
        def step(i, carry):
            at = pl.ds(pl.multiple_of(sub_start(level) + i * 256, 256), 256)
            high, low = split(update[at, :])
            update_high[at, :] = high
            update_low[at, :] = low
            first = lax.dot_general(solved_both, high, NT, preferred_element_type=F32)
            second = lax.dot_general(solved_high, low, NT, preferred_element_type=F32)
            top, bottom = split(first[:RHS] + first[RHS:] + second)
            terms[:RHS, at] = top
            terms[RHS:, at] = bottom
            return carry

        lax.fori_loop(0, (ROWS >> level) // 512, step, 0)

    places = []
    for level in range(LEVELS):
        count = ROWS >> level + 1
        places.append(reorder(rows[:, sub_start(level) : sub_start(level) + count]))

    def chosen(level, i):
        count = ROWS >> level + 1
        ids = iota((256, count), 0) + i * 256
        return jnp.where(ids == places[level], 1.0, 0.0).astype(BF16)

    mark = jnp.where(iota((BLK, LANES), 1) == z * 16 + c * BLK + iota((BLK, LANES), 0), 1.0, 0.0)

    def node_terms(level, ut, first, last):
        count = ROWS >> level + 1
        listed = terms[:, sub_start(level) : sub_start(level) + count]

        def step(i, carry):
            both = lax.dot_general(listed, chosen(level, i), NT, preferred_element_type=F32)
            total = (both[:RHS] + both[RHS:]) * -weight_scale(level)
            for k in range(2):
                part = total[:, k * LANES : (k + 1) * LANES]
                if level == 0:
                    ut[i // 2, i % 2 * 2 + k] = part
                elif level == 1:
                    ut[i % 2 * 2 + k, i // 2] = part
                else:
                    ut[2 * i + k] = part
            return carry

        lax.fori_loop(first, last, step, 0)

    def own_term(level):
        return lax.dot_general(
            rhs_sep[level], mark, TN, precision=lax.Precision.HIGHEST, preferred_element_type=F32
        )

    mine = pl.ds(pl.multiple_of(c * LANES, LANES), LANES)
    other = pl.ds(pl.multiple_of((1 - c) * LANES, LANES), LANES)
    cols = pl.ds(pl.multiple_of(z * COLS, COLS), COLS)
    spread = pl.ds(pl.multiple_of(c * LANES + z * COLS, COLS), COLS)

    def add_own(total, own):
        def step(i, carry):
            total[i] = total[i] + own[i, mine, :]
            return carry

        lax.fori_loop(0, total.shape[0], step, 0)

    def z_stage(summed, parts):
        return [
            send(summed.at[pl.ds(pl.multiple_of(zs(d) * COLS, COLS), COLS), :], parts.at[d - 1], device(x, y, zs(d), c))
            for d in Z_PEERS
        ]

    def z_sum(summed, parts, batch):
        arrive(batch)
        total = summed[cols, :]
        for d in range(NZ - 1):
            total = total + parts[d]
        return total

    pieces = [(2, i) for i in range(2)] + [(1, i) for i in range(4)] + [(0, i) for i in range(8)]

    def work(amount):
        for _ in range(amount):
            if pieces:
                level, i = pieces.pop()
                count = ROWS >> level + 1
                listed = slice(sub_start(level), sub_start(level) + count)
                at = slice(row_start(level) + i * 256, row_start(level) + i * 256 + 256)
                pick = chosen(level, i)
                entries = jnp.dot(pick, update_high[listed, :], preferred_element_type=F32)
                entries = entries + jnp.dot(pick, update_low[listed, :], preferred_element_type=F32)
                high, low = split(small_dot(entries * scale, (inverse_high[...], inverse_low[...]), NN))
                moved_high[at, :] = high
                moved_low[at, :] = low

    def x_send(piece, landed):
        return [send(piece(xs(a)), landed.at[a - 1], device(xs(a), y, z, c)) for a in X_PEERS]

    def y_send(piece, landed):
        return [send(piece(ys(b)), landed.at[b - 1], device(x, ys(b), z, c)) for b in Y_PEERS]

    coupling_terms(2)
    node_terms(2, ut2, 0, 2)
    ut2[x] = ut2[x] + own_term(2)
    c2 = send(ut2.at[:, other, :], b2c, sibling)
    coupling_terms(1)
    arrive([c2])
    add_own(b2c, ut2)
    x2s = x_send(lambda to: b2c.at[to], b2x)
    node_terms(1, ut1, 0, 4)
    ut1[x, yy] = ut1[x, yy] + own_term(1)
    c1 = send(ut1.at[:, :, other, :], b1c, sibling)
    advance(0)
    coupling_terms(0)
    mid, mid0 = LANES // 2, 48
    arrive([c1])

    def add_pair(i, carry):
        for k in range(2):
            b1c[i, k] = b1c[i, k] + ut1[i, k, mine, :]
        return carry

    lax.fori_loop(0, NX, add_pair, 0)
    x1s = x_send(lambda to: b1c.at[to, :, 0:mid, :], b1x)
    y1s = send(b1c.at[:, 1 - yy, mid:LANES, :], b1y, device(x, partner, z, c))
    advance(1)
    node_terms(0, ut0, 0, 2)
    node_terms(0, ut0, 2, 4)
    lower = jnp.where(y < 2, 1.0, 0.0)
    own0 = own_term(0)
    ut0[y % 2, x] = ut0[y % 2, x] + own0 * lower
    c0a = send(ut0.at[0:2, :, other, :], b0c.at[0:2], sibling)
    arrive(x2s)
    b2s[...] = b2c[x] + b2x[0] + b2x[1] + b2x[2]
    z2s = z_stage(b2s, b2z)
    node_terms(0, ut0, 4, 6)
    advance(2)
    node_terms(0, ut0, 6, 8)
    ut0[2 + y % 2, x] = ut0[2 + y % 2, x] + own0 * (1.0 - lower)
    c0b = send(ut0.at[2:4, :, other, :], b0c.at[2:4], sibling)
    advance(0)

    def add_rows(first):
        def step(i, carry):
            for k in range(NX):
                b0c[first + i, k] = b0c[first + i, k] + ut0[first + i, k, mine, :]
            return carry

        lax.fori_loop(0, 2, step, 0)

    arrive([c0a])
    add_rows(0)
    x0s = x_send(lambda to: b0c.at[0:2, to, mid0:LANES, :], b0x.at[:, 0:2])
    arrive([c0b])
    add_rows(2)
    y0s = y_send(lambda to: b0c.at[to, :, 0:mid0, :], b0y)
    x0s += x_send(lambda to: b0c.at[2:4, to, mid0:LANES, :], b0x.at[:, 2:4])
    advance(1)
    advance(2)
    advance(0)
    r2 = z_sum(b2s, b2z, z2s)
    g2[x] = r2
    a2 = [send(g2.at[x], g2.at[x], device(xs(a), y, z, c)) for a in X_PEERS]
    arrive(x1s)
    for i in range(2):
        b1p[i] = b1c[x, i, 0:mid, :] + b1x[0, i] + b1x[1, i] + b1x[2, i]
    y1t = send(b1p.at[1 - yy], b1v, device(x, partner, z, c))
    arrive([y1s])
    for i in range(NX):
        b1q[i] = b1c[i, yy, mid:LANES, :] + b1y[i]
    x1t = x_send(lambda to: b1q.at[to], b1u)
    advance(1)
    high, low = split(inverse[...])
    inverse_high[...] = high
    inverse_low[...] = low
    work(1)
    arrive([y1t])
    b1t[0:mid, :] = b1p[yy] + b1v[...]
    arrive(x1t)
    b1t[mid:LANES, :] = b1q[x] + b1u[0] + b1u[1] + b1u[2]
    z1s = z_stage(b1t, b1z)
    advance(0)

    def joined(ref):
        return jnp.concatenate([ref[i] for i in range(ref.shape[0])], axis=1)

    def spill(value, ref):
        for i in range(ref.shape[0]):
            ref[i] = value[:, i * LANES : (i + 1) * LANES]

    def columns(start, size):
        return m_high[:, start : start + size], m_low[:, start : start + size]

    def unpack(turn):
        arrive(shared[turn])
        start, stop = ROUNDS[turn]
        for at in range(start, stop, 512):
            high, low = split(m_ref[:, :, :, at : at + 512].reshape(LANES, 512))
            m_high[:, at : at + 512] = high
            m_low[:, at : at + 512] = low

    here1 = yy * NX + x
    here0 = y * NX + x

    def scatter_half(part, landed):
        return [
            send(part.at[(yy if b == 0 else 1 - yy) * NX + xs(a)], landed.at[k], device(xs(a), pair_y(b), z, c))
            for k, (a, b) in enumerate(HALF)
        ]

    def gather_half(whole):
        return [send(whole.at[here1], whole.at[here1], device(xs(a), pair_y(b), z, c)) for a, b in HALF]

    def scatter_plane(part, landed):
        return [
            send(part.at[ys(b) * NX + xs(a)], landed.at[k], device(xs(a), ys(b), z, c))
            for k, (a, b) in enumerate(PLANE)
        ]

    def gather_plane(whole):
        return [send(whole.at[here0], whole.at[here0], device(xs(a), ys(b), z, c)) for a, b in PLANE]

    def summed(part, here, landed, batch):
        arrive(batch)
        total = part[here]
        for k in range(landed.shape[0]):
            total = total + landed[k]
        return total

    s0_scale, s1_scale = weight_scale(0), weight_scale(1)

    arrive(a2)
    advance(2)
    unpack(0)
    solved2 = small_dot(joined(g2), columns(G2, 512), NT)
    spill(small_dot(solved2, columns(E21, 1024), NN), p1)
    p1s = scatter_half(p1, p1r)
    advance(1)
    work(1)
    arrive(y0s)
    for i in range(NX):
        b0p[i] = b0c[y, i, 0:mid0, :] + b0y[0, i] + b0y[1, i] + b0y[2, i]
    x0t = x_send(lambda to: b0p.at[to], b0u)
    arrive(x0s)
    for i in range(NY):
        b0q[i] = b0c[i, x, mid0:LANES, :] + b0x[0, i] + b0x[1, i] + b0x[2, i]
    y0t = y_send(lambda to: b0q.at[to], b0v)
    r1 = z_sum(b1t, b1z, z1s)
    g1[here1] = r1 - s1_scale * summed(p1, here1, p1r, p1s)
    a1 = gather_half(g1)
    unpack(1)
    up0 = small_dot(solved2, columns(E20, 2048), NN)
    advance(2)
    arrive(x0t)
    b0t[0:mid0, :] = b0p[x] + b0u[0] + b0u[1] + b0u[2]
    arrive(y0t)
    b0t[mid0:LANES, :] = b0q[y] + b0v[0] + b0v[1] + b0v[2]
    z0s = z_stage(b0t, b0z)
    arrive(a1)
    solved1 = small_dot(joined(g1), columns(G1, 1024), NT)
    unpack(2)
    spill(up0 + small_dot(solved1, columns(E10, 2048), NN), p0)
    p0s = scatter_plane(p0, p0r)
    work(2)
    r0 = z_sum(b0t, b0z, z0s)
    g0[here0] = r0 - s0_scale * summed(p0, here0, p0r, p0s)
    a0 = gather_plane(g0)
    work(3)
    arrive(a0)
    solved0 = small_dot(joined(g0), columns(G0, 2048), NT)

    def block_of(d):
        return pl.ds(pl.multiple_of(c * LANES + zs(d) * COLS, COLS), COLS)

    def first_leg(ds):
        return [send(h0, x0.at[:, spread, :], device(x, y, zs(d), c)) for d in ds]

    def second_leg():
        arrive(far0)
        low, high = x0.at[:, block_of(6), :], x0.at[:, block_of(2), :]
        first, second = x0.at[0:8, block_of(6), :], x0.at[8:16, block_of(2), :]
        steps = ((low, 1), (high, 7), (first, 2), (second, 6))
        return [send(part, part, device(x, y, zs(d), c)) for part, d in steps]

    def along_z(chunk, at, result):
        result[at, spread, :] = chunk[at]
        return [send(chunk.at[at], result.at[at, spread, :], device(x, y, zs(d), c)) for d in Z_PEERS]

    spill(small_dot(solved0, columns(G0, 2048), NN), q0)
    q0s = scatter_plane(q0, q0r)
    work(2)
    h0[here0] = summed(q0, here0, q0r, q0s)
    a0 = gather_plane(h0)
    work(3)
    arrive(a0)
    x0[:, spread, :] = h0[...]
    far0 = first_leg((2, 6))
    near0 = first_leg((1, 7))
    found0 = joined(h0)
    y1 = solved1 - s0_scale * small_dot(found0, columns(E10, 2048), NT)
    spill(small_dot(y1, columns(G1, 1024), NN), q1)
    q1s = scatter_half(q1, q1r)
    y2 = solved2 - s0_scale * small_dot(found0, columns(E20, 2048), NT)
    work(1)
    h1[here1] = summed(q1, here1, q1r, q1s)
    a1 = gather_half(h1)
    z1h = along_z(h1, here1, x1)
    work(1)
    arrive(a1)
    y2 = y2 - s1_scale * small_dot(joined(h1), columns(E21, 1024), NT)
    spill(small_dot(y2, columns(G2, 512), NN), q2)
    q2s = x_send(lambda to: q2.at[to], q2r)
    near0 += second_leg()
    arrive(z1h)
    w1s = [send(x1.at[here1, mine, :], x1.at[here1, mine, :], device(xs(a), pair_y(b), z, c)) for a, b in HALF]
    h2[x] = summed(q2, x, q2r, q2s)
    x2[x, spread, :] = h2[x]
    z2h = [send(h2.at[x], x2.at[x, spread, :], device(xs(a), y, zs(d), c)) for a, d in SIDE]
    work(99)
    current[...] = small_dot(solved_t[...] * scale, (inverse_high[...], inverse_low[...]), NN)

    def swap_cores(result, batch):
        arrive(batch)
        return send(result.at[:, mine, :], result.at[:, mine, :], sibling)

    def product(result, i, half, first, second):
        both = jnp.concatenate([result[2 * i, half, :], result[2 * i + 1, half, :]], axis=1)
        return small_dot(both, (first, second), NN)

    def take_in(level, result, half):
        def step(i, carry):
            at = pl.ds(pl.multiple_of(row_start(level) + i * 256, 256), 256)
            total = product(result, i, half, moved_high[at, :], moved_low[at, :])
            current[half, :] = current[half, :] - weight_scale(level) * total
            return carry

        lax.fori_loop(0, (ROWS >> level) // 256, step, 0)

    def own_result(level, result, chunk):
        out_sep[level] = lax.dot_general(
            mark, result[chunk], NT, precision=lax.Precision.HIGHEST, preferred_element_type=F32
        )

    w0 = swap_cores(x0, near0)
    w1 = swap_cores(x1, w1s)
    take_in(0, x0, mine)
    w2 = swap_cores(x2, z2h)
    take_in(1, x1, mine)
    arrive([w0])
    take_in(0, x0, other)
    own_result(0, x0, here0)
    arrive([w1])
    take_in(1, x1, other)
    own_result(1, x1, here1)
    take_in(2, x2, mine)
    arrive([w2])
    take_in(2, x2, other)
    out_sub[...] = current[...].T
    own_result(2, x2, x)
    for copy in copies:
        copy.wait_send()


N_COPIES = 320


def whole(*operands):
    def piece(*lead, rows=COLS):
        return pltpu.VMEM((*lead, rows, LANES), F32)

    scratch = [
        pltpu.VMEM((LOC, LOC), F32), pltpu.VMEM((LOC, RHS), F32), pltpu.VMEM((1792, LOC), F32),
        pltpu.VMEM((LOC, LOC), F32), pltpu.VMEM((RHS, LOC), F32), pltpu.VMEM((RHS, LOC), F32),
        pltpu.VMEM((2 * RHS, 1792), BF16), pltpu.VMEM((1792, LOC), BF16), pltpu.VMEM((1792, LOC), BF16),
        pltpu.VMEM((3584, LOC), BF16), pltpu.VMEM((3584, LOC), BF16),
        pltpu.VMEM((LOC, LOC), BF16), pltpu.VMEM((LOC, LOC), BF16),
        piece(4, 4, rows=RHS), piece(4, 2, rows=RHS), piece(4, rows=RHS),
        pltpu.VMEM((NZ, 2, BLK, WIDE), F32), pltpu.VMEM((LANES, WIDE), BF16), pltpu.VMEM((LANES, WIDE), BF16),
        piece(16, rows=RHS), piece(8, rows=RHS), piece(4, rows=RHS),
        piece(4, rows=LANES), piece(4, 2, rows=LANES), piece(4, 4, rows=LANES),
        piece(3, rows=LANES), piece(rows=LANES), piece(7),
        piece(3, 2, rows=64), piece(4, rows=64), piece(2, rows=64), piece(4, rows=64),
        piece(3, rows=64), piece(rows=64), piece(rows=LANES), piece(7),
        piece(3, 4, rows=48), piece(3, 4, rows=80), piece(4, rows=48), piece(4, rows=80),
        piece(3, rows=48), piece(3, rows=80), piece(rows=LANES), piece(7),
        piece(4), piece(8), piece(7), piece(8), piece(16), piece(15), piece(16),
        piece(16), piece(15), piece(16), piece(8), piece(7), piece(8), piece(4), piece(3), piece(4),
        pltpu.SemaphoreType.DMA((3,)), pltpu.SemaphoreType.DMA((N_COPIES,)), pltpu.SemaphoreType.DMA((N_COPIES,)),
    ]
    vmem = pl.BlockSpec(memory_space=pltpu.VMEM)
    hbm = pl.BlockSpec(memory_space=pl.ANY)
    return pl.pallas_call(
        whole_kernel,
        out_shape=[jax.ShapeDtypeStruct((LOC, RHS), F32), jax.ShapeDtypeStruct((LEVELS, BLK, RHS), F32)],
        in_specs=[vmem] * 6 + [hbm] * 3,
        out_specs=[vmem] * 2,
        scratch_shapes=scratch,
        compiler_params=pltpu.CompilerParams(
            collective_id=0, has_side_effects=True, vmem_limit_bytes=58 * 1024 * 1024
        ),
    )(*operands)


def copy_kernel(first, second, first_out, second_out):
    first_out[...] = first[...]
    second_out[...] = second[...]


def hand_on(*results):
    vmem = pl.BlockSpec(memory_space=pltpu.VMEM)
    return pl.pallas_call(
        copy_kernel,
        out_shape=[jax.ShapeDtypeStruct(result.shape, F32) for result in results],
        in_specs=[vmem] * 2,
        out_specs=[vmem] * 2,
        compiler_params=pltpu.CompilerParams(vmem_limit_bytes=58 * 1024 * 1024),
    )(*results)


def body(rhs_sub, rhs_sep, sub_factor, sub_diag, sep_factor, sep_diag, sub_update, update_rows, sep_update):
    result_sub, result_sep = whole(
        sub_diag, update_rows, rhs_sep, sep_factor, sep_diag, sep_update[0].T, sub_factor[0], rhs_sub[0], sub_update[0]
    )
    return hand_on(result_sub[None], result_sep)


def solution(mesh):
    both = ("leaf", "panel")
    in_specs = (
        P(both, None, None), P(None, both, None), P(both, None, None), P(both, None), P(both, None),
        P(None, both), P(both, None, None), P(both, None), P(both, None, None),
    )
    out_specs = (P(both, None, None), P(None, both, None))
    return jax.shard_map(body, mesh=mesh, in_specs=in_specs, out_specs=out_specs, check_vma=False)
```

```python
import jax
import jax.numpy as jnp
from jax import lax
from jax.experimental import pallas as pl
from jax.experimental.pallas import tpu as pltpu
from jax.sharding import PartitionSpec as P

MESH = pl.DeviceIdType.MESH
F32 = jnp.float32
BF16 = jnp.bfloat16
NN = (((1,), (0,)), ((), ()))
NT = (((1,), (1,)), ((), ()))
TN = (((0,), (0,)), ((), ()))

NX, NY, NZ = 4, 4, 8
ROWS, RHS, LOC, BLK = 2048, 256, 512, 8
LEVELS = 3
LANES = 128
COLS = 16
G2, E21, G1, E20, E10, G0, WIDE = 0, 512, 1536, 2560, 4608, 6656, 8704


def weight_scale(target):
    fan_total = (256 >> target) * LOC // 2 + (LEVELS - 1 - target) * (ROWS >> target)
    return float(fan_total) ** (-0.5)


def split(value):
    high = value.astype(BF16)
    return high, (value - high.astype(F32)).astype(BF16)


def small_dot(left, right, dims):
    left_high, left_low = split(left)
    right_high, right_low = right if isinstance(right, tuple) else split(right)
    rows = left.shape[0]
    both = jnp.concatenate([left_high, left_low], axis=0)
    first = lax.dot_general(both, right_high, dims, preferred_element_type=F32)
    second = lax.dot_general(left_high, right_low, dims, preferred_element_type=F32)
    return first[:rows] + first[rows:] + second


def place():
    leaf, panel = lax.axis_index("leaf"), lax.axis_index("panel")
    return panel // 2, leaf // NZ, leaf % NZ, panel % 2


def device(x, y, z, c):
    return (y * NZ + z, x * 2 + c)


def hops(step, size):
    return min(step, size - step)


X_PEERS = (2, 1, 3)
Y_PEERS = (2, 1, 3)
Z_PEERS = (4, 3, 5, 2, 6, 1, 7)
PLANE = sorted(
    [(a, b) for a in range(NX) for b in range(NY)][1:], key=lambda ab: -hops(ab[0], NX) - hops(ab[1], NY)
)
SIDE = sorted(
    [(a, d) for a in range(NX) for d in range(NZ)][1:], key=lambda ad: -hops(ad[0], NX) - hops(ad[1], NZ)
)
HALF = sorted([(a, b) for a in range(NX) for b in range(2)][1:], key=lambda ab: -hops(ab[0], NX) - ab[1])
ROUNDS = ((0, 1536), (1536, 4608), (4608, 8704))


def split3(value):
    high = value.astype(BF16)
    rest = value - high.astype(F32)
    middle = rest.astype(BF16)
    return high, middle, (rest - middle.astype(F32)).astype(BF16)


def exact_dot(left, right):
    return jnp.dot(left, right, precision=lax.Precision.HIGHEST, preferred_element_type=F32)


def iota(shape, dim):
    return lax.broadcasted_iota(jnp.int32, shape, dim)


def reorder(rows):
    return (rows >> 9 << 9) + ((rows >> 4 & 3) << 7) + ((rows >> 6 & 7) << 4) + (rows & 15)


def sub_start(level):
    return sum(ROWS >> k + 1 for k in range(level))


def row_start(level):
    return sum(ROWS >> k for k in range(level))


def invert(factor, scale, inverse):
    lane = iota((32, LANES), 1)
    row, col = iota((LANES, LANES), 0), iota((LANES, LANES), 1)
    blocks, packed = [], []
    for g in range(4):
        at = slice(g * LANES, (g + 1) * LANES)
        block = jnp.where(row > col, factor[at, at] * scale[:, at], 0.0)
        blocks.append(block)
        parts = [jnp.where(lane >> 5 == q, block[32 * q : 32 * q + 32], 0.0) for q in range(4)]
        packed.append(parts[0] + parts[1] + parts[2] + parts[3])
    unit = (iota((32, LANES), 0) == (lane & 31)).astype(F32)
    found = [unit] * 4
    for k in range(31):
        index = (lane & 96) + k
        for g in range(4):
            coefficient = jnp.take_along_axis(packed[g], index, axis=1, mode="promise_in_bounds")
            found[g] = found[g] - coefficient * found[g][k : k + 1, :]
    whole = []
    for g in range(4):
        total = jnp.concatenate([jnp.where(lane >> 5 == q, found[g], 0.0) for q in range(4)], axis=0)
        whole.append(total)
    for bit in (5, 6):
        below = (row >> bit + 1 == col >> bit + 1) & (row >> bit > col >> bit)
        inner = [exact_dot(jnp.where(below, blocks[g], 0.0), whole[g]) for g in range(4)]
        whole = [whole[g] - exact_dot(whole[g], inner[g]) for g in range(4)]
    inverse[...] = jnp.zeros_like(inverse)
    for h in range(2):
        first = slice(h * 256, h * 256 + 128)
        second = slice(h * 256 + 128, h * 256 + 256)
        inner = exact_dot(factor[second, first] * scale[:, first], whole[2 * h])
        inverse[first, first] = whole[2 * h]
        inverse[second, second] = whole[2 * h + 1]
        inverse[second, first] = -exact_dot(whole[2 * h + 1], inner)
    inner = exact_dot(factor[256:, :256] * scale[:, :256], inverse[:256, :256])
    inverse[256:, :256] = -exact_dot(inverse[256:, 256:], inner)


def separator_rows(sep_factor, sep_diag, turned, position):
    inverses = []
    eye = iota((BLK, BLK), 0) == iota((BLK, BLK), 1)
    for level in range(LEVELS):
        node_rows = ROWS >> level
        start = row_start(level)
        strict = sep_factor[:, start : start + node_rows]
        diagonal = jnp.sum(jnp.where(eye, sep_diag[level : level + 1, :], 0.0), axis=1, keepdims=True)
        own = position % (256 >> level) * BLK + iota((BLK, node_rows), 0)
        cols = iota((BLK, node_rows), 1)
        inverses.append(jnp.where(cols < own, strict, 0.0) + jnp.where(cols == own, diagonal, 0.0))
    e10, e20, e21 = turned[:, :2048], turned[:, 2048:4096], turned[:, 4096:]
    pieces = [inverses[2], e21, inverses[1], e20, e10, inverses[0]]
    blocks = [piece[:, i : i + 512] for piece in pieces for i in range(0, piece.shape[1], 512)]
    stacked = jnp.concatenate(blocks, axis=0)
    swap = jnp.where(reorder(iota((512, 512), 0)) == iota((512, 512), 1), 1.0, 0.0).astype(BF16)
    count = stacked.shape[0]
    exact = jnp.concatenate([part.astype(F32) for part in split3(stacked)], axis=0).astype(BF16)
    moved = jnp.dot(exact, swap, preferred_element_type=F32)
    return moved[:count] + moved[count : 2 * count] + moved[2 * count :]


def whole_kernel(
    diag, rows, rhs_sep, sep_factor, sep_diag, turned, factor_hbm, rhs_hbm, update_hbm,
    out_sub, out_sep,
    factor, rhs, update, inverse, solved_t, current, terms, update_high, update_low, moved_high, moved_low,
    inverse_high, inverse_low,
    ut0, ut1, ut2, m_ref, m_high, m_low, x0, x1, x2,
    b2c, b1c, b0c, b2x, b2s, b2z, b1x, b1y, b1p, b1q, b1u, b1v, b1t, b1z, b0y, b0x, b0p, b0q, b0u, b0v, b0t, b0z,
    g2, p1, p1r, g1, p0, p0r, g0, q0, q0r, h0, q1, q1r, h1, q2, q2r, h2,
    lsem, ssem, rsem,
):
    x, y, z, c = place()
    position = lax.axis_index("leaf") * 8 + lax.axis_index("panel")
    partner = y + 1 - 2 * (y % 2)
    yy = y % 2
    sibling = device(x, y, z, 1 - c)
    loads = [
        pltpu.make_async_copy(src, dst, lsem.at[i])
        for i, (src, dst) in enumerate(((factor_hbm, factor), (rhs_hbm, rhs), (update_hbm, update)))
    ]
    for load in loads:
        load.start()

    def xs(a):
        return (x + a) % NX

    def ys(b):
        return (y + b) % NY

    def zs(d):
        return (z + d) % NZ

    def pair_y(b):
        return partner if b else y

    barrier = pltpu.get_barrier_semaphore()
    greeted = [device(xs(a), ys(b), z, c) for a, b in PLANE]
    greeted += [device(xs(a), y, zs(d), c) for a, d in SIDE if d > 0] + [sibling]
    for peer in greeted:
        pl.semaphore_signal(barrier, inc=1, device_id=peer, device_id_type=MESH)

    copies = []

    def send(src, dst, peer):
        at = len(copies)
        copy = pltpu.make_async_remote_copy(
            src_ref=src, dst_ref=dst, send_sem=ssem.at[at], recv_sem=rsem.at[at],
            device_id=peer, device_id_type=MESH,
        )
        copy.start()
        copies.append(copy)
        return copy

    def arrive(batch):
        for copy in batch:
            copy.wait_recv()

    loads[0].wait()
    loads[1].wait()
    own_rows = separator_rows(sep_factor, sep_diag, turned, position)
    for i in range(WIDE // 512):
        m_ref[z, c, :, i * 512 : (i + 1) * 512] = own_rows[i * BLK : (i + 1) * BLK]

    scale = 1.0 / diag[...]
    invert(factor, scale, inverse)
    right_t = rhs[...].T
    solved_t[...] = small_dot(right_t, inverse[...], NT) * scale

    pl.semaphore_wait(barrier, len(greeted))

    right, left = device(x, y, zs(1), c), device(x, y, zs(NZ - 1), c)

    def pass_on(block, start, size, peer):
        ref = m_ref.at[block, c, :, pl.ds(start, size)]
        return send(ref, ref, peer)

    ring, steps, shared = [], [1] * len(ROUNDS), [None] * len(ROUNDS)
    for start, stop in ROUNDS:
        ring.append([pass_on(z, start, stop - start, right), pass_on(z, start, stop - start, left)])

    def advance(turn):
        step = steps[turn]
        steps[turn] = step + 1
        start, stop = ROUNDS[turn]
        size = stop - start
        from_left, from_right = zs(NZ - step), zs(step)
        arrive(ring[turn])
        if step < 3:
            ring[turn] = [pass_on(from_left, start, size, right), pass_on(from_right, start, size, left)]
        elif step == 3:
            ring[turn] = [
                pass_on(from_left, start, size // 2, right),
                pass_on(from_right, start + size // 2, size // 2, left),
            ]
        else:
            ref = m_ref.at[:, c, :, pl.ds(start, size)]
            shared[turn] = [send(ref, ref, sibling)]

    loads[2].wait()
    solved_high, solved_low = split(solved_t[...])
    solved_both = jnp.concatenate([solved_high, solved_low], axis=0)

    def coupling_terms(level):
        def step(i, carry):
            at = pl.ds(pl.multiple_of(sub_start(level) + i * 256, 256), 256)
            high, low = split(update[at, :])
            update_high[at, :] = high
            update_low[at, :] = low
            first = lax.dot_general(solved_both, high, NT, preferred_element_type=F32)
            second = lax.dot_general(solved_high, low, NT, preferred_element_type=F32)
            top, bottom = split(first[:RHS] + first[RHS:] + second)
            terms[:RHS, at] = top
            terms[RHS:, at] = bottom
            return carry

        lax.fori_loop(0, (ROWS >> level) // 512, step, 0)

    places = []
    for level in range(LEVELS):
        count = ROWS >> level + 1
        places.append(reorder(rows[:, sub_start(level) : sub_start(level) + count]))

    def chosen(level, i):
        count = ROWS >> level + 1
        ids = iota((256, count), 0) + i * 256
        return jnp.where(ids == places[level], 1.0, 0.0).astype(BF16)

    mark = jnp.where(iota((BLK, LANES), 1) == z * 16 + c * BLK + iota((BLK, LANES), 0), 1.0, 0.0)

    def node_terms(level, ut, first, last):
        count = ROWS >> level + 1
        listed = terms[:, sub_start(level) : sub_start(level) + count]

        def step(i, carry):
            both = lax.dot_general(listed, chosen(level, i), NT, preferred_element_type=F32)
            total = (both[:RHS] + both[RHS:]) * -weight_scale(level)
            for k in range(2):
                part = total[:, k * LANES : (k + 1) * LANES]
                if level == 0:
                    ut[i // 2, i % 2 * 2 + k] = part
                elif level == 1:
                    ut[i % 2 * 2 + k, i // 2] = part
                else:
                    ut[2 * i + k] = part
            return carry

        lax.fori_loop(first, last, step, 0)

    def own_term(level):
        return lax.dot_general(
            rhs_sep[level], mark, TN, precision=lax.Precision.HIGHEST, preferred_element_type=F32
        )

    mine = pl.ds(pl.multiple_of(c * LANES, LANES), LANES)
    other = pl.ds(pl.multiple_of((1 - c) * LANES, LANES), LANES)
    cols = pl.ds(pl.multiple_of(z * COLS, COLS), COLS)
    spread = pl.ds(pl.multiple_of(c * LANES + z * COLS, COLS), COLS)

    def add_own(total, own):
        def step(i, carry):
            total[i] = total[i] + own[i, mine, :]
            return carry

        lax.fori_loop(0, total.shape[0], step, 0)

    def z_stage(summed, parts):
        return [
            send(summed.at[pl.ds(pl.multiple_of(zs(d) * COLS, COLS), COLS), :], parts.at[d - 1], device(x, y, zs(d), c))
            for d in Z_PEERS
        ]

    def z_sum(summed, parts, batch):
        arrive(batch)
        total = summed[cols, :]
        for d in range(NZ - 1):
            total = total + parts[d]
        return total

    pieces = [(2, i) for i in range(2)] + [(1, i) for i in range(4)] + [(0, i) for i in range(8)]

    def work(amount):
        for _ in range(amount):
            if pieces:
                level, i = pieces.pop()
                count = ROWS >> level + 1
                listed = slice(sub_start(level), sub_start(level) + count)
                at = slice(row_start(level) + i * 256, row_start(level) + i * 256 + 256)
                pick = chosen(level, i)
                entries = jnp.dot(pick, update_high[listed, :], preferred_element_type=F32)
                entries = entries + jnp.dot(pick, update_low[listed, :], preferred_element_type=F32)
                high, low = split(small_dot(entries * scale, (inverse_high[...], inverse_low[...]), NN))
                moved_high[at, :] = high
                moved_low[at, :] = low

    def x_send(piece, landed):
        return [send(piece(xs(a)), landed.at[a - 1], device(xs(a), y, z, c)) for a in X_PEERS]

    def y_send(piece, landed):
        return [send(piece(ys(b)), landed.at[b - 1], device(x, ys(b), z, c)) for b in Y_PEERS]

    coupling_terms(2)
    node_terms(2, ut2, 0, 2)
    ut2[x] = ut2[x] + own_term(2)
    c2 = send(ut2.at[:, other, :], b2c, sibling)
    coupling_terms(1)
    arrive([c2])
    add_own(b2c, ut2)
    x2s = x_send(lambda to: b2c.at[to], b2x)
    node_terms(1, ut1, 0, 4)
    ut1[x, yy] = ut1[x, yy] + own_term(1)
    c1 = send(ut1.at[:, :, other, :], b1c, sibling)
    advance(0)
    coupling_terms(0)
    mid, mid0 = LANES // 2, 48
    arrive([c1])

    def add_pair(i, carry):
        for k in range(2):
            b1c[i, k] = b1c[i, k] + ut1[i, k, mine, :]
        return carry

    lax.fori_loop(0, NX, add_pair, 0)
    x1s = x_send(lambda to: b1c.at[to, :, 0:mid, :], b1x)
    y1s = send(b1c.at[:, 1 - yy, mid:LANES, :], b1y, device(x, partner, z, c))
    advance(1)
    node_terms(0, ut0, 0, 2)
    node_terms(0, ut0, 2, 4)
    lower = jnp.where(y < 2, 1.0, 0.0)
    own0 = own_term(0)
    ut0[y % 2, x] = ut0[y % 2, x] + own0 * lower
    c0a = send(ut0.at[0:2, :, other, :], b0c.at[0:2], sibling)
    arrive(x2s)
    b2s[...] = b2c[x] + b2x[0] + b2x[1] + b2x[2]
    z2s = z_stage(b2s, b2z)
    node_terms(0, ut0, 4, 6)
    advance(2)
    node_terms(0, ut0, 6, 8)
    ut0[2 + y % 2, x] = ut0[2 + y % 2, x] + own0 * (1.0 - lower)
    c0b = send(ut0.at[2:4, :, other, :], b0c.at[2:4], sibling)
    advance(0)

    def add_rows(first):
        def step(i, carry):
            for k in range(NX):
                b0c[first + i, k] = b0c[first + i, k] + ut0[first + i, k, mine, :]
            return carry

        lax.fori_loop(0, 2, step, 0)

    arrive([c0a])
    add_rows(0)
    x0s = x_send(lambda to: b0c.at[0:2, to, mid0:LANES, :], b0x.at[:, 0:2])
    arrive(x1s)
    for i in range(2):
        b1p[i] = b1c[x, i, 0:mid, :] + b1x[0, i] + b1x[1, i] + b1x[2, i]
    y1t = send(b1p.at[1 - yy], b1v, device(x, partner, z, c))
    arrive([y1s])
    for i in range(NX):
        b1q[i] = b1c[i, yy, mid:LANES, :] + b1y[i]
    x1t = x_send(lambda to: b1q.at[to], b1u)
    arrive([c0b])
    add_rows(2)
    y0s = y_send(lambda to: b0c.at[to, :, 0:mid0, :], b0y)
    x0s += x_send(lambda to: b0c.at[2:4, to, mid0:LANES, :], b0x.at[:, 2:4])
    advance(1)
    r2 = z_sum(b2s, b2z, z2s)
    g2[x] = r2
    a2 = [send(g2.at[x], g2.at[x], device(xs(a), y, z, c)) for a in X_PEERS]
    advance(2)
    advance(0)
    high, low = split(inverse[...])
    inverse_high[...] = high
    inverse_low[...] = low
    work(1)
    arrive([y1t])
    b1t[0:mid, :] = b1p[yy] + b1v[...]
    arrive(x1t)
    b1t[mid:LANES, :] = b1q[x] + b1u[0] + b1u[1] + b1u[2]
    z1s = z_stage(b1t, b1z)
    advance(1)
    advance(0)

    def joined(ref):
        return jnp.concatenate([ref[i] for i in range(ref.shape[0])], axis=1)

    def spill(value, ref):
        for i in range(ref.shape[0]):
            ref[i] = value[:, i * LANES : (i + 1) * LANES]

    def columns(start, size):
        return m_high[:, start : start + size], m_low[:, start : start + size]

    def unpack(turn):
        arrive(shared[turn])
        start, stop = ROUNDS[turn]
        for at in range(start, stop, 512):
            high, low = split(m_ref[:, :, :, at : at + 512].reshape(LANES, 512))
            m_high[:, at : at + 512] = high
            m_low[:, at : at + 512] = low

    here1 = yy * NX + x
    here0 = y * NX + x

    def scatter_half(part, landed):
        return [
            send(part.at[(yy if b == 0 else 1 - yy) * NX + xs(a)], landed.at[k], device(xs(a), pair_y(b), z, c))
            for k, (a, b) in enumerate(HALF)
        ]

    def gather_half(whole):
        return [send(whole.at[here1], whole.at[here1], device(xs(a), pair_y(b), z, c)) for a, b in HALF]

    def scatter_plane(part, landed):
        return [
            send(part.at[ys(b) * NX + xs(a)], landed.at[k], device(xs(a), ys(b), z, c))
            for k, (a, b) in enumerate(PLANE)
        ]

    def gather_plane(whole):
        return [send(whole.at[here0], whole.at[here0], device(xs(a), ys(b), z, c)) for a, b in PLANE]

    def summed(part, here, landed, batch):
        arrive(batch)
        total = part[here]
        for k in range(landed.shape[0]):
            total = total + landed[k]
        return total

    s0_scale, s1_scale = weight_scale(0), weight_scale(1)

    arrive(a2)
    advance(2)
    unpack(0)
    solved2 = small_dot(joined(g2), columns(G2, 512), NT)
    spill(small_dot(solved2, columns(E21, 1024), NN), p1)
    p1s = scatter_half(p1, p1r)
    advance(1)
    work(1)
    arrive(y0s)
    for i in range(NX):
        b0p[i] = b0c[y, i, 0:mid0, :] + b0y[0, i] + b0y[1, i] + b0y[2, i]
    x0t = x_send(lambda to: b0p.at[to], b0u)
    arrive(x0s)
    for i in range(NY):
        b0q[i] = b0c[i, x, mid0:LANES, :] + b0x[0, i] + b0x[1, i] + b0x[2, i]
    y0t = y_send(lambda to: b0q.at[to], b0v)
    r1 = z_sum(b1t, b1z, z1s)
    g1[here1] = r1 - s1_scale * summed(p1, here1, p1r, p1s)
    a1 = gather_half(g1)
    unpack(1)
    up0 = small_dot(solved2, columns(E20, 2048), NN)
    advance(2)
    arrive(x0t)
    b0t[0:mid0, :] = b0p[x] + b0u[0] + b0u[1] + b0u[2]
    arrive(y0t)
    b0t[mid0:LANES, :] = b0q[y] + b0v[0] + b0v[1] + b0v[2]
    z0s = z_stage(b0t, b0z)
    arrive(a1)
    solved1 = small_dot(joined(g1), columns(G1, 1024), NT)
    unpack(2)
    spill(up0 + small_dot(solved1, columns(E10, 2048), NN), p0)
    p0s = scatter_plane(p0, p0r)
    work(2)
    r0 = z_sum(b0t, b0z, z0s)
    g0[here0] = r0 - s0_scale * summed(p0, here0, p0r, p0s)
    a0 = gather_plane(g0)
    work(3)
    arrive(a0)
    solved0 = small_dot(joined(g0), columns(G0, 2048), NT)

    def block_of(d):
        return pl.ds(pl.multiple_of(c * LANES + zs(d) * COLS, COLS), COLS)

    def first_leg(ds):
        return [send(h0, x0.at[:, spread, :], device(x, y, zs(d), c)) for d in ds]

    def second_leg():
        arrive(far0)
        low, high = x0.at[:, block_of(6), :], x0.at[:, block_of(2), :]
        first, second = x0.at[0:8, block_of(6), :], x0.at[8:16, block_of(2), :]
        steps = ((low, 1), (high, 7), (first, 2), (second, 6))
        return [send(part, part, device(x, y, zs(d), c)) for part, d in steps]

    def along_z(chunk, at, result):
        result[at, spread, :] = chunk[at]
        return [send(chunk.at[at], result.at[at, spread, :], device(x, y, zs(d), c)) for d in Z_PEERS]

    spill(small_dot(solved0, columns(G0, 2048), NN), q0)
    q0s = scatter_plane(q0, q0r)
    work(2)
    h0[here0] = summed(q0, here0, q0r, q0s)
    a0 = gather_plane(h0)
    work(3)
    arrive(a0)
    x0[:, spread, :] = h0[...]
    far0 = first_leg((2, 6))
    near0 = first_leg((1, 7))
    found0 = joined(h0)
    y1 = solved1 - s0_scale * small_dot(found0, columns(E10, 2048), NT)
    spill(small_dot(y1, columns(G1, 1024), NN), q1)
    q1s = scatter_half(q1, q1r)
    y2 = solved2 - s0_scale * small_dot(found0, columns(E20, 2048), NT)
    work(1)
    h1[here1] = summed(q1, here1, q1r, q1s)
    a1 = gather_half(h1)
    z1h = along_z(h1, here1, x1)
    work(1)
    arrive(a1)
    y2 = y2 - s1_scale * small_dot(joined(h1), columns(E21, 1024), NT)
    spill(small_dot(y2, columns(G2, 512), NN), q2)
    q2s = x_send(lambda to: q2.at[to], q2r)
    near0 += second_leg()
    arrive(z1h)
    w1s = [send(x1.at[here1, mine, :], x1.at[here1, mine, :], device(xs(a), pair_y(b), z, c)) for a, b in HALF]
    h2[x] = summed(q2, x, q2r, q2s)
    x2[x, spread, :] = h2[x]
    z2h = [send(h2.at[x], x2.at[x, spread, :], device(xs(a), y, zs(d), c)) for a, d in SIDE]
    work(99)
    current[...] = small_dot(solved_t[...] * scale, (inverse_high[...], inverse_low[...]), NN)

    def swap_cores(result, batch):
        arrive(batch)
        return send(result.at[:, mine, :], result.at[:, mine, :], sibling)

    def product(result, i, half, first, second):
        both = jnp.concatenate([result[2 * i, half, :], result[2 * i + 1, half, :]], axis=1)
        return small_dot(both, (first, second), NN)

    def take_in(level, result, half):
        def step(i, carry):
            at = pl.ds(pl.multiple_of(row_start(level) + i * 256, 256), 256)
            total = product(result, i, half, moved_high[at, :], moved_low[at, :])
            current[half, :] = current[half, :] - weight_scale(level) * total
            return carry

        lax.fori_loop(0, (ROWS >> level) // 256, step, 0)

    def own_result(level, result, chunk):
        out_sep[level] = lax.dot_general(
            mark, result[chunk], NT, precision=lax.Precision.HIGHEST, preferred_element_type=F32
        )

    w0 = swap_cores(x0, near0)
    w1 = swap_cores(x1, w1s)
    take_in(0, x0, mine)
    w2 = swap_cores(x2, z2h)
    take_in(1, x1, mine)
    arrive([w0])
    take_in(0, x0, other)
    arrive([w1])
    take_in(1, x1, other)
    take_in(2, x2, mine)
    own_result(0, x0, here0)
    own_result(1, x1, here1)
    arrive([w2])
    take_in(2, x2, other)
    out_sub[...] = current[...].T
    own_result(2, x2, x)
    for copy in copies:
        copy.wait_send()


N_COPIES = 320


def whole(*operands):
    def piece(*lead, rows=COLS):
        return pltpu.VMEM((*lead, rows, LANES), F32)

    scratch = [
        pltpu.VMEM((LOC, LOC), F32), pltpu.VMEM((LOC, RHS), F32), pltpu.VMEM((1792, LOC), F32),
        pltpu.VMEM((LOC, LOC), F32), pltpu.VMEM((RHS, LOC), F32), pltpu.VMEM((RHS, LOC), F32),
        pltpu.VMEM((2 * RHS, 1792), BF16), pltpu.VMEM((1792, LOC), BF16), pltpu.VMEM((1792, LOC), BF16),
        pltpu.VMEM((3584, LOC), BF16), pltpu.VMEM((3584, LOC), BF16),
        pltpu.VMEM((LOC, LOC), BF16), pltpu.VMEM((LOC, LOC), BF16),
        piece(4, 4, rows=RHS), piece(4, 2, rows=RHS), piece(4, rows=RHS),
        pltpu.VMEM((NZ, 2, BLK, WIDE), F32), pltpu.VMEM((LANES, WIDE), BF16), pltpu.VMEM((LANES, WIDE), BF16),
        piece(16, rows=RHS), piece(8, rows=RHS), piece(4, rows=RHS),
        piece(4, rows=LANES), piece(4, 2, rows=LANES), piece(4, 4, rows=LANES),
        piece(3, rows=LANES), piece(rows=LANES), piece(7),
        piece(3, 2, rows=64), piece(4, rows=64), piece(2, rows=64), piece(4, rows=64),
        piece(3, rows=64), piece(rows=64), piece(rows=LANES), piece(7),
        piece(3, 4, rows=48), piece(3, 4, rows=80), piece(4, rows=48), piece(4, rows=80),
        piece(3, rows=48), piece(3, rows=80), piece(rows=LANES), piece(7),
        piece(4), piece(8), piece(7), piece(8), piece(16), piece(15), piece(16),
        piece(16), piece(15), piece(16), piece(8), piece(7), piece(8), piece(4), piece(3), piece(4),
        pltpu.SemaphoreType.DMA((3,)), pltpu.SemaphoreType.DMA((N_COPIES,)), pltpu.SemaphoreType.DMA((N_COPIES,)),
    ]
    vmem = pl.BlockSpec(memory_space=pltpu.VMEM)
    hbm = pl.BlockSpec(memory_space=pl.ANY)
    return pl.pallas_call(
        whole_kernel,
        out_shape=[jax.ShapeDtypeStruct((LOC, RHS), F32), jax.ShapeDtypeStruct((LEVELS, BLK, RHS), F32)],
        in_specs=[vmem] * 6 + [hbm] * 3,
        out_specs=[vmem] * 2,
        scratch_shapes=scratch,
        compiler_params=pltpu.CompilerParams(
            collective_id=0, has_side_effects=True, vmem_limit_bytes=58 * 1024 * 1024
        ),
    )(*operands)


def copy_kernel(first, second, first_out, second_out):
    first_out[...] = first[...]
    second_out[...] = second[...]


def hand_on(*results):
    vmem = pl.BlockSpec(memory_space=pltpu.VMEM)
    return pl.pallas_call(
        copy_kernel,
        out_shape=[jax.ShapeDtypeStruct(result.shape, F32) for result in results],
        in_specs=[vmem] * 2,
        out_specs=[vmem] * 2,
        compiler_params=pltpu.CompilerParams(vmem_limit_bytes=58 * 1024 * 1024),
    )(*results)


def body(rhs_sub, rhs_sep, sub_factor, sub_diag, sep_factor, sep_diag, sub_update, update_rows, sep_update):
    result_sub, result_sep = whole(
        sub_diag, update_rows, rhs_sep, sep_factor, sep_diag, sep_update[0].T, sub_factor[0], rhs_sub[0], sub_update[0]
    )
    return hand_on(result_sub[None], result_sep)


def solution(mesh):
    both = ("leaf", "panel")
    in_specs = (
        P(both, None, None), P(None, both, None), P(both, None, None), P(both, None), P(both, None),
        P(None, both), P(both, None, None), P(both, None), P(both, None, None),
    )
    out_specs = (P(both, None, None), P(None, both, None))
    return jax.shard_map(body, mesh=mesh, in_specs=in_specs, out_specs=out_specs, check_vma=False)
```
